32 devices in a mesh: lon: 4 (over z), lat: 4 (over x, core), rep: 2 (over y).
Axes of the slice: x: 2, y: 2, z: 4, core: 2. Of those that a mesh axis runs over, the one named last changes fastest.
Arguments:
- inputs: float32 [2, 64, 128, 256], P('rep', 'lat', 'lon'), may hold values from -6 to 6
- cotangent: float32 [2, 64, 128, 256], P('rep', 'lat', 'lon'), may hold values from -6 to 6
- first_weight: float32 [2304, 256], replicated, may hold values from -0.125 to 0.125
- second_weight: float32 [2304, 256], replicated, may hold values from -0.125 to 0.125
Outputs:
- output: float32 [2, 64, 128, 256], P('rep', 'lat', 'lon')
- input_grad: float32 [2, 64, 128, 256], P('rep', 'lat', 'lon')
- first_grad: float32 [2304, 256], P('lon', ('lat', 'rep'))
- second_grad: float32 [2304, 256], P('lon', ('lat', 'rep'))
The draws below stay inside these ranges and needn't reach their ends.
All inputs are finite; a program needn't handle non-finite values.
Results may differ from the reference program's by a relative error of at most 0.00012.
Values sent between devices are 32-bit elements; how exact they have to be, the bound alone decides.
No kernel may reach another device: no remote copies, remote signals or barrier semaphores. Data moves between devices by JAX's collectives and lax.ppermute only.
A program may use at most 128 MiB of HBM per device.

```python
import math
import jax
import jax.numpy as jnp
from jax import lax

C = 256
IMGS = 2
NH = 64
NW = 128


def levels(stream_key, extent, pieces, smallest, top_value):
    def one(dim, blocks):
        heights = jax.random.uniform(jax.random.fold_in(jax.random.fold_in(stream_key, 6), dim), (blocks,), jnp.float32, smallest / len(pieces), top_value / len(pieces))
        return jnp.repeat(jnp.exp(heights), extent[dim] // blocks).reshape((-1,) + (1,) * (len(extent) - dim - 1))

    loudness = one(*pieces[0])
    for cut in pieces[1:]:
        loudness = loudness * one(*cut)
    return loudness


def scatter_about(key, dims, deviation, bound, split=(), dtype=jnp.bfloat16):
    gain = levels(key, dims, split, -0.22, 0.18) if split else 1.0
    entries = jax.random.normal(key, dims, jnp.float32) * deviation * gain
    return jnp.minimum(jnp.maximum(entries, -bound), bound).astype(dtype)


def setup_inputs(seed: int = 0) -> dict:
    key_of = jax.random.split(jax.random.key(seed), 5)
    inputs = scatter_about(key_of[0], (IMGS, NH, NW, C), 1.0, 6.0, ((0, 2), (1, 4), (2, 4)), jnp.float32)
    cotangent = scatter_about(key_of[1], (IMGS, NH, NW, C), 1.0, 6.0, ((0, 2), (1, 4), (2, 4)), jnp.float32)
    first_weight = scatter_about(key_of[2], (9 * C, C), (9 * C) ** -0.5, 0.125, (), jnp.float32)
    second_weight = scatter_about(key_of[3], (9 * C, C), (9 * C) ** -0.5, 0.125, (), jnp.float32)
    return dict(inputs=inputs, cotangent=cotangent, first_weight=first_weight, second_weight=second_weight)


def pad_field(field):
    beside_all = jnp.concatenate([field[:, -1:], field, field[:, :1]], axis=1)
    return jnp.pad(beside_all, ((1, 1), (0, 0), (0, 0)))

def convolve(field, weights):
    channels = field.shape[-1]
    padded = pad_field(field)
    total = jnp.zeros((NH * NW, channels), jnp.float32)
    for tap_row in range(3):
        for tap_col in range(3):
            offset = (tap_row * 3 + tap_col) * channels
            piece = padded[tap_row:tap_row + NH, tap_col:tap_col + NW].reshape(NH * NW, channels)
            total = total + jnp.dot(piece, weights[offset:offset + channels], precision=lax.Precision.HIGHEST, preferred_element_type=jnp.float32)
    return total.reshape(NH, NW, channels)

def forward(image, first_weight, second_weight):
    hidden = convolve(jax.nn.silu(image), first_weight)
    return image + convolve(jax.nn.silu(hidden), second_weight)

def reference(inputs, cotangent, first_weight, second_weight):

    def one_image(pair):
        image, grad_out = pair
        result, pullback = jax.vjp(forward, image, first_weight, second_weight)
        grad_in, grad_first, grad_second = pullback(grad_out)
        return (result, grad_in, grad_first, grad_second)
    output, input_grad, first_all, second_all = lax.map(one_image, (inputs, cotangent))
    scale = 1.0 / math.sqrt(IMGS * NH * NW)
    first_grad = lax.optimization_barrier(jnp.sum(first_all, axis=0)) * scale
    second_grad = lax.optimization_barrier(jnp.sum(second_all, axis=0)) * scale
    return (output, input_grad, first_grad, second_grad)
```

```python
import math

import jax
import jax.numpy as jnp
from jax import lax
from jax.sharding import PartitionSpec as P

HIGH = lax.Precision.HIGH


def shift_perm(count, periodic):
    forward = [(i, i + 1) for i in range(count - 1)]
    if periodic:
        forward.append((count - 1, 0))
    return forward, [(b, a) for a, b in forward]


def halo(block, axis, dim, width, periodic):
    forward, backward = shift_perm(lax.axis_size(axis), periodic)
    size = block.shape[dim]
    low = lax.ppermute(lax.slice_in_dim(block, size - width, size, axis=dim), axis, forward)
    high = lax.ppermute(lax.slice_in_dim(block, 0, width, axis=dim), axis, backward)
    return jnp.concatenate([low, block, high], axis=dim)


def taps_of(padded, rows, cols, flipped):
    pieces = []
    for a in range(3):
        for b in range(3):
            r, c = (2 - a, 2 - b) if flipped else (a, b)
            pieces.append(padded[r : r + rows, c : c + cols, :])
    return jnp.concatenate(pieces, axis=-1).reshape(rows * cols, -1)


def matmul(taps, weights):
    return jnp.dot(taps, weights, precision=HIGH, preferred_element_type=jnp.float32)


def transpose_kernel(weights):
    channels = weights.shape[1]
    stacked = weights.reshape(9, channels, channels)
    return jnp.swapaxes(stacked, 1, 2).reshape(9 * channels, channels)


def silu_slope(value):
    sigma = jax.nn.sigmoid(value)
    return sigma * (1.0 + value * (1.0 - sigma))


def kernel_grad_t(taps, grad_out):
    return jnp.einsum(
        "rd,rk->dk", grad_out, taps, precision=HIGH, preferred_element_type=jnp.float32
    )


def xor_perm(count, bit):
    return [(i, i ^ bit) for i in range(count)]


def pick(array, index, axis):
    return lax.dynamic_index_in_dim(array, index, axis, keepdims=False)


def scatter_sum(part):
    channels, taps = part.shape
    lon, lat, rep = lax.axis_size("lon"), lax.axis_size("lat"), lax.axis_size("rep")
    here_lat, here_rep, here_lon = (lax.axis_index(a) for a in ("lat", "rep", "lon"))
    x, core, y = here_lat // 2, here_lat % 2, here_rep
    each = channels // (lat * rep)
    view = part.reshape(2, 2, 2, each, taps)
    half = lax.ppermute(pick(view, 1 - core, 1), "lat", xor_perm(lat, 1))
    held = (pick(view, core, 1) + half).reshape(2, 2, 2, each // 2, taps)
    ahead, behind = held[:, :, 0], held[:, :, 1]
    got_0 = lax.ppermute(pick(ahead, 1 - y, 1), "rep", xor_perm(rep, 1))
    got_1 = lax.ppermute(pick(behind, 1 - x, 0), "lat", xor_perm(lat, 2))
    sum_0 = pick(ahead, y, 1) + got_0
    sum_1 = pick(behind, x, 0) + got_1
    got_0 = lax.ppermute(pick(sum_0, 1 - x, 0), "lat", xor_perm(lat, 2))
    got_1 = lax.ppermute(pick(sum_1, 1 - y, 0), "rep", xor_perm(rep, 1))
    tail = jnp.concatenate([pick(sum_0, x, 0) + got_0, pick(sum_1, y, 0) + got_1], axis=0)
    if lon & (lon - 1) or lon > 8:
        return lax.psum_scatter(tail, "lon", scatter_dimension=1, tiled=True).T
    blocks = jnp.swapaxes(tail.reshape(each, lon, taps // lon), 0, 1)
    total = pick(blocks, here_lon, 0)
    for step in range(1, lon):
        total = total + lax.ppermute(
            pick(blocks, here_lon ^ step, 0), "lon", xor_perm(lon, step)
        )
    return total.T


def local(inputs, cotangent, first_weight, second_weight):
    channels = inputs.shape[3]
    rows, cols = inputs.shape[1], inputs.shape[2]
    here = inputs[0]
    grad = cotangent[0]
    first_back = transpose_kernel(first_weight)
    second_back = transpose_kernel(second_weight)
    both = jnp.concatenate([here, grad], axis=-1)
    both = halo(both, "lat", 0, 2, False)
    both = halo(both, "lon", 1, 2, True)
    wide_in, wide_cot = both[..., :channels], both[..., channels:]
    row = lax.axis_index("lat") * rows - 1 + jnp.arange(rows + 2)
    inside = ((row >= 0) & (row < rows * lax.axis_size("lat")))[:, None, None]
    er, ec = rows + 2, cols + 2
    act_in = jax.nn.silu(wide_in)
    hidden = matmul(taps_of(act_in, er, ec, False), first_weight).reshape(er, ec, channels)
    act_hidden = jnp.where(inside, jax.nn.silu(hidden), 0.0)
    second_taps = taps_of(act_hidden, rows, cols, False)
    scale = 1.0 / math.sqrt(
        rows * cols * lax.axis_size("rep") * lax.axis_size("lat") * lax.axis_size("lon")
    )
    second_part = kernel_grad_t(second_taps, grad.reshape(rows * cols, channels)) * scale
    second_grad = scatter_sum(second_part)
    hidden_grad = matmul(taps_of(wide_cot, er, ec, True), second_back).reshape(er, ec, channels)
    hidden_grad = jnp.where(inside, hidden_grad * silu_slope(hidden), 0.0)
    first_taps = taps_of(act_in[1:-1, 1:-1], rows, cols, False)
    first_part = (
        kernel_grad_t(first_taps, hidden_grad[1:-1, 1:-1].reshape(rows * cols, channels)) * scale
    )
    first_grad = scatter_sum(first_part)
    output = inputs + matmul(second_taps, second_weight).reshape(inputs.shape)
    back = matmul(taps_of(hidden_grad, rows, cols, True), first_back).reshape(inputs.shape)
    input_grad = cotangent + back * silu_slope(inputs)
    return (output, input_grad, first_grad, second_grad)


def solution(mesh):
    in_specs = (P("rep", "lat", "lon", None), P("rep", "lat", "lon", None), P(), P())
    out_specs = (
        P("rep", "lat", "lon", None),
        P("rep", "lat", "lon", None),
        P("lon", ("lat", "rep")),
        P("lon", ("lat", "rep")),
    )
    return jax.shard_map(local, mesh=mesh, in_specs=in_specs, out_specs=out_specs, check_vma=False)
```

```python
import math

import jax
import jax.numpy as jnp
from jax import lax
from jax.sharding import PartitionSpec as P

HIGH = lax.Precision.HIGH


def shift_perm(count, periodic):
    forward = [(i, i + 1) for i in range(count - 1)]
    if periodic:
        forward.append((count - 1, 0))
    return forward, [(b, a) for a, b in forward]


def pair_swap(block_low, block_high, axis):
    count = lax.axis_size(axis)
    even = lax.axis_index(axis) % 2 == 0
    pairs = [(i, i + 1) for i in range(0, count - 1, 2)]
    mates = [(i, i + 1) for i in range(1, count - 1, 2)]

    def swap(block, who):
        return lax.ppermute(block, axis, who + [(b, a) for a, b in who])

    one = swap(jnp.where(even, block_high, block_low), pairs)
    two = swap(jnp.where(even, block_low, block_high), mates)
    return jnp.where(even, two, one), jnp.where(even, one, two)


def extend(field, width):
    rows, cols, channels = field.shape
    low, high = pair_swap(field[:width], field[rows - width :], "lat")
    forward, backward = shift_perm(lax.axis_size("lon"), True)
    left = lax.ppermute(jnp.swapaxes(field[:, cols - width :], 0, 1), "lon", forward)
    right = lax.ppermute(jnp.swapaxes(field[:, :width], 0, 1), "lon", backward)
    edge = jnp.concatenate([low, high], axis=0)
    corner_left = lax.ppermute(
        edge[:, cols - width :].reshape(-1, channels), "lon", forward
    ).reshape(2, width, width, channels)
    corner_right = lax.ppermute(edge[:, :width].reshape(-1, channels), "lon", backward).reshape(
        2, width, width, channels
    )
    left, right = jnp.swapaxes(left, 0, 1), jnp.swapaxes(right, 0, 1)
    return jnp.concatenate(
        [
            jnp.concatenate([corner_left[0], low, corner_right[0]], axis=1),
            jnp.concatenate([left, field, right], axis=1),
            jnp.concatenate([corner_left[1], high, corner_right[1]], axis=1),
        ],
        axis=0,
    )


def taps_of(padded, rows, cols, flipped):
    pieces = []
    for a in range(3):
        for b in range(3):
            r, c = (2 - a, 2 - b) if flipped else (a, b)
            pieces.append(padded[r : r + rows, c : c + cols, :])
    return jnp.concatenate(pieces, axis=-1).reshape(rows * cols, -1)


def matmul(taps, weights):
    return jnp.dot(taps, weights, precision=HIGH, preferred_element_type=jnp.float32)


def transpose_kernel(weights):
    channels = weights.shape[1]
    stacked = weights.reshape(9, channels, channels)
    return jnp.swapaxes(stacked, 1, 2).reshape(9 * channels, channels)


def silu_slope(value):
    sigma = jax.nn.sigmoid(value)
    return sigma * (1.0 + value * (1.0 - sigma))


def kernel_grad_t(taps, grad_out, order):
    rows, channels = grad_out.shape
    blocks = grad_out.T.reshape(8, channels // 8, rows)
    grad_t = jnp.concatenate(
        [lax.dynamic_index_in_dim(blocks, i, 0, keepdims=False) for i in order], axis=0
    )
    return jnp.einsum(
        "dr,rk->dk", grad_t, taps, precision=HIGH, preferred_element_type=jnp.float32
    )


def plane_perm(count, even, odd):
    return [(i, i ^ (odd if (i // 2) % 2 else even)) for i in range(count)]


def relative_blocks(flip):
    lat, y = lax.axis_index("lat"), lax.axis_index("rep")
    x, core = lat // 2, lat % 2
    order = []
    for r_core in range(2):
        c = core ^ r_core
        y_first = (c == 0) != flip
        for r_first in range(2):
            for r_second in range(2):
                there_y = y ^ jnp.where(y_first, r_first, r_second)
                there_x = x ^ jnp.where(y_first, r_second, r_first)
                order.append(there_x * 4 + c * 2 + there_y)
    return order


def scatter_sum(part, flip):
    channels, taps = part.shape
    lon, lat, rep = lax.axis_size("lon"), lax.axis_size("lat"), lax.axis_size("rep")
    plane = lat * rep
    each = channels // plane
    one, two = (4, 1) if flip else (1, 4)
    view = part.reshape(2, 2, 2, each, taps)
    held = view[0] + lax.ppermute(view[1], ("lat", "rep"), plane_perm(plane, 2, 2))
    held = held[0] + lax.ppermute(held[1], ("lat", "rep"), plane_perm(plane, one, two))
    tail = held[0] + lax.ppermute(held[1], ("lat", "rep"), plane_perm(plane, two, one))
    if lon != 4:
        return lax.psum_scatter(tail, "lon", scatter_dimension=1, tiled=True).T
    blocks = jnp.swapaxes(tail.reshape(each, lon, taps // lon), 0, 1)
    z = lax.axis_index("lon")
    low_first = (lax.axis_index("lat") % 2 == 0) != flip
    ordered = []
    for r_first in range(2):
        for r_second in range(2):
            step = jnp.where(low_first, r_first + 2 * r_second, 2 * r_first + r_second)
            ordered.append(lax.dynamic_index_in_dim(blocks, z ^ step, 0, keepdims=False))
    blocks = jnp.stack(ordered).reshape(2, 2, each, taps // lon)
    axes = ("lon", "lat")
    low, high = (2, 1) if flip else (1, 2)

    def lane(even, odd):
        return [(i, i ^ (lat * (odd if i % 2 else even))) for i in range(lon * lat)]

    held = blocks[0] + lax.ppermute(blocks[1], axes, lane(low, high))
    return (held[0] + lax.ppermute(held[1], axes, lane(high, low))).T


def local(inputs, cotangent, first_weight, second_weight):
    channels = inputs.shape[3]
    rows, cols = inputs.shape[1], inputs.shape[2]
    here = inputs[0]
    grad = cotangent[0]
    first_back = transpose_kernel(first_weight)
    second_back = transpose_kernel(second_weight)
    wide_in, wide_cot = extend(here, 2), extend(grad, 2)
    row = lax.axis_index("lat") * rows - 1 + jnp.arange(rows + 2)
    inside = ((row >= 0) & (row < rows * lax.axis_size("lat")))[:, None, None]
    er, ec = rows + 2, cols + 2
    act_in = jax.nn.silu(wide_in)
    hidden = matmul(taps_of(act_in, er, ec, False), first_weight).reshape(er, ec, channels)
    act_hidden = jnp.where(inside, jax.nn.silu(hidden), 0.0)
    second_taps = taps_of(act_hidden, rows, cols, False)
    scale = 1.0 / math.sqrt(
        rows * cols * lax.axis_size("rep") * lax.axis_size("lat") * lax.axis_size("lon")
    )
    second_part = kernel_grad_t(second_taps, grad.reshape(rows * cols, channels), relative_blocks(False)) * scale
    second_grad = scatter_sum(second_part, False)
    hidden_grad = matmul(taps_of(wide_cot, er, ec, True), second_back).reshape(er, ec, channels)
    hidden_grad = jnp.where(inside, hidden_grad * silu_slope(hidden), 0.0)
    first_taps = taps_of(act_in[1:-1, 1:-1], rows, cols, False)
    first_part = (
        kernel_grad_t(first_taps, hidden_grad[1:-1, 1:-1].reshape(rows * cols, channels), relative_blocks(True)) * scale
    )
    first_grad = scatter_sum(first_part, True)
    output = inputs + matmul(second_taps, second_weight).reshape(inputs.shape)
    back = matmul(taps_of(hidden_grad, rows, cols, True), first_back).reshape(inputs.shape)
    input_grad = cotangent + back * silu_slope(inputs)
    return (output, input_grad, first_grad, second_grad)


def solution(mesh):
    in_specs = (P("rep", "lat", "lon", None), P("rep", "lat", "lon", None), P(), P())
    out_specs = (
        P("rep", "lat", "lon", None),
        P("rep", "lat", "lon", None),
        P("lon", ("lat", "rep")),
        P("lon", ("lat", "rep")),
    )
    return jax.shard_map(local, mesh=mesh, in_specs=in_specs, out_specs=out_specs, check_vma=False)
```

```python
import math

import jax
import jax.numpy as jnp
from jax import lax
from jax.experimental import pallas as pl
from jax.experimental.pallas import tpu as pltpu
from jax.sharding import PartitionSpec as P

F32 = jnp.float32
BF16 = jnp.bfloat16
VMEM = pl.BlockSpec(memory_space=pltpu.VMEM)
LINE = 24
EDGE = 8


def call(body, outs, ins, flops=0, scratch=(), limit=32):
    size = sum(math.prod(a.shape) * a.dtype.itemsize for a in ins)
    return pl.pallas_call(
        body,
        out_shape=[jax.ShapeDtypeStruct(shape, dtype) for shape, dtype in outs],
        in_specs=[VMEM] * len(ins),
        out_specs=[VMEM] * len(outs),
        scratch_shapes=[pltpu.VMEM(shape, dtype) for shape, dtype in scratch],
        compiler_params=pltpu.CompilerParams(vmem_limit_bytes=limit * 1024 * 1024),
        cost_estimate=pl.CostEstimate(flops=flops, bytes_accessed=size, transcendentals=0),
    )(*ins)


def split(value):
    high = value.astype(BF16)
    return high, (value - high.astype(F32)).astype(BF16)


def dot(a, b):
    return jnp.dot(a, b, preferred_element_type=F32)


def silu(value):
    return value / (1.0 + jnp.exp(-value))


def slope(value):
    sigma = 1.0 / (1.0 + jnp.exp(-value))
    return sigma * (1.0 + value * (1.0 - sigma))


def relative_blocks(flip):
    lat, y = lax.axis_index("lat"), lax.axis_index("rep")
    x, core = lat // 2, lat % 2
    order = []
    for r_core in range(2):
        c = core + r_core - 2 * core * r_core
        y_first = c == (1 if flip else 0)
        for r_first in range(2):
            for r_second in range(2):
                move_y = jnp.where(y_first, r_first, r_second)
                move_x = jnp.where(y_first, r_second, r_first)
                there_y = y + move_y - 2 * y * move_y
                there_x = x + move_x - 2 * x * move_x
                order.append(there_x * 4 + c * 2 + there_y)
    return order


def pack_rows(here, grad, one, two):
    rows = here.shape[0]
    even = lax.axis_index("lat") % 2 == 0
    for f, field in enumerate((here, grad)):
        low, high = field[0:2], field[rows - 2 : rows]
        one[f] = jnp.where(even, high, low)
        two[f] = jnp.where(even, low, high)


def pack_cols(here, grad, one, two, first, second):
    rows, cols = here.shape[:2]
    even_lat = lax.axis_index("lat") % 2 == 0
    even = lax.axis_index("lon") % 2 == 0
    for f, field in enumerate((here, grad)):
        low = jnp.where(even_lat, two[f], one[f])
        high = jnp.where(even_lat, one[f], two[f])
        for c in range(2):
            edges = []
            for col in (c, cols - 2 + c):
                edges.append(
                    jnp.concatenate(
                        [
                            low[:, col],
                            field[:, col],
                            high[:, col],
                            jnp.zeros((LINE - rows - 4, field.shape[2]), F32),
                        ],
                        axis=0,
                    )
                )
            first[f, c] = jnp.where(even, edges[1], edges[0])
            second[f, c] = jnp.where(even, edges[0], edges[1])


def pair_swap(one, two, axis, periodic):
    count = lax.axis_size(axis)
    pairs = [(i, i + 1) for i in range(0, count - 1, 2)]
    mates = [(i, i + 1) for i in range(1, count - 1, 2)]
    if periodic:
        mates.append((count - 1, 0))
    return tuple(
        lax.ppermute(block, axis, who + [(b, a) for a, b in who])
        for block, who in ((one, pairs), (two, mates))
    )


def prepare(weights, high, low):
    high[...], low[...] = split(weights[...])


def prepare_back(weights, high, low):
    size = weights.shape[1]
    for tap in range(9):
        there = 8 - tap
        block = weights[there * size : (there + 1) * size, :].T
        high[tap * size : (tap + 1) * size, :], low[tap * size : (tap + 1) * size, :] = split(block)


def turn(flip, value, high, low, scratch):
    channels = value.shape[1]
    each = channels // 8
    scratch[...] = value.T
    for i, block in enumerate(relative_blocks(flip)):
        part = scratch[pl.ds(pl.multiple_of(block * each, each), each), :]
        high[i * each : (i + 1) * each, :], low[i * each : (i + 1) * each, :] = split(part)


def turn_grad(grad, high, low, scratch):
    cells = grad.shape[0] * grad.shape[1]
    turn(False, grad[...].reshape(cells, grad.shape[2]), high, low, scratch)


def lay_taps(wide, x_high, x_low):
    rows, padded, channels = wide.shape
    cols = padded - 2 * EDGE
    for b in range(3):
        part = wide[:, EDGE - 1 + b : EDGE - 1 + b + cols, :].reshape(rows * cols, channels)
        high, low = split(part)
        x_high[:, b * channels : (b + 1) * channels] = high
        x_low[:, b * channels : (b + 1) * channels] = low


def convolve(x_high, x_low, first_row, rows, cols, w_high, w_low):
    channels = w_high.shape[1]
    total = None
    for a in range(3):
        cells = slice((first_row + a) * cols, (first_row + a + rows) * cols)
        taps = slice(a * 3 * channels, (a + 1) * 3 * channels)
        for x, w in ((x_high, w_high), (x_high, w_low), (x_low, w_high)):
            part = dot(x[cells, :], w[taps, :])
            total = part if total is None else total + part
    return total


def side_columns(mine_one, mine_two, got_one, got_two, f):
    even = lax.axis_index("lon") % 2 == 0

    def either(a, b):
        return jnp.where(even, a, b)

    left = [either(got_two[f, c], got_one[f, c]) for c in range(2)]
    left.append(either(mine_two[f, 0], mine_one[f, 0]))
    right = [either(mine_one[f, 1], mine_two[f, 1])]
    right += [either(got_one[f, c], got_two[f, c]) for c in range(2)]
    return left, right


def ring(left, right, w_high, w_low, r_high, r_low):
    channels = w_high.shape[1]
    for s, columns in enumerate((left, right)):
        for a in range(3):
            for b in range(3):
                high, low = split(columns[b])
                value = columns[b]
                if a:
                    value = jnp.concatenate(
                        [value[a:], jnp.zeros((a, value.shape[1]), F32)], axis=0
                    )
                place = (
                    slice(s * LINE, (s + 1) * LINE),
                    slice((a * 3 + b) * channels, (a * 3 + b + 1) * channels),
                )
                r_high[place], r_low[place] = split(value)
    return (
        dot(r_high[...], w_high[...])
        + dot(r_high[...], w_low[...])
        + dot(r_low[...], w_high[...])
    )


def spread(value, function, got_rows, columns, f, wide):
    rows, cols, channels = value.shape
    even_lat = lax.axis_index("lat") % 2 == 0
    one, two = got_rows
    wide[2 : rows + 2, EDGE : EDGE + cols, :] = function(value[...])
    wide[0:2, EDGE : EDGE + cols, :] = function(jnp.where(even_lat, two[f], one[f]))
    wide[rows + 2 : rows + 4, EDGE : EDGE + cols, :] = function(
        jnp.where(even_lat, one[f], two[f])
    )
    left, right = columns
    wide[:, EDGE - 1 : EDGE, :] = left[1][: rows + 4].reshape(rows + 4, 1, channels)
    wide[:, EDGE + cols : EDGE + cols + 1, :] = right[1][: rows + 4].reshape(rows + 4, 1, channels)


def inside(rows):
    row = lax.axis_index("lat") * rows - 1 + lax.broadcasted_iota(jnp.int32, (rows + 2, 1, 1), 0)
    return (row >= 0) & (row < rows * lax.axis_size("lat"))


def inside_line(rows):
    row = lax.axis_index("lat") * rows - 1 + lax.broadcasted_iota(jnp.int32, (LINE, 1), 0)
    return (row >= 0) & (row < rows * lax.axis_size("lat"))


def spread_ext(main, side, wide):
    tall, cols, channels = main.shape
    wide[:, EDGE : EDGE + cols, :] = main
    wide[:, EDGE - 1 : EDGE, :] = side[:tall].reshape(tall, 1, channels)
    wide[:, EDGE + cols : EDGE + cols + 1, :] = side[LINE : LINE + tall].reshape(tall, 1, channels)


def products(t_high, t_low, x_high, x_low, first_row, cells, cols, scale, away, keep):
    half = t_high.shape[0] // 2
    width = x_high.shape[1]
    for a in range(3):
        rows = slice((first_row + a) * cols, (first_row + a) * cols + cells)
        total = (
            dot(t_high[...], x_high[rows, :])
            + dot(t_high[...], x_low[rows, :])
            + dot(t_low[...], x_high[rows, :])
        ) * scale
        away[:, a * width : (a + 1) * width] = total[half:]
        keep[:, a * width : (a + 1) * width] = total[:half]


def hidden_kernel(
    scale, here, r1, r2, m1, m2, q1, q2, w_high, w_low, t_high, t_low,
    hidden, side, x1_high, x1_low, x2_high, x2_low, away, keep,
    wide, wide2, r_high, r_low,
):
    rows, cols, channels = here.shape
    left, right = side_columns(m1, m2, q1, q2, 0)
    left, right = [silu(v) for v in left], [silu(v) for v in right]
    spread(here, silu, (r1, r2), (left, right), 0, wide)
    lay_taps(wide, x1_high, x1_low)
    main = convolve(x1_high, x1_low, 0, rows + 2, cols, w_high, w_low)
    around = ring(left, right, w_high, w_low, r_high, r_low)
    hidden[...] = main
    side[...] = around
    act = jnp.where(inside(rows), silu(main).reshape(rows + 2, cols, channels), 0.0)
    line = inside_line(rows)
    around = jnp.where(jnp.concatenate([line, line], axis=0), silu(around), 0.0)
    spread_ext(act, around, wide2)
    lay_taps(wide2, x2_high, x2_low)
    products(t_high, t_low, x2_high, x2_low, 0, rows * cols, cols, scale, away, keep)


def inner_kernel(
    scale, grad, r1, r2, m1, m2, q1, q2, w_high, w_low, hidden, side, x1_high, x1_low,
    x3_high, x3_low, away, keep,
    wide, xc_high, xc_low, wide2, r_high, r_low, turned, t_high, t_low,
):
    rows, cols, channels = grad.shape
    columns = side_columns(m1, m2, q1, q2, 1)
    spread(grad, lambda v: v, (r1, r2), columns, 1, wide)
    lay_taps(wide, xc_high, xc_low)
    main = convolve(xc_high, xc_low, 0, rows + 2, cols, w_high, w_low) * slope(hidden[...])
    around = ring(*columns, w_high, w_low, r_high, r_low) * slope(side[...])
    main = jnp.where(inside(rows), main.reshape(rows + 2, cols, channels), 0.0)
    line = inside_line(rows)
    around = jnp.where(jnp.concatenate([line, line], axis=0), around, 0.0)
    turn(True, main[1 : rows + 1].reshape(rows * cols, channels), t_high, t_low, turned)
    products(t_high, t_low, x1_high, x1_low, 1, rows * cols, cols, scale, away, keep)
    spread_ext(main, around, wide2)
    lay_taps(wide2, x3_high, x3_low)


def output_kernel(here, x_high, x_low, w_high, w_low, out):
    rows, cols, channels = here.shape
    total = convolve(x_high, x_low, 0, rows, cols, w_high, w_low)
    out[...] = here[...] + total.reshape(rows, cols, channels)


def input_grad_kernel(here, grad, x_high, x_low, w_high, w_low, out):
    rows, cols, channels = here.shape
    total = convolve(x_high, x_low, 0, rows, cols, w_high, w_low)
    out[...] = grad[...] + total.reshape(rows, cols, channels) * slope(here[...])


def plane_perm(count, even, odd):
    return [(i, i ^ (odd if (i // 2) % 2 else even)) for i in range(count)]


def scatter_sum(away, keep, flip):
    half, taps = keep.shape
    lon, lat, rep = lax.axis_size("lon"), lax.axis_size("lat"), lax.axis_size("rep")
    plane = lat * rep
    axes = ("lat", "rep")
    one, two = (4, 1) if flip else (1, 4)
    held = keep + lax.ppermute(away, axes, plane_perm(plane, 2, 2))
    held = held[: half // 2] + lax.ppermute(held[half // 2 :], axes, plane_perm(plane, one, two))
    each = half // 4
    tail = held[:each] + lax.ppermute(held[each:], axes, plane_perm(plane, two, one))
    if lon != 4:
        return lax.psum_scatter(tail, "lon", scatter_dimension=1, tiled=True).T
    blocks = jnp.swapaxes(tail.reshape(each, lon, taps // lon), 0, 1)
    z = lax.axis_index("lon")
    total = lax.dynamic_index_in_dim(blocks, z, 0, keepdims=False)
    for step in range(1, lon):
        block = lax.dynamic_index_in_dim(blocks, z ^ step, 0, keepdims=False)
        total = total + lax.ppermute(block, "lon", [(i, i ^ step) for i in range(lon)])
    return total.T


def local(inputs, cotangent, first_weight, second_weight):
    here, grad = inputs[0], cotangent[0]
    rows, cols, channels = here.shape
    cells, tall = rows * cols, rows + 2
    width = 3 * channels
    scale = 1.0 / math.sqrt(
        cells * lax.axis_size("rep") * lax.axis_size("lat") * lax.axis_size("lon")
    )
    edge = ((2, 2, cols, channels), F32)
    one, two = call(pack_rows, [edge] * 2, [here, grad])
    r1, r2 = pair_swap(one, two, "lat", False)
    pair = [((9 * channels, channels), BF16)] * 2
    w1_high, w1_low = call(prepare, pair, [first_weight])
    t_high, t_low = call(
        turn_grad, [((channels, cells), BF16)] * 2, [grad], scratch=[((channels, cells), F32)]
    )
    line = ((2, 2, LINE, channels), F32)
    m1, m2 = call(pack_cols, [line] * 2, [here, grad, r1, r2])
    q1, q2 = pair_swap(m1, m2, "lon", True)
    b2_high, b2_low = call(prepare_back, pair, [second_weight])
    conv_flops = 2 * 3 * 9 * tall * cols * channels * channels
    grad_flops = 2 * 3 * 9 * cells * channels * channels
    lines = ((2 * LINE, channels), F32)
    wide = ((rows + 4, cols + 2 * EDGE, channels), F32)
    wide2 = ((tall, cols + 2 * EDGE, channels), F32)
    taps_1 = [(((rows + 4) * cols, width), BF16)] * 2
    taps_2 = [((tall * cols, width), BF16)] * 2
    around = [((2 * LINE, 3 * width), BF16)] * 2
    halves = [((channels // 2, 9 * channels), F32)] * 2
    hidden, side, x1_high, x1_low, x2_high, x2_low, away, keep = call(
        lambda *refs: hidden_kernel(scale, *refs),
        [((tall * cols, channels), F32), lines] + taps_1 + taps_2 + halves,
        [here, r1, r2, m1, m2, q1, q2, w1_high, w1_low, t_high, t_low],
        conv_flops + grad_flops,
        scratch=[wide, wide2] + around,
    )
    second_grad = scatter_sum(away, keep, False)
    x3_high, x3_low, away, keep = call(
        lambda *refs: inner_kernel(scale, *refs),
        taps_2 + halves,
        [grad, r1, r2, m1, m2, q1, q2, b2_high, b2_low, hidden, side, x1_high, x1_low],
        conv_flops + grad_flops,
        scratch=[wide] + taps_1 + [wide2] + around + [((channels, cells), F32)]
        + [((channels, cells), BF16)] * 2,
    )
    first_grad = scatter_sum(away, keep, True)
    w2_high, w2_low = call(prepare, pair, [second_weight])
    b1_high, b1_low = call(prepare_back, pair, [first_weight])
    shape = ((rows, cols, channels), F32)
    (output,) = call(
        output_kernel, [shape], [here, x2_high, x2_low, w2_high, w2_low], grad_flops
    )
    (input_grad,) = call(
        input_grad_kernel, [shape], [here, grad, x3_high, x3_low, b1_high, b1_low], grad_flops
    )
    return (output[None], input_grad[None], first_grad, second_grad)


def solution(mesh):
    in_specs = (P("rep", "lat", "lon", None), P("rep", "lat", "lon", None), P(), P())
    out_specs = (
        P("rep", "lat", "lon", None),
        P("rep", "lat", "lon", None),
        P("lon", ("lat", "rep")),
        P("lon", ("lat", "rep")),
    )
    return jax.shard_map(local, mesh=mesh, in_specs=in_specs, out_specs=out_specs, check_vma=False)
```

```python
import math

import jax
import jax.numpy as jnp
from jax import lax
from jax.experimental import pallas as pl
from jax.experimental.pallas import tpu as pltpu
from jax.sharding import PartitionSpec as P

F32 = jnp.float32
BF16 = jnp.bfloat16
VMEM = pl.BlockSpec(memory_space=pltpu.VMEM)
LINE = 24
EDGE = 8


def call(body, outs, ins, flops=0, scratch=(), limit=16, after=()):
    size = sum(math.prod(a.shape) * a.dtype.itemsize for a in ins)
    used, skip = len(ins), len(after)

    def kernel(*refs):
        body(*refs[:used], *refs[used + skip :])

    ins = list(ins) + list(after)
    return pl.pallas_call(
        kernel,
        out_shape=[jax.ShapeDtypeStruct(shape, dtype) for shape, dtype in outs],
        in_specs=[VMEM] * used + [pl.BlockSpec(memory_space=pl.ANY)] * skip,
        out_specs=[VMEM] * len(outs),
        scratch_shapes=[pltpu.VMEM(shape, dtype) for shape, dtype in scratch],
        compiler_params=pltpu.CompilerParams(vmem_limit_bytes=limit * 1024 * 1024),
        cost_estimate=pl.CostEstimate(flops=flops, bytes_accessed=size, transcendentals=0),
    )(*ins)


def split(value):
    high = value.astype(BF16)
    return high, (value - high.astype(F32)).astype(BF16)


def dot(a, b):
    return jnp.dot(a, b, preferred_element_type=F32)


def silu(value):
    return value / (1.0 + jnp.exp(-value))


def slope(value):
    sigma = 1.0 / (1.0 + jnp.exp(-value))
    return sigma * (1.0 + value * (1.0 - sigma))


def relative_blocks(flip):
    lat, y = lax.axis_index("lat"), lax.axis_index("rep")
    x, core = lat // 2, lat % 2
    order = []
    for r_core in range(2):
        c = core + r_core - 2 * core * r_core
        y_first = c == (1 if flip else 0)
        for r_first in range(2):
            for r_second in range(2):
                move_y = jnp.where(y_first, r_first, r_second)
                move_x = jnp.where(y_first, r_second, r_first)
                there_y = y + move_y - 2 * y * move_y
                there_x = x + move_x - 2 * x * move_x
                order.append(there_x * 4 + c * 2 + there_y)
    return order


def pack_rows(low_here, high_here, low_grad, high_grad, one, two):
    even = lax.axis_index("lat") % 2 == 0
    for f, (low, high) in enumerate(((low_here, high_here), (low_grad, high_grad))):
        one[f] = jnp.where(even, high[...], low[...])
        two[f] = jnp.where(even, low[...], high[...])


def rows_messages(here, grad):
    rows, cols, channels = here.shape
    block = (2, cols, channels)
    low = pl.BlockSpec(block, lambda i: (0, 0, 0))
    high = pl.BlockSpec(block, lambda i: (rows // 2 - 1, 0, 0))
    shape = (2, *block)
    whole = pl.BlockSpec(shape, lambda i: (0, 0, 0, 0))
    return pl.pallas_call(
        pack_rows,
        grid=(1,),
        out_shape=[jax.ShapeDtypeStruct(shape, F32)] * 2,
        in_specs=[low, high] * 2,
        out_specs=[VMEM] * 2,
        compiler_params=pltpu.CompilerParams(vmem_limit_bytes=4 * 1024 * 1024),
    )(here, here, grad, grad)


def pack_cols(here, grad, one, two, first, second):
    rows, cols = here.shape[:2]
    even_lat = lax.axis_index("lat") % 2 == 0
    even = lax.axis_index("lon") % 2 == 0
    for f, field in enumerate((here, grad)):
        low = jnp.where(even_lat, two[f], one[f])
        high = jnp.where(even_lat, one[f], two[f])
        for c in range(2):
            edges = []
            for col in (c, cols - 2 + c):
                edges.append(
                    jnp.concatenate(
                        [
                            low[:, col],
                            field[:, col],
                            high[:, col],
                            jnp.zeros((LINE - rows - 4, field.shape[2]), F32),
                        ],
                        axis=0,
                    )
                )
            first[f, c] = jnp.where(even, edges[1], edges[0])
            second[f, c] = jnp.where(even, edges[0], edges[1])


def pair_swap(one, two, axis, periodic):
    count = lax.axis_size(axis)
    pairs = [(i, i + 1) for i in range(0, count - 1, 2)]
    mates = [(i, i + 1) for i in range(1, count - 1, 2)]
    if periodic:
        mates.append((count - 1, 0))
    return tuple(
        lax.ppermute(block, axis, who + [(b, a) for a, b in who])
        for block, who in ((one, pairs), (two, mates))
    )


def prepare(weights, high, low):
    high[...], low[...] = split(weights[...])


def prepare_back(weights, high, low):
    size = weights.shape[1]
    for tap in range(9):
        there = 8 - tap
        block = weights[there * size : (there + 1) * size, :].T
        high[tap * size : (tap + 1) * size, :], low[tap * size : (tap + 1) * size, :] = split(block)


def turn(flip, value, high, low, scratch):
    channels = value.shape[1]
    each = channels // 8
    scratch[...] = value.T
    for i, block in enumerate(relative_blocks(flip)):
        part = scratch[pl.ds(pl.multiple_of(block * each, each), each), :]
        high[i * each : (i + 1) * each, :], low[i * each : (i + 1) * each, :] = split(part)


def turn_grad(grad, high, low, scratch):
    cells = grad.shape[0] * grad.shape[1]
    turn(False, grad[...].reshape(cells, grad.shape[2]), high, low, scratch)


def lay_taps(wide, x_high, x_low):
    rows, padded, channels = wide.shape
    cols = padded - 2 * EDGE
    for b in range(3):
        part = wide[:, EDGE - 1 + b : EDGE - 1 + b + cols, :].reshape(rows * cols, channels)
        high, low = split(part)
        x_high[:, b * channels : (b + 1) * channels] = high
        x_low[:, b * channels : (b + 1) * channels] = low


def convolve(x_high, x_low, first_row, rows, cols, w_high, w_low):
    channels = w_high.shape[1]
    total = None
    for a in range(3):
        cells = slice((first_row + a) * cols, (first_row + a + rows) * cols)
        taps = slice(a * 3 * channels, (a + 1) * 3 * channels)
        for x, w in ((x_high, w_high), (x_high, w_low), (x_low, w_high)):
            part = dot(x[cells, :], w[taps, :])
            total = part if total is None else total + part
    return total


def side_columns(mine_one, mine_two, got_one, got_two, f):
    even = lax.axis_index("lon") % 2 == 0

    def either(a, b):
        return jnp.where(even, a, b)

    left = [either(got_two[f, c], got_one[f, c]) for c in range(2)]
    left.append(either(mine_two[f, 0], mine_one[f, 0]))
    right = [either(mine_one[f, 1], mine_two[f, 1])]
    right += [either(got_one[f, c], got_two[f, c]) for c in range(2)]
    return left, right


def ring(left, right, w_high, w_low, r_high, r_low):
    channels = w_high.shape[1]
    for s, columns in enumerate((left, right)):
        for a in range(3):
            for b in range(3):
                high, low = split(columns[b])
                value = columns[b]
                if a:
                    value = jnp.concatenate(
                        [value[a:], jnp.zeros((a, value.shape[1]), F32)], axis=0
                    )
                place = (
                    slice(s * LINE, (s + 1) * LINE),
                    slice((a * 3 + b) * channels, (a * 3 + b + 1) * channels),
                )
                r_high[place], r_low[place] = split(value)
    return (
        dot(r_high[...], w_high[...])
        + dot(r_high[...], w_low[...])
        + dot(r_low[...], w_high[...])
    )


def spread(value, function, got_rows, columns, f, wide):
    rows, cols, channels = value.shape
    even_lat = lax.axis_index("lat") % 2 == 0
    one, two = got_rows
    wide[2 : rows + 2, EDGE : EDGE + cols, :] = function(value[...])
    wide[0:2, EDGE : EDGE + cols, :] = function(jnp.where(even_lat, two[f], one[f]))
    wide[rows + 2 : rows + 4, EDGE : EDGE + cols, :] = function(
        jnp.where(even_lat, one[f], two[f])
    )
    left, right = columns
    wide[:, EDGE - 1 : EDGE, :] = left[1][: rows + 4].reshape(rows + 4, 1, channels)
    wide[:, EDGE + cols : EDGE + cols + 1, :] = right[1][: rows + 4].reshape(rows + 4, 1, channels)


def inside(rows):
    row = lax.axis_index("lat") * rows - 1 + lax.broadcasted_iota(jnp.int32, (rows + 2, 1, 1), 0)
    return (row >= 0) & (row < rows * lax.axis_size("lat"))


def inside_line(rows):
    row = lax.axis_index("lat") * rows - 1 + lax.broadcasted_iota(jnp.int32, (LINE, 1), 0)
    return (row >= 0) & (row < rows * lax.axis_size("lat"))


def spread_ext(main, side, wide):
    tall, cols, channels = main.shape
    wide[:, EDGE : EDGE + cols, :] = main
    wide[:, EDGE - 1 : EDGE, :] = side[:tall].reshape(tall, 1, channels)
    wide[:, EDGE + cols : EDGE + cols + 1, :] = side[LINE : LINE + tall].reshape(tall, 1, channels)


def products(t_high, t_low, x_high, x_low, first_row, cells, cols, scale, away, keep):
    half = t_high.shape[0] // 2
    width = x_high.shape[1]
    for a in range(3):
        rows = slice((first_row + a) * cols, (first_row + a) * cols + cells)
        total = (
            dot(t_high[...], x_high[rows, :])
            + dot(t_high[...], x_low[rows, :])
            + dot(t_low[...], x_high[rows, :])
        ) * scale
        away[:, a * width : (a + 1) * width] = total[half:]
        keep[:, a * width : (a + 1) * width] = total[:half]


def hidden_kernel(
    scale, here, r1, r2, m1, m2, q1, q2, w_high, w_low, t_high, t_low,
    hidden, side, x1_high, x1_low, x2_high, x2_low, away, keep,
    wide, wide2, r_high, r_low,
):
    rows, cols, channels = here.shape
    left, right = side_columns(m1, m2, q1, q2, 0)
    left, right = [silu(v) for v in left], [silu(v) for v in right]
    spread(here, silu, (r1, r2), (left, right), 0, wide)
    lay_taps(wide, x1_high, x1_low)
    main = convolve(x1_high, x1_low, 0, rows + 2, cols, w_high, w_low)
    around = ring(left, right, w_high, w_low, r_high, r_low)
    hidden[...] = main
    side[...] = around
    act = jnp.where(inside(rows), silu(main).reshape(rows + 2, cols, channels), 0.0)
    line = inside_line(rows)
    around = jnp.where(jnp.concatenate([line, line], axis=0), silu(around), 0.0)
    spread_ext(act, around, wide2)
    lay_taps(wide2, x2_high, x2_low)
    products(t_high, t_low, x2_high, x2_low, 0, rows * cols, cols, scale, away, keep)


def inner_kernel(
    grad, r1, r2, m1, m2, q1, q2, w_high, w_low, hidden, side,
    x3_high, x3_low, t_high, t_low,
    wide, xc_high, xc_low, wide2, r_high, r_low, turned,
):
    rows, cols, channels = grad.shape
    columns = side_columns(m1, m2, q1, q2, 1)
    spread(grad, lambda v: v, (r1, r2), columns, 1, wide)
    lay_taps(wide, xc_high, xc_low)
    main = convolve(xc_high, xc_low, 0, rows + 2, cols, w_high, w_low) * slope(hidden[...])
    around = ring(*columns, w_high, w_low, r_high, r_low) * slope(side[...])
    main = jnp.where(inside(rows), main.reshape(rows + 2, cols, channels), 0.0)
    line = inside_line(rows)
    around = jnp.where(jnp.concatenate([line, line], axis=0), around, 0.0)
    turn(True, main[1 : rows + 1].reshape(rows * cols, channels), t_high, t_low, turned)
    spread_ext(main, around, wide2)
    lay_taps(wide2, x3_high, x3_low)


def inner_products(scale, cols, t_high, t_low, x1_high, x1_low, away, keep):
    products(t_high, t_low, x1_high, x1_low, 1, t_high.shape[1], cols, scale, away, keep)


def output_kernel(here, x_high, x_low, w_high, w_low, out):
    rows, cols, channels = here.shape
    total = convolve(x_high, x_low, 0, rows, cols, w_high, w_low)
    out[...] = here[...] + total.reshape(rows, cols, channels)


def input_grad_kernel(here, grad, x_high, x_low, w_high, w_low, out):
    rows, cols, channels = here.shape
    total = convolve(x_high, x_low, 0, rows, cols, w_high, w_low)
    out[...] = grad[...] + total.reshape(rows, cols, channels) * slope(here[...])


def plane_perm(count, even, odd):
    return [(i, i ^ (odd if (i // 2) % 2 else even)) for i in range(count)]


def plane_swap(away, flip, second):
    count = lax.axis_size("lat") * lax.axis_size("rep")
    one, two = (1, 4) if flip == second else (4, 1)
    return lax.ppermute(away, ("lat", "rep"), plane_perm(count, one, two))


def core_swap(away):
    count = lax.axis_size("lat") * lax.axis_size("rep")
    return lax.ppermute(away, ("lat", "rep"), plane_perm(count, 2, 2))


def add_halves(keep, got, next_keep, next_away):
    half = keep.shape[0] // 2
    next_keep[...] = keep[:half] + got[:half]
    next_away[...] = keep[half:] + got[half:]


def add_both(keep_1, got_1, keep_2, got_2, *outs):
    add_halves(keep_1, got_1, *outs[:2])
    add_halves(keep_2, got_2, *outs[2:])


def cut_blocks(keep, got, *blocks):
    total = keep[...] + got[...]
    count = len(blocks)
    size = total.shape[1] // count
    parts = [total[:, i * size : (i + 1) * size] for i in range(count)]
    z = lax.axis_index("lon")
    for step, block in enumerate(blocks):
        value = parts[step]
        for place in range(1, count):
            value = jnp.where(z == place, parts[place ^ step], value)
        block[...] = value


def last_sum(keep, got, after=()):
    each, taps = keep.shape
    lon = lax.axis_size("lon")
    if lon != 4:
        return lax.psum_scatter(keep + got, "lon", scatter_dimension=1, tiled=True).T
    blocks = call(cut_blocks, [((each, taps // lon), F32)] * lon, [keep, got], after=after)
    total = blocks[0]
    for step in range(1, lon):
        total = total + lax.ppermute(blocks[step], "lon", [(i, i ^ step) for i in range(lon)])
    return total.T


def local(inputs, cotangent, first_weight, second_weight):
    here, grad = inputs[0], cotangent[0]
    rows, cols, channels = here.shape
    cells, tall = rows * cols, rows + 2
    width = 3 * channels
    scale = 1.0 / math.sqrt(
        cells * lax.axis_size("rep") * lax.axis_size("lat") * lax.axis_size("lon")
    )
    one, two = rows_messages(here, grad)
    r1, r2 = pair_swap(one, two, "lat", False)
    pair = [((9 * channels, channels), BF16)] * 2
    w1_high, w1_low = call(prepare, pair, [first_weight])
    t_high, t_low = call(
        turn_grad, [((channels, cells), BF16)] * 2, [grad], scratch=[((channels, cells), F32)]
    )
    line = ((2, 2, LINE, channels), F32)
    m1, m2 = call(pack_cols, [line] * 2, [here, grad, r1, r2])
    q1, q2 = pair_swap(m1, m2, "lon", True)
    b2_high, b2_low = call(prepare_back, pair, [second_weight])
    conv_flops = 2 * 3 * 9 * tall * cols * channels * channels
    grad_flops = 2 * 3 * 9 * cells * channels * channels
    lines = ((2 * LINE, channels), F32)
    wide = ((rows + 4, cols + 2 * EDGE, channels), F32)
    wide2 = ((tall, cols + 2 * EDGE, channels), F32)
    taps_1 = [(((rows + 4) * cols, width), BF16)] * 2
    taps_2 = [((tall * cols, width), BF16)] * 2
    around = [((2 * LINE, 3 * width), BF16)] * 2
    halves = [((channels // 2, 9 * channels), F32)] * 2
    hidden, side, x1_high, x1_low, x2_high, x2_low, away, keep = call(
        lambda *refs: hidden_kernel(scale, *refs),
        [((tall * cols, channels), F32), lines] + taps_1 + taps_2 + halves,
        [here, r1, r2, m1, m2, q1, q2, w1_high, w1_low, t_high, t_low],
        conv_flops + grad_flops,
        scratch=[wide, wide2] + around,
    )
    got_2 = core_swap(away)
    keep_2 = keep
    x3_high, x3_low, t_high, t_low = call(
        inner_kernel,
        taps_2 + [((channels, cells), BF16)] * 2,
        [grad, r1, r2, m1, m2, q1, q2, b2_high, b2_low, hidden, side],
        conv_flops,
        scratch=[wide] + taps_1 + [wide2] + around + [((channels, cells), F32)],
    )

    def halves_of(count):
        return [((count, 9 * channels), F32)] * 2

    keep_2, away_2 = call(add_halves, halves_of(channels // 4), [keep_2, got_2], after=[t_low])
    got_2 = plane_swap(away_2, False, False)
    away, keep_1 = call(
        lambda *refs: inner_products(scale, cols, *refs),
        halves,
        [t_high, t_low, x1_high, x1_low],
        grad_flops,
        after=[keep_2],
    )
    got_1 = core_swap(away)
    w2_high, w2_low = call(prepare, pair, [second_weight])
    b1_high, b1_low = call(prepare_back, pair, [first_weight])
    shape = ((rows, cols, channels), F32)
    (output,) = call(
        output_kernel, [shape], [here, x2_high, x2_low, w2_high, w2_low], grad_flops, after=[keep_1]
    )
    keep_1, away_1, keep_2, away_2 = call(
        add_both,
        halves_of(channels // 4) + halves_of(channels // 8),
        [keep_1, got_1, keep_2, got_2],
        after=[output],
    )
    got_1 = plane_swap(away_1, True, False)
    got_2 = plane_swap(away_2, False, True)
    (input_grad,) = call(
        input_grad_kernel,
        [shape],
        [here, grad, x3_high, x3_low, b1_high, b1_low],
        grad_flops,
        after=[keep_2],
    )
    second_grad = last_sum(keep_2, got_2, after=[input_grad])
    keep_1, away_1 = call(add_halves, halves_of(channels // 8), [keep_1, got_1])
    got_1 = plane_swap(away_1, True, True)
    first_grad = last_sum(keep_1, got_1)
    return (output[None], input_grad[None], first_grad, second_grad)


def solution(mesh):
    in_specs = (P("rep", "lat", "lon", None), P("rep", "lat", "lon", None), P(), P())
    out_specs = (
        P("rep", "lat", "lon", None),
        P("rep", "lat", "lon", None),
        P("lon", ("lat", "rep")),
        P("lon", ("lat", "rep")),
    )
    return jax.shard_map(local, mesh=mesh, in_specs=in_specs, out_specs=out_specs, check_vma=False)
```

```python
import math

import jax
import jax.numpy as jnp
from jax import lax
from jax.experimental import pallas as pl
from jax.experimental.pallas import tpu as pltpu
from jax.sharding import PartitionSpec as P

F32 = jnp.float32
BF16 = jnp.bfloat16
VMEM = pl.BlockSpec(memory_space=pltpu.VMEM)
LINE = 24
EDGE = 8


def call(body, outs, ins, scratch=(), limit=16, after=()):
    used, skip = len(ins), len(after)

    def kernel(*refs):
        body(*refs[:used], *refs[used + skip :])

    ins = list(ins) + list(after)
    return pl.pallas_call(
        kernel,
        out_shape=[jax.ShapeDtypeStruct(shape, dtype) for shape, dtype in outs],
        in_specs=[VMEM] * used + [pl.BlockSpec(memory_space=pl.ANY)] * skip,
        out_specs=[VMEM] * len(outs),
        scratch_shapes=[pltpu.VMEM(shape, dtype) for shape, dtype in scratch],
        compiler_params=pltpu.CompilerParams(vmem_limit_bytes=limit * 1024 * 1024),
        cost_estimate=pl.CostEstimate(flops=0, bytes_accessed=0, transcendentals=0),
    )(*ins)


def split(value):
    high = value.astype(BF16)
    return high, (value - high.astype(F32)).astype(BF16)


def dot(a, b):
    return jnp.dot(a, b, preferred_element_type=F32)


def sigmoid(value):
    return 0.5 * jnp.tanh(0.5 * value) + 0.5


def silu(value):
    return value * sigmoid(value)


def slope(value):
    sigma = sigmoid(value)
    return sigma * (1.0 + value * (1.0 - sigma))


def relative_blocks():
    lat, y = lax.axis_index("lat"), lax.axis_index("rep")
    x, core = lat // 2, lat % 2
    order = []
    for r_core in range(2):
        c = core + r_core - 2 * core * r_core
        y_first = c == 0
        for r_first in range(2):
            for r_second in range(2):
                move_y = jnp.where(y_first, r_first, r_second)
                move_x = jnp.where(y_first, r_second, r_first)
                there_y = y + move_y - 2 * y * move_y
                there_x = x + move_x - 2 * x * move_x
                order.append(there_x * 4 + c * 2 + there_y)
    return order


def pack_rows(low_here, high_here, low_grad, high_grad, one, two):
    even = lax.axis_index("lat") % 2 == 0
    for f, (low, high) in enumerate(((low_here, high_here), (low_grad, high_grad))):
        one[f] = jnp.where(even, high[...], low[...])
        two[f] = jnp.where(even, low[...], high[...])


def pack_cols(here, grad, one, two, first, second):
    rows, cols = here.shape[:2]
    even_lat = lax.axis_index("lat") % 2 == 0
    even = lax.axis_index("lon") % 2 == 0
    for f, field in enumerate((here, grad)):
        low = jnp.where(even_lat, two[f], one[f])
        high = jnp.where(even_lat, one[f], two[f])
        for c in range(2):
            edges = []
            for col in (c, cols - 2 + c):
                edges.append(
                    jnp.concatenate(
                        [
                            low[:, col],
                            field[:, col],
                            high[:, col],
                            jnp.zeros((LINE - rows - 4, field.shape[2]), F32),
                        ],
                        axis=0,
                    )
                )
            first[f, c] = jnp.where(even, edges[1], edges[0])
            second[f, c] = jnp.where(even, edges[0], edges[1])


def pair_swap(one, two, axis, periodic):
    count = lax.axis_size(axis)
    pairs = [(i, i + 1) for i in range(0, count - 1, 2)]
    mates = [(i, i + 1) for i in range(1, count - 1, 2)]
    if periodic:
        mates.append((count - 1, 0))
    return tuple(
        lax.ppermute(block, axis, who + [(b, a) for a, b in who])
        for block, who in ((one, pairs), (two, mates))
    )


def prepare(weights, high, low):
    high[...], low[...] = split(weights[...])


def prepare_back(weights, high, low):
    size = weights.shape[1]
    for tap in range(9):
        there = 8 - tap
        block = weights[there * size : (there + 1) * size, :].T
        high[tap * size : (tap + 1) * size, :], low[tap * size : (tap + 1) * size, :] = split(block)


def turn(value, high, low, scratch):
    channels = value.shape[1]
    each = channels // 8
    scratch[...] = value.T
    for i, block in enumerate(relative_blocks()):
        part = scratch[pl.ds(pl.multiple_of(block * each, each), each), :]
        high[i * each : (i + 1) * each, :], low[i * each : (i + 1) * each, :] = split(part)


def turn_grad(grad, high, low, scratch):
    cells = grad.shape[0] * grad.shape[1]
    turn(grad[...].reshape(cells, grad.shape[2]), high, low, scratch)


def lay_taps(wide, x_high, x_low):
    rows, padded, channels = wide.shape
    cols = padded - 2 * EDGE
    for b in range(3):
        part = wide[:, EDGE - 1 + b : EDGE - 1 + b + cols, :].reshape(rows * cols, channels)
        high, low = split(part)
        x_high[:, b * channels : (b + 1) * channels] = high
        x_low[:, b * channels : (b + 1) * channels] = low


def convolve(x_high, x_low, first_row, rows, cols, w_high, w_low):
    channels = w_high.shape[1]
    total = None
    for a in range(3):
        cells = slice((first_row + a) * cols, (first_row + a + rows) * cols)
        taps = slice(a * 3 * channels, (a + 1) * 3 * channels)
        for x, w in ((x_high, w_high), (x_high, w_low), (x_low, w_high)):
            part = dot(x[cells, :], w[taps, :])
            total = part if total is None else total + part
    return total


def side_columns(mine_one, mine_two, got_one, got_two, f):
    even = lax.axis_index("lon") % 2 == 0

    def either(a, b):
        return jnp.where(even, a, b)

    left = [either(got_two[f, c], got_one[f, c]) for c in range(2)]
    left.append(either(mine_two[f, 0], mine_one[f, 0]))
    right = [either(mine_one[f, 1], mine_two[f, 1])]
    right += [either(got_one[f, c], got_two[f, c]) for c in range(2)]
    return left, right


def ring(left, right, w_high, w_low, r_high, r_low):
    channels = w_high.shape[1]
    for s, columns in enumerate((left, right)):
        for a in range(3):
            for b in range(3):
                high, low = split(columns[b])
                value = columns[b]
                if a:
                    value = jnp.concatenate(
                        [value[a:], jnp.zeros((a, value.shape[1]), F32)], axis=0
                    )
                place = (
                    slice(s * LINE, (s + 1) * LINE),
                    slice((a * 3 + b) * channels, (a * 3 + b + 1) * channels),
                )
                r_high[place], r_low[place] = split(value)
    return (
        dot(r_high[...], w_high[...])
        + dot(r_high[...], w_low[...])
        + dot(r_low[...], w_high[...])
    )


def spread(value, function, got_rows, columns, f, wide):
    rows, cols, channels = value.shape
    even_lat = lax.axis_index("lat") % 2 == 0
    one, two = got_rows
    wide[2 : rows + 2, EDGE : EDGE + cols, :] = function(value[...])
    wide[0:2, EDGE : EDGE + cols, :] = function(jnp.where(even_lat, two[f], one[f]))
    wide[rows + 2 : rows + 4, EDGE : EDGE + cols, :] = function(
        jnp.where(even_lat, one[f], two[f])
    )
    left, right = columns
    wide[:, EDGE - 1 : EDGE, :] = left[1][: rows + 4].reshape(rows + 4, 1, channels)
    wide[:, EDGE + cols : EDGE + cols + 1, :] = right[1][: rows + 4].reshape(rows + 4, 1, channels)


def inside(rows):
    row = lax.axis_index("lat") * rows - 1 + lax.broadcasted_iota(jnp.int32, (rows + 2, 1, 1), 0)
    return (row >= 0) & (row < rows * lax.axis_size("lat"))


def inside_line(rows):
    row = lax.axis_index("lat") * rows - 1 + lax.broadcasted_iota(jnp.int32, (LINE, 1), 0)
    return (row >= 0) & (row < rows * lax.axis_size("lat"))


def spread_ext(main, side, wide):
    tall, cols, channels = main.shape
    wide[:, EDGE : EDGE + cols, :] = main
    wide[:, EDGE - 1 : EDGE, :] = side[:tall].reshape(tall, 1, channels)
    wide[:, EDGE + cols : EDGE + cols + 1, :] = side[LINE : LINE + tall].reshape(tall, 1, channels)


def products(t_high, t_low, x_high, x_low, first_row, cells, cols, scale, away, keep):
    half = t_high.shape[0] // 2
    width = x_high.shape[1]
    for a in range(3):
        rows = slice((first_row + a) * cols, (first_row + a) * cols + cells)
        total = (
            dot(t_high[...], x_high[rows, :])
            + dot(t_high[...], x_low[rows, :])
            + dot(t_low[...], x_high[rows, :])
        ) * scale
        away[:, a * width : (a + 1) * width] = total[half:]
        keep[:, a * width : (a + 1) * width] = total[:half]


def hidden_kernel(
    scale, here, r1, r2, m1, m2, q1, q2, w_high, w_low, t_high, t_low,
    hidden, side, x1_high, x1_low, x2_high, x2_low, away, keep,
    wide, wide2, r_high, r_low,
):
    rows, cols, channels = here.shape
    left, right = side_columns(m1, m2, q1, q2, 0)
    left, right = [silu(v) for v in left], [silu(v) for v in right]
    spread(here, silu, (r1, r2), (left, right), 0, wide)
    lay_taps(wide, x1_high, x1_low)
    main = convolve(x1_high, x1_low, 0, rows + 2, cols, w_high, w_low)
    around = ring(left, right, w_high, w_low, r_high, r_low)
    hidden[...] = main
    side[...] = around
    act = jnp.where(inside(rows), silu(main).reshape(rows + 2, cols, channels), 0.0)
    line = inside_line(rows)
    around = jnp.where(jnp.concatenate([line, line], axis=0), silu(around), 0.0)
    spread_ext(act, around, wide2)
    lay_taps(wide2, x2_high, x2_low)
    products(t_high, t_low, x2_high, x2_low, 0, rows * cols, cols, scale, away, keep)


def inner_kernel(
    grad, r1, r2, m1, m2, q1, q2, w_high, w_low, hidden, side,
    x3_high, x3_low, t_high, t_low,
    wide, xc_high, xc_low, wide2, r_high, r_low, turned,
):
    rows, cols, channels = grad.shape
    columns = side_columns(m1, m2, q1, q2, 1)
    spread(grad, lambda v: v, (r1, r2), columns, 1, wide)
    lay_taps(wide, xc_high, xc_low)
    main = convolve(xc_high, xc_low, 0, rows + 2, cols, w_high, w_low) * slope(hidden[...])
    around = ring(*columns, w_high, w_low, r_high, r_low) * slope(side[...])
    main = jnp.where(inside(rows), main.reshape(rows + 2, cols, channels), 0.0)
    line = inside_line(rows)
    around = jnp.where(jnp.concatenate([line, line], axis=0), around, 0.0)
    turn(main[1 : rows + 1].reshape(rows * cols, channels), t_high, t_low, turned)
    spread_ext(main, around, wide2)
    lay_taps(wide2, x3_high, x3_low)


def inner_products(scale, cols, t_high, t_low, x1_high, x1_low, away, keep):
    products(t_high, t_low, x1_high, x1_low, 1, t_high.shape[1], cols, scale, away, keep)


def output_kernel(here, x_high, x_low, w_high, w_low, out, token):
    token[...] = jnp.zeros(token.shape, F32)
    rows, cols, channels = here.shape
    total = convolve(x_high, x_low, 0, rows, cols, w_high, w_low)
    out[...] = here[...] + total.reshape(rows, cols, channels)


def input_grad_kernel(here, grad, x_high, x_low, w_high, w_low, out, token):
    token[...] = jnp.zeros(token.shape, F32)
    rows, cols, channels = here.shape
    total = convolve(x_high, x_low, 0, rows, cols, w_high, w_low)
    out[...] = grad[...] + total.reshape(rows, cols, channels) * slope(here[...])


def plane_perm(count, even, odd):
    return [(i, i ^ (odd if (i // 2) % 2 else even)) for i in range(count)]


def plane_swap(away, second):
    count = lax.axis_size("lat") * lax.axis_size("rep")
    one, two = (4, 1) if second else (1, 4)
    return lax.ppermute(away, ("lat", "rep"), plane_perm(count, one, two))


def core_swap(away):
    count = lax.axis_size("lat") * lax.axis_size("rep")
    return lax.ppermute(away, ("lat", "rep"), plane_perm(count, 2, 2))


def add_halves(keep, got, next_keep, next_away):
    half = keep.shape[0] // 2
    next_keep[...] = keep[:half] + got[:half]
    next_away[...] = keep[half:] + got[half:]


def cut_blocks(keep, got, *blocks):
    total = keep[...] + got[...]
    count = len(blocks)
    size = total.shape[1] // count
    parts = [total[:, i * size : (i + 1) * size] for i in range(count)]
    z = lax.axis_index("lon")
    for step, block in enumerate(blocks):
        value = parts[step]
        for place in range(1, count):
            value = jnp.where(z == place, parts[place ^ step], value)
        block[...] = value


def last_sum(keep, got, after=()):
    each, taps = keep.shape
    lon = lax.axis_size("lon")
    if lon != 4:
        return lax.psum_scatter(keep + got, "lon", scatter_dimension=1, tiled=True).T
    blocks = call(cut_blocks, [((each, taps // lon), F32)] * lon, [keep, got], after=after)
    total = blocks[0]
    for step in range(1, lon):
        total = total + lax.ppermute(blocks[step], "lon", [(i, i ^ step) for i in range(lon)])
    return total.T


def local(inputs, cotangent, first_weight, second_weight):
    here, grad = inputs[0], cotangent[0]
    rows, cols, channels = here.shape
    cells, tall = rows * cols, rows + 2
    width = 3 * channels
    scale = 1.0 / math.sqrt(
        cells * lax.axis_size("rep") * lax.axis_size("lat") * lax.axis_size("lon")
    )
    edge = ((2, 2, cols, channels), F32)
    edges = [here[:2], here[rows - 2 :], grad[:2], grad[rows - 2 :]]
    one, two = call(pack_rows, [edge] * 2, edges)
    r1, r2 = pair_swap(one, two, "lat", False)
    pair = [((9 * channels, channels), BF16)] * 2
    w1_high, w1_low = call(prepare, pair, [first_weight])
    t_high, t_low = call(
        turn_grad, [((channels, cells), BF16)] * 2, [grad], scratch=[((channels, cells), F32)]
    )
    line = ((2, 2, LINE, channels), F32)
    m1, m2 = call(pack_cols, [line] * 2, [here, grad, r1, r2])
    q1, q2 = pair_swap(m1, m2, "lon", True)
    b2_high, b2_low = call(prepare_back, pair, [second_weight])
    lines = ((2 * LINE, channels), F32)
    wide = ((rows + 4, cols + 2 * EDGE, channels), F32)
    wide2 = ((tall, cols + 2 * EDGE, channels), F32)
    taps_1 = [(((rows + 4) * cols, width), BF16)] * 2
    taps_2 = [((tall * cols, width), BF16)] * 2
    around = [((2 * LINE, 3 * width), BF16)] * 2
    halves = [((channels // 2, 9 * channels), F32)] * 2
    hidden, side, x1_high, x1_low, x2_high, x2_low, away, keep = call(
        lambda *refs: hidden_kernel(scale, *refs),
        [((tall * cols, channels), F32), lines] + taps_1 + taps_2 + halves,
        [here, r1, r2, m1, m2, q1, q2, w1_high, w1_low, t_high, t_low],
        scratch=[wide, wide2] + around,
    )
    got_2 = core_swap(away)
    keep_2 = keep
    x3_high, x3_low, t_high, t_low = call(
        inner_kernel,
        taps_2 + [((channels, cells), BF16)] * 2,
        [grad, r1, r2, m1, m2, q1, q2, b2_high, b2_low, hidden, side],
        scratch=[wide] + taps_1 + [wide2] + around + [((channels, cells), F32)],
    )

    def halves_of(count):
        return [((count, 9 * channels), F32)] * 2

    keep_2, away_2 = call(add_halves, halves_of(channels // 4), [keep_2, got_2], after=[t_low])
    got_2 = plane_swap(away_2, False)
    away, keep_1 = call(
        lambda *refs: inner_products(scale, cols, *refs),
        halves,
        [t_high, t_low, x1_high, x1_low],
        after=[keep_2],
    )
    got_1 = core_swap(away)
    keep_1, away_1 = call(add_halves, halves_of(channels // 4), [keep_1, got_1])
    got_1 = plane_swap(away_1, False)
    w2_high, w2_low = call(prepare, pair, [second_weight])
    b1_high, b1_low = call(prepare_back, pair, [first_weight])
    outs = [((rows, cols, channels), F32), ((8, 128), F32)]
    output, token = call(
        output_kernel, outs, [here, x2_high, x2_low, w2_high, w2_low], after=[keep_1]
    )
    keep_2, away_2 = call(add_halves, halves_of(channels // 8), [keep_2, got_2], after=[token])
    got_2 = plane_swap(away_2, True)
    input_grad, token = call(
        input_grad_kernel,
        outs,
        [here, grad, x3_high, x3_low, b1_high, b1_low],
        after=[keep_2],
    )
    keep_1, away_1 = call(add_halves, halves_of(channels // 8), [keep_1, got_1], after=[token])
    got_1 = plane_swap(away_1, True)
    second_grad = last_sum(keep_2, got_2, after=[keep_1])
    first_grad = last_sum(keep_1, got_1)
    return (output[None], input_grad[None], first_grad, second_grad)


def solution(mesh):
    in_specs = (P("rep", "lat", "lon", None), P("rep", "lat", "lon", None), P(), P())
    out_specs = (
        P("rep", "lat", "lon", None),
        P("rep", "lat", "lon", None),
        P("lon", ("lat", "rep")),
        P("lon", ("lat", "rep")),
    )
    return jax.shard_map(local, mesh=mesh, in_specs=in_specs, out_specs=out_specs, check_vma=False)
```

```python
import math

import jax
import jax.numpy as jnp
from jax import lax
from jax.experimental import pallas as pl
from jax.experimental.pallas import tpu as pltpu
from jax.sharding import PartitionSpec as P

F32 = jnp.float32
BF16 = jnp.bfloat16
VMEM = pl.BlockSpec(memory_space=pltpu.VMEM)
PIECES = 4
LINE = 24
EDGE = 8


def call(body, outs, ins, scratch=(), limit=16, after=()):
    used, skip = len(ins), len(after)

    def kernel(*refs):
        body(*refs[:used], *refs[used + skip :])

    ins = list(ins) + list(after)
    return pl.pallas_call(
        kernel,
        out_shape=[jax.ShapeDtypeStruct(shape, dtype) for shape, dtype in outs],
        in_specs=[VMEM] * used + [pl.BlockSpec(memory_space=pl.ANY)] * skip,
        out_specs=[VMEM] * len(outs),
        scratch_shapes=[pltpu.VMEM(shape, dtype) for shape, dtype in scratch],
        compiler_params=pltpu.CompilerParams(vmem_limit_bytes=limit * 1024 * 1024),
        cost_estimate=pl.CostEstimate(flops=0, bytes_accessed=0, transcendentals=0),
    )(*ins)


def split(value):
    high = value.astype(BF16)
    return high, (value - high.astype(F32)).astype(BF16)


def dot(a, b):
    return jnp.dot(a, b, preferred_element_type=F32)


def sigmoid(value):
    return 0.5 * jnp.tanh(0.5 * value) + 0.5


def silu(value):
    return value * sigmoid(value)


def slope(value):
    sigma = sigmoid(value)
    return sigma * (1.0 + value * (1.0 - sigma))


def relative_blocks():
    lat, y = lax.axis_index("lat"), lax.axis_index("rep")
    x, core = lat // 2, lat % 2
    order = []
    for r_core in range(2):
        c = core + r_core - 2 * core * r_core
        y_first = c == 0
        for r_first in range(2):
            for r_second in range(2):
                move_y = jnp.where(y_first, r_first, r_second)
                move_x = jnp.where(y_first, r_second, r_first)
                there_y = y + move_y - 2 * y * move_y
                there_x = x + move_x - 2 * x * move_x
                order.append(there_x * 4 + c * 2 + there_y)
    return order


def pack_rows(low_here, high_here, low_grad, high_grad, one, two):
    even = lax.axis_index("lat") % 2 == 0
    for f, (low, high) in enumerate(((low_here, high_here), (low_grad, high_grad))):
        one[f] = jnp.where(even, high[...], low[...])
        two[f] = jnp.where(even, low[...], high[...])


def pack_cols(here, grad, one, two, first, second):
    rows, cols = here.shape[:2]
    even_lat = lax.axis_index("lat") % 2 == 0
    even = lax.axis_index("lon") % 2 == 0
    for f, field in enumerate((here, grad)):
        low = jnp.where(even_lat, two[f], one[f])
        high = jnp.where(even_lat, one[f], two[f])
        for c in range(2):
            edges = []
            for col in (c, cols - 2 + c):
                edges.append(
                    jnp.concatenate(
                        [
                            low[:, col],
                            field[:, col],
                            high[:, col],
                            jnp.zeros((LINE - rows - 4, field.shape[2]), F32),
                        ],
                        axis=0,
                    )
                )
            first[f, c] = jnp.where(even, edges[1], edges[0])
            second[f, c] = jnp.where(even, edges[0], edges[1])


def pair_swap(one, two, axis, periodic):
    count = lax.axis_size(axis)
    pairs = [(i, i + 1) for i in range(0, count - 1, 2)]
    mates = [(i, i + 1) for i in range(1, count - 1, 2)]
    if periodic:
        mates.append((count - 1, 0))
    return tuple(
        lax.ppermute(block, axis, who + [(b, a) for a, b in who])
        for block, who in ((one, pairs), (two, mates))
    )


def prepare(weights, high, low):
    high[...], low[...] = split(weights[...])


def prepare_back(weights, high, low):
    size = weights.shape[1]
    for tap in range(9):
        there = 8 - tap
        block = weights[there * size : (there + 1) * size, :].T
        high[tap * size : (tap + 1) * size, :], low[tap * size : (tap + 1) * size, :] = split(block)


def turn(value, high, low, scratch):
    channels = value.shape[1]
    each = channels // 8
    scratch[...] = value.T
    for i, block in enumerate(relative_blocks()):
        part = scratch[pl.ds(pl.multiple_of(block * each, each), each), :]
        high[i * each : (i + 1) * each, :], low[i * each : (i + 1) * each, :] = split(part)


def turn_grad(here, grad, act, high, low, scratch):
    cells = grad.shape[0] * grad.shape[1]
    act[...] = silu(here[...])
    turn(grad[...].reshape(cells, grad.shape[2]), high, low, scratch)


def lay_taps(wide, x_high, x_low):
    rows, padded, channels = wide.shape
    cols = padded - 2 * EDGE
    for b in range(3):
        part = wide[:, EDGE - 1 + b : EDGE - 1 + b + cols, :].reshape(rows * cols, channels)
        high, low = split(part)
        x_high[:, b * channels : (b + 1) * channels] = high
        x_low[:, b * channels : (b + 1) * channels] = low


def convolve(x_high, x_low, first_row, rows, cols, w_high, w_low):
    channels = w_high.shape[1]
    total = None
    for a in range(3):
        cells = slice((first_row + a) * cols, (first_row + a + rows) * cols)
        taps = slice(a * 3 * channels, (a + 1) * 3 * channels)
        for x, w in ((x_high, w_high), (x_high, w_low), (x_low, w_high)):
            part = dot(x[cells, :], w[taps, :])
            total = part if total is None else total + part
    return total


def side_columns(mine_one, mine_two, got_one, got_two, f):
    even = lax.axis_index("lon") % 2 == 0

    def either(a, b):
        return jnp.where(even, a, b)

    left = [either(got_two[f, c], got_one[f, c]) for c in range(2)]
    left.append(either(mine_two[f, 0], mine_one[f, 0]))
    right = [either(mine_one[f, 1], mine_two[f, 1])]
    right += [either(got_one[f, c], got_two[f, c]) for c in range(2)]
    return left, right


def ring(left, right, w_high, w_low, r_high, r_low):
    channels = w_high.shape[1]
    for s, columns in enumerate((left, right)):
        for a in range(3):
            for b in range(3):
                high, low = split(columns[b])
                value = columns[b]
                if a:
                    value = jnp.concatenate(
                        [value[a:], jnp.zeros((a, value.shape[1]), F32)], axis=0
                    )
                place = (
                    slice(s * LINE, (s + 1) * LINE),
                    slice((a * 3 + b) * channels, (a * 3 + b + 1) * channels),
                )
                r_high[place], r_low[place] = split(value)
    return (
        dot(r_high[...], w_high[...])
        + dot(r_high[...], w_low[...])
        + dot(r_low[...], w_high[...])
    )


def spread(value, function, got_rows, columns, f, wide):
    rows, cols, channels = value.shape
    even_lat = lax.axis_index("lat") % 2 == 0
    one, two = got_rows
    wide[2 : rows + 2, EDGE : EDGE + cols, :] = value[...]
    wide[0:2, EDGE : EDGE + cols, :] = function(jnp.where(even_lat, two[f], one[f]))
    wide[rows + 2 : rows + 4, EDGE : EDGE + cols, :] = function(
        jnp.where(even_lat, one[f], two[f])
    )
    left, right = columns
    wide[:, EDGE - 1 : EDGE, :] = left[1][: rows + 4].reshape(rows + 4, 1, channels)
    wide[:, EDGE + cols : EDGE + cols + 1, :] = right[1][: rows + 4].reshape(rows + 4, 1, channels)


def inside(rows):
    row = lax.axis_index("lat") * rows - 1 + lax.broadcasted_iota(jnp.int32, (rows + 2, 1, 1), 0)
    return (row >= 0) & (row < rows * lax.axis_size("lat"))


def inside_line(rows):
    row = lax.axis_index("lat") * rows - 1 + lax.broadcasted_iota(jnp.int32, (LINE, 1), 0)
    return (row >= 0) & (row < rows * lax.axis_size("lat"))


def spread_ext(main, side, wide):
    tall, cols, channels = main.shape
    wide[:, EDGE : EDGE + cols, :] = main
    wide[:, EDGE - 1 : EDGE, :] = side[:tall].reshape(tall, 1, channels)
    wide[:, EDGE + cols : EDGE + cols + 1, :] = side[LINE : LINE + tall].reshape(tall, 1, channels)


def products(t_high, t_low, x_high, x_low, first_row, cells, cols, scale, *outs):
    half = t_high.shape[0] // 2
    width = x_high.shape[1]
    for a in range(3):
        rows = slice((first_row + a) * cols, (first_row + a) * cols + cells)
        total = (
            dot(t_high[...], x_high[rows, :])
            + dot(t_high[...], x_low[rows, :])
            + dot(t_low[...], x_high[rows, :])
        ) * scale
        *aways, keep = outs
        keep[:, a * width : (a + 1) * width] = total[:half]
        size = half // len(aways)
        for i, away in enumerate(aways):
            part = total[half + i * size : half + (i + 1) * size]
            away[:, a * width : (a + 1) * width] = part


def hidden_kernel(
    act, r1, r2, m1, m2, q1, q2, w_high, w_low,
    hidden, side, x1_high, x1_low, x2_high, x2_low,
    wide, wide2, r_high, r_low,
):
    rows, cols, channels = act.shape
    left, right = side_columns(m1, m2, q1, q2, 0)
    left, right = [silu(v) for v in left], [silu(v) for v in right]
    spread(act, silu, (r1, r2), (left, right), 0, wide)
    lay_taps(wide, x1_high, x1_low)
    main = convolve(x1_high, x1_low, 0, rows + 2, cols, w_high, w_low)
    around = ring(left, right, w_high, w_low, r_high, r_low)
    hidden[...] = main
    side[...] = around
    after = jnp.where(inside(rows), silu(main).reshape(rows + 2, cols, channels), 0.0)
    line = inside_line(rows)
    around = jnp.where(jnp.concatenate([line, line], axis=0), silu(around), 0.0)
    spread_ext(after, around, wide2)
    lay_taps(wide2, x2_high, x2_low)


def inner_kernel(
    grad, r1, r2, m1, m2, q1, q2, w_high, w_low, hidden, side,
    x3_high, x3_low, t_high, t_low,
    wide, xc_high, xc_low, wide2, r_high, r_low, turned,
):
    rows, cols, channels = grad.shape
    columns = side_columns(m1, m2, q1, q2, 1)
    spread(grad, lambda v: v, (r1, r2), columns, 1, wide)
    lay_taps(wide, xc_high, xc_low)
    main = convolve(xc_high, xc_low, 0, rows + 2, cols, w_high, w_low) * slope(hidden[...])
    around = ring(*columns, w_high, w_low, r_high, r_low) * slope(side[...])
    main = jnp.where(inside(rows), main.reshape(rows + 2, cols, channels), 0.0)
    line = inside_line(rows)
    around = jnp.where(jnp.concatenate([line, line], axis=0), around, 0.0)
    turn(main[1 : rows + 1].reshape(rows * cols, channels), t_high, t_low, turned)
    spread_ext(main, around, wide2)
    lay_taps(wide2, x3_high, x3_low)


def products_kernel(scale, cols, first_row, t_high, t_low, x_high, x_low, *outs):
    products(t_high, t_low, x_high, x_low, first_row, t_high.shape[1], cols, scale, *outs)


def output_kernel(here, x_high, x_low, w_high, w_low, out, token):
    token[...] = jnp.zeros(token.shape, F32)
    rows, cols, channels = here.shape
    total = convolve(x_high, x_low, 0, rows, cols, w_high, w_low)
    out[...] = here[...] + total.reshape(rows, cols, channels)


def input_grad_kernel(here, grad, x_high, x_low, w_high, w_low, out, token):
    token[...] = jnp.zeros(token.shape, F32)
    rows, cols, channels = here.shape
    total = convolve(x_high, x_low, 0, rows, cols, w_high, w_low)
    out[...] = grad[...] + total.reshape(rows, cols, channels) * slope(here[...])


def plane_perm(count, even, odd):
    return [(i, i ^ (odd if (i // 2) % 2 else even)) for i in range(count)]


def plane_swap(away, second):
    count = lax.axis_size("lat") * lax.axis_size("rep")
    one, two = (4, 1) if second else (1, 4)
    return lax.ppermute(away, ("lat", "rep"), plane_perm(count, one, two))


def core_swap(away):
    count = lax.axis_size("lat") * lax.axis_size("rep")
    return lax.ppermute(away, ("lat", "rep"), plane_perm(count, 2, 2))


def add_halves(keep, got, next_keep, next_away, *token):
    for ref in token:
        ref[...] = jnp.zeros(ref.shape, F32)
    half = keep.shape[0] // 2
    next_keep[...] = keep[:half] + got[:half]
    next_away[...] = keep[half:] + got[half:]


def add_pieces(keep, *refs):
    *gots, next_keep, next_away = refs
    size = gots[0].shape[0]
    for i, got in enumerate(gots):
        value = keep[i * size : (i + 1) * size] + got[...]
        target = next_keep if i < len(gots) // 2 else next_away
        place = i % (len(gots) // 2) * size
        target[place : place + size] = value


def cut_blocks(keep, got, *blocks):
    total = keep[...] + got[...]
    count = len(blocks)
    size = total.shape[1] // count
    parts = [total[:, i * size : (i + 1) * size] for i in range(count)]
    z = lax.axis_index("lon")
    for step, block in enumerate(blocks):
        value = parts[step]
        for place in range(1, count):
            value = jnp.where(z == place, parts[place ^ step], value)
        block[...] = value


def wide_sum(keep, got):
    return lax.psum_scatter(keep + got, "lon", scatter_dimension=1, tiled=True).T


def last_sum(keep, got, after=()):
    each, taps = keep.shape
    lon = lax.axis_size("lon")
    if lon != 4:
        return wide_sum(keep, got)
    blocks = call(cut_blocks, [((each, taps // lon), F32)] * lon, [keep, got], after=after)
    total = blocks[0]
    for step in (3, 2, 1):
        total = total + lax.ppermute(blocks[step], "lon", [(i, i ^ step) for i in range(lon)])
    return total.T


def local(inputs, cotangent, first_weight, second_weight):
    here, grad = inputs[0], cotangent[0]
    rows, cols, channels = here.shape
    cells, tall = rows * cols, rows + 2
    width = 3 * channels
    scale = 1.0 / math.sqrt(
        cells * lax.axis_size("rep") * lax.axis_size("lat") * lax.axis_size("lon")
    )
    edge = ((2, 2, cols, channels), F32)
    edges = [here[:2], here[rows - 2 :], grad[:2], grad[rows - 2 :]]
    one, two = call(pack_rows, [edge] * 2, edges)
    r1, r2 = pair_swap(one, two, "lat", False)
    pair = [((9 * channels, channels), BF16)] * 2
    w1_high, w1_low = call(prepare, pair, [first_weight])
    act, t_high, t_low = call(
        turn_grad,
        [((rows, cols, channels), F32)] + [((channels, cells), BF16)] * 2,
        [here, grad],
        scratch=[((channels, cells), F32)],
    )
    line = ((2, 2, LINE, channels), F32)
    m1, m2 = call(pack_cols, [line] * 2, [here, grad, r1, r2], after=[t_low])
    q1, q2 = pair_swap(m1, m2, "lon", True)
    b2_high, b2_low = call(prepare_back, pair, [second_weight])
    lines = ((2 * LINE, channels), F32)
    wide = ((rows + 4, cols + 2 * EDGE, channels), F32)
    wide2 = ((tall, cols + 2 * EDGE, channels), F32)
    taps_1 = [(((rows + 4) * cols, width), BF16)] * 2
    taps_2 = [((tall * cols, width), BF16)] * 2
    around = [((2 * LINE, 3 * width), BF16)] * 2
    halves = [((channels // 2, 9 * channels), F32)] * 2
    hidden, side, x1_high, x1_low, x2_high, x2_low = call(
        hidden_kernel,
        [((tall * cols, channels), F32), lines] + taps_1 + taps_2,
        [act, r1, r2, m1, m2, q1, q2, w1_high, w1_low],
        scratch=[wide, wide2] + around,
    )
    away, keep = call(
        lambda *refs: products_kernel(scale, cols, 0, *refs),
        halves,
        [t_high, t_low, x2_high, x2_low],
    )
    got_2 = core_swap(away)
    keep_2 = keep
    x3_high, x3_low, t_high, t_low = call(
        inner_kernel,
        taps_2 + [((channels, cells), BF16)] * 2,
        [grad, r1, r2, m1, m2, q1, q2, b2_high, b2_low, hidden, side],
        scratch=[wide] + taps_1 + [wide2] + around + [((channels, cells), F32)],
    )

    def halves_of(count):
        return [((count, 9 * channels), F32)] * 2

    keep_2, away_2 = call(add_halves, halves_of(channels // 4), [keep_2, got_2], after=[t_low])
    got_2 = plane_swap(away_2, False)
    *aways, keep_1 = call(
        lambda *refs: products_kernel(scale, cols, 1, *refs),
        [((channels // 2 // PIECES, 9 * channels), F32)] * PIECES + halves[:1],
        [t_high, t_low, x1_high, x1_low],
        after=[keep_2],
    )
    gots = [core_swap(away) for away in aways]
    keep_1, away_1 = call(add_pieces, halves_of(channels // 4), [keep_1, *gots])
    got_1 = plane_swap(away_1, False)
    w2_high, w2_low = call(prepare, pair, [second_weight])
    b1_high, b1_low = call(prepare_back, pair, [first_weight])
    outs = [((rows, cols, channels), F32), ((8, 128), F32)]
    output, token = call(
        output_kernel, outs, [here, x2_high, x2_low, w2_high, w2_low], after=[keep_1]
    )
    keep_2, away_2 = call(add_halves, halves_of(channels // 8), [keep_2, got_2], after=[token])
    got_2 = plane_swap(away_2, True)
    input_grad, token = call(
        input_grad_kernel,
        outs,
        [here, grad, x3_high, x3_low, b1_high, b1_low],
        after=[keep_2],
    )
    each = channels // 8
    keep_1, away_1 = call(add_halves, halves_of(each), [keep_1, got_1], after=[token])
    got_1 = plane_swap(away_1, True)
    second_grad = last_sum(keep_2, got_2, after=[keep_1])
    first_grad = last_sum(keep_1, got_1)
    return (output[None], input_grad[None], first_grad, second_grad)


def solution(mesh):
    in_specs = (P("rep", "lat", "lon", None), P("rep", "lat", "lon", None), P(), P())
    out_specs = (
        P("rep", "lat", "lon", None),
        P("rep", "lat", "lon", None),
        P("lon", ("lat", "rep")),
        P("lon", ("lat", "rep")),
    )
    return jax.shard_map(local, mesh=mesh, in_specs=in_specs, out_specs=out_specs, check_vma=False)
```

```python
import math

import jax
import jax.numpy as jnp
from jax import lax
from jax.experimental import pallas as pl
from jax.experimental.pallas import tpu as pltpu
from jax.sharding import PartitionSpec as P

F32 = jnp.float32
BF16 = jnp.bfloat16
VMEM = pl.BlockSpec(memory_space=pltpu.VMEM)
LONG = 10**10
LINE = 24
EDGE = 8


def call(body, outs, ins, scratch=(), limit=16, after=(), flops=0):
    used, skip = len(ins), len(after)

    def kernel(*refs):
        body(*refs[:used], *refs[used + skip :])

    ins = list(ins) + list(after)
    return pl.pallas_call(
        kernel,
        out_shape=[jax.ShapeDtypeStruct(shape, dtype) for shape, dtype in outs],
        in_specs=[VMEM] * used + [pl.BlockSpec(memory_space=pl.ANY)] * skip,
        out_specs=[VMEM] * len(outs),
        scratch_shapes=[pltpu.VMEM(shape, dtype) for shape, dtype in scratch],
        compiler_params=pltpu.CompilerParams(vmem_limit_bytes=limit * 1024 * 1024),
        cost_estimate=pl.CostEstimate(flops=flops, bytes_accessed=0, transcendentals=0),
    )(*ins)


def split(value):
    high = value.astype(BF16)
    return high, (value - high.astype(F32)).astype(BF16)


def dot(a, b):
    return jnp.dot(a, b, preferred_element_type=F32)


def sigmoid(value):
    return 0.5 * jnp.tanh(0.5 * value) + 0.5


def silu(value):
    return value * sigmoid(value)


def slope(value):
    sigma = sigmoid(value)
    return sigma * (1.0 + value * (1.0 - sigma))


def relative_blocks():
    lat, y = lax.axis_index("lat"), lax.axis_index("rep")
    x, core = lat // 2, lat % 2
    order = []
    for r_core in range(2):
        c = core + r_core - 2 * core * r_core
        y_first = c == 0
        for r_first in range(2):
            for r_second in range(2):
                move_y = jnp.where(y_first, r_first, r_second)
                move_x = jnp.where(y_first, r_second, r_first)
                there_y = y + move_y - 2 * y * move_y
                there_x = x + move_x - 2 * x * move_x
                order.append(there_x * 4 + c * 2 + there_y)
    return order


def pack_rows(low_here, high_here, low_grad, high_grad, one, two):
    even = lax.axis_index("lat") % 2 == 0
    for f, (low, high) in enumerate(((low_here, high_here), (low_grad, high_grad))):
        one[f] = jnp.where(even, high[...], low[...])
        two[f] = jnp.where(even, low[...], high[...])


def pack_cols(here, grad, one, two, first, second):
    rows, cols = here.shape[:2]
    even_lat = lax.axis_index("lat") % 2 == 0
    even = lax.axis_index("lon") % 2 == 0
    for f, field in enumerate((here, grad)):
        low = jnp.where(even_lat, two[f], one[f])
        high = jnp.where(even_lat, one[f], two[f])
        for c in range(2):
            edges = []
            for col in (c, cols - 2 + c):
                edges.append(
                    jnp.concatenate(
                        [
                            low[:, col],
                            field[:, col],
                            high[:, col],
                            jnp.zeros((LINE - rows - 4, field.shape[2]), F32),
                        ],
                        axis=0,
                    )
                )
            first[f, c] = jnp.where(even, edges[1], edges[0])
            second[f, c] = jnp.where(even, edges[0], edges[1])


def pair_swap(one, two, axis, periodic):
    count = lax.axis_size(axis)
    pairs = [(i, i + 1) for i in range(0, count - 1, 2)]
    mates = [(i, i + 1) for i in range(1, count - 1, 2)]
    if periodic:
        mates.append((count - 1, 0))
    return tuple(
        lax.ppermute(block, axis, who + [(b, a) for a, b in who])
        for block, who in ((one, pairs), (two, mates))
    )


def prepare(weights, high, low):
    high[...], low[...] = split(weights[...])


def prepare_back(weights, high, low):
    size = weights.shape[1]
    for tap in range(9):
        there = 8 - tap
        block = weights[there * size : (there + 1) * size, :].T
        high[tap * size : (tap + 1) * size, :], low[tap * size : (tap + 1) * size, :] = split(block)


def turn(value, high, low, scratch):
    channels = value.shape[1]
    each = channels // 8
    scratch[...] = value.T
    for i, block in enumerate(relative_blocks()):
        part = scratch[pl.ds(pl.multiple_of(block * each, each), each), :]
        high[i * each : (i + 1) * each, :], low[i * each : (i + 1) * each, :] = split(part)


def turn_grad(here, grad, act, high, low, scratch):
    cells = grad.shape[0] * grad.shape[1]
    act[...] = silu(here[...])
    turn(grad[...].reshape(cells, grad.shape[2]), high, low, scratch)


def lay_taps(wide, x_high, x_low):
    rows, padded, channels = wide.shape
    cols = padded - 2 * EDGE
    for b in range(3):
        part = wide[:, EDGE - 1 + b : EDGE - 1 + b + cols, :].reshape(rows * cols, channels)
        high, low = split(part)
        x_high[:, b * channels : (b + 1) * channels] = high
        x_low[:, b * channels : (b + 1) * channels] = low


def convolve(x_high, x_low, first_row, rows, cols, w_high, w_low):
    channels = w_high.shape[1]
    total = None
    for a in range(3):
        cells = slice((first_row + a) * cols, (first_row + a + rows) * cols)
        taps = slice(a * 3 * channels, (a + 1) * 3 * channels)
        for x, w in ((x_high, w_high), (x_high, w_low), (x_low, w_high)):
            part = dot(x[cells, :], w[taps, :])
            total = part if total is None else total + part
    return total


def side_columns(mine_one, mine_two, got_one, got_two, f):
    even = lax.axis_index("lon") % 2 == 0

    def either(a, b):
        return jnp.where(even, a, b)

    left = [either(got_two[f, c], got_one[f, c]) for c in range(2)]
    left.append(either(mine_two[f, 0], mine_one[f, 0]))
    right = [either(mine_one[f, 1], mine_two[f, 1])]
    right += [either(got_one[f, c], got_two[f, c]) for c in range(2)]
    return left, right


def ring(left, right, w_high, w_low, r_high, r_low):
    channels = w_high.shape[1]
    for s, columns in enumerate((left, right)):
        for a in range(3):
            for b in range(3):
                high, low = split(columns[b])
                value = columns[b]
                if a:
                    value = jnp.concatenate(
                        [value[a:], jnp.zeros((a, value.shape[1]), F32)], axis=0
                    )
                place = (
                    slice(s * LINE, (s + 1) * LINE),
                    slice((a * 3 + b) * channels, (a * 3 + b + 1) * channels),
                )
                r_high[place], r_low[place] = split(value)
    return (
        dot(r_high[...], w_high[...])
        + dot(r_high[...], w_low[...])
        + dot(r_low[...], w_high[...])
    )


def spread(value, function, got_rows, columns, f, wide):
    rows, cols, channels = value.shape
    even_lat = lax.axis_index("lat") % 2 == 0
    one, two = got_rows
    wide[2 : rows + 2, EDGE : EDGE + cols, :] = value[...]
    wide[0:2, EDGE : EDGE + cols, :] = function(jnp.where(even_lat, two[f], one[f]))
    wide[rows + 2 : rows + 4, EDGE : EDGE + cols, :] = function(
        jnp.where(even_lat, one[f], two[f])
    )
    left, right = columns
    wide[:, EDGE - 1 : EDGE, :] = left[1][: rows + 4].reshape(rows + 4, 1, channels)
    wide[:, EDGE + cols : EDGE + cols + 1, :] = right[1][: rows + 4].reshape(rows + 4, 1, channels)


def inside(rows):
    row = lax.axis_index("lat") * rows - 1 + lax.broadcasted_iota(jnp.int32, (rows + 2, 1, 1), 0)
    return (row >= 0) & (row < rows * lax.axis_size("lat"))


def inside_line(rows):
    row = lax.axis_index("lat") * rows - 1 + lax.broadcasted_iota(jnp.int32, (LINE, 1), 0)
    return (row >= 0) & (row < rows * lax.axis_size("lat"))


def spread_ext(main, side, wide):
    tall, cols, channels = main.shape
    wide[:, EDGE : EDGE + cols, :] = main
    wide[:, EDGE - 1 : EDGE, :] = side[:tall].reshape(tall, 1, channels)
    wide[:, EDGE + cols : EDGE + cols + 1, :] = side[LINE : LINE + tall].reshape(tall, 1, channels)


def products(t_high, t_low, x_high, x_low, first_row, cells, cols, scale, *outs):
    width = x_high.shape[1]
    size = t_high.shape[0] // len(outs)
    for a in range(3):
        rows = slice((first_row + a) * cols, (first_row + a) * cols + cells)
        total = (
            dot(t_high[...], x_high[rows, :])
            + dot(t_high[...], x_low[rows, :])
            + dot(t_low[...], x_high[rows, :])
        ) * scale
        for i, out in enumerate(outs):
            out[:, a * width : (a + 1) * width] = total[i * size : (i + 1) * size]


def hidden_kernel(
    act, r1, r2, m1, m2, q1, q2, w_high, w_low,
    hidden, side, x1_high, x1_low, x2_high, x2_low,
    wide, wide2, r_high, r_low,
):
    rows, cols, channels = act.shape
    left, right = side_columns(m1, m2, q1, q2, 0)
    left, right = [silu(v) for v in left], [silu(v) for v in right]
    spread(act, silu, (r1, r2), (left, right), 0, wide)
    lay_taps(wide, x1_high, x1_low)
    main = convolve(x1_high, x1_low, 0, rows + 2, cols, w_high, w_low)
    around = ring(left, right, w_high, w_low, r_high, r_low)
    hidden[...] = main
    side[...] = around
    after = jnp.where(inside(rows), silu(main).reshape(rows + 2, cols, channels), 0.0)
    line = inside_line(rows)
    around = jnp.where(jnp.concatenate([line, line], axis=0), silu(around), 0.0)
    spread_ext(after, around, wide2)
    lay_taps(wide2, x2_high, x2_low)


def inner_kernel(
    grad, r1, r2, m1, m2, q1, q2, w_high, w_low, hidden, side,
    x3_high, x3_low, t_high, t_low,
    wide, xc_high, xc_low, wide2, r_high, r_low, turned,
):
    rows, cols, channels = grad.shape
    columns = side_columns(m1, m2, q1, q2, 1)
    spread(grad, lambda v: v, (r1, r2), columns, 1, wide)
    lay_taps(wide, xc_high, xc_low)
    main = convolve(xc_high, xc_low, 0, rows + 2, cols, w_high, w_low) * slope(hidden[...])
    around = ring(*columns, w_high, w_low, r_high, r_low) * slope(side[...])
    main = jnp.where(inside(rows), main.reshape(rows + 2, cols, channels), 0.0)
    line = inside_line(rows)
    around = jnp.where(jnp.concatenate([line, line], axis=0), around, 0.0)
    turn(main[1 : rows + 1].reshape(rows * cols, channels), t_high, t_low, turned)
    spread_ext(main, around, wide2)
    lay_taps(wide2, x3_high, x3_low)


def products_kernel(scale, cols, first_row, t_high, t_low, x_high, x_low, *outs):
    products(t_high, t_low, x_high, x_low, first_row, t_high.shape[1], cols, scale, *outs)


def output_kernel(here, x_high, x_low, w_high, w_low, out, token):
    token[...] = jnp.zeros(token.shape, F32)
    rows, cols, channels = here.shape
    total = convolve(x_high, x_low, 0, rows, cols, w_high, w_low)
    out[...] = here[...] + total.reshape(rows, cols, channels)


def input_grad_kernel(here, grad, x_high, x_low, w_high, w_low, out, token):
    token[...] = jnp.zeros(token.shape, F32)
    rows, cols, channels = here.shape
    total = convolve(x_high, x_low, 0, rows, cols, w_high, w_low)
    out[...] = grad[...] + total.reshape(rows, cols, channels) * slope(here[...])


def plane_perm(count, even, odd):
    return [(i, i ^ (odd if (i // 2) % 2 else even)) for i in range(count)]


def plane_swap(away, second):
    count = lax.axis_size("lat") * lax.axis_size("rep")
    one, two = (4, 1) if second else (1, 4)
    return lax.ppermute(away, ("lat", "rep"), plane_perm(count, one, two))


def core_swap(away):
    count = lax.axis_size("lat") * lax.axis_size("rep")
    return lax.ppermute(away, ("lat", "rep"), plane_perm(count, 2, 2))


def add_halves(keep, got, next_keep, next_away, *token):
    for ref in token:
        ref[...] = jnp.zeros(ref.shape, F32)
    half = keep.shape[0] // 2
    next_keep[...] = keep[:half] + got[:half]
    next_away[...] = keep[half:] + got[half:]


def cut_blocks(keep, got, *outs):
    *blocks, token = outs
    token[...] = jnp.zeros(token.shape, F32)
    total = keep[...] + got[...]
    count = len(blocks)
    size = total.shape[1] // count
    parts = [total[:, i * size : (i + 1) * size] for i in range(count)]
    z = lax.axis_index("lon")
    for step, block in enumerate(blocks):
        value = parts[step]
        for place in range(1, count):
            value = jnp.where(z == place, parts[place ^ step], value)
        block[...] = value


def wide_sum(keep, got):
    return lax.psum_scatter(keep + got, "lon", scatter_dimension=1, tiled=True).T


def add_blocks(one, two, three, four, out):
    out[...] = (one[...] + two[...] + three[...] + four[...]).T


def send_blocks(keep, got, after=(), flops=0):
    each, taps = keep.shape
    lon = lax.axis_size("lon")
    outs = [((each, taps // lon), F32)] * lon + [((8, 128), F32)]
    *blocks, token = call(cut_blocks, outs, [keep, got], after=after, flops=flops)
    gots = [
        lax.ppermute(blocks[step], "lon", [(i, i ^ step) for i in range(lon)])
        for step in (3, 2, 1)
    ]
    return [blocks[0], *gots], token


def local(inputs, cotangent, first_weight, second_weight):
    here, grad = inputs[0], cotangent[0]
    rows, cols, channels = here.shape
    cells, tall = rows * cols, rows + 2
    width = 3 * channels
    scale = 1.0 / math.sqrt(
        cells * lax.axis_size("rep") * lax.axis_size("lat") * lax.axis_size("lon")
    )
    edge = ((2, 2, cols, channels), F32)
    edges = [here[:2], here[rows - 2 :], grad[:2], grad[rows - 2 :]]
    one, two = call(pack_rows, [edge] * 2, edges)
    r1, r2 = pair_swap(one, two, "lat", False)
    pair = [((9 * channels, channels), BF16)] * 2
    w1_high, w1_low = call(prepare, pair, [first_weight])
    act, t_high, t_low = call(
        turn_grad,
        [((rows, cols, channels), F32)] + [((channels, cells), BF16)] * 2,
        [here, grad],
        scratch=[((channels, cells), F32)],
    )
    line = ((2, 2, LINE, channels), F32)
    m1, m2 = call(pack_cols, [line] * 2, [here, grad, r1, r2], after=[t_low])
    q1, q2 = pair_swap(m1, m2, "lon", True)
    lines = ((2 * LINE, channels), F32)
    wide = ((rows + 4, cols + 2 * EDGE, channels), F32)
    wide2 = ((tall, cols + 2 * EDGE, channels), F32)
    taps_1 = [(((rows + 4) * cols, width), BF16)] * 2
    taps_2 = [((tall * cols, width), BF16)] * 2
    around = [((2 * LINE, 3 * width), BF16)] * 2
    halves = [((channels // 2, 9 * channels), F32)] * 2
    hidden, side, x1_high, x1_low, x2_high, x2_low = call(
        hidden_kernel,
        [((tall * cols, channels), F32), lines] + taps_1 + taps_2,
        [act, r1, r2, m1, m2, q1, q2, w1_high, w1_low],
        scratch=[wide, wide2] + around,
    )
    half = halves[0]
    each = channels // 8

    def halves_of(count):
        return [((count, 9 * channels), F32)] * 2

    def second_products(name, after):
        part = slice(0, channels // 2) if name == "keep" else slice(channels // 2, channels)
        return call(
            lambda high, low, *refs: products_kernel(
                scale, cols, 0, high.at[part], low.at[part], *refs
            ),
            [half],
            [t_high, t_low, x2_high, x2_low],
            after=after,
        )[0]

    away_2 = second_products("away", [])
    got_2 = core_swap(away_2)
    keep_2 = second_products("keep", [away_2])
    b2_high, b2_low = call(prepare_back, pair, [second_weight], after=[away_2])
    w2_high, w2_low = call(prepare, pair, [second_weight], after=[away_2])
    b1_high, b1_low = call(prepare_back, pair, [first_weight], after=[away_2])
    keep_2, away_2 = call(
        add_halves, halves_of(2 * each), [keep_2, got_2], after=[b2_low]
    )
    got_2 = plane_swap(away_2, False)
    x3_high, x3_low, t_high, t_low = call(
        inner_kernel,
        taps_2 + [((channels, cells), BF16)] * 2,
        [grad, r1, r2, m1, m2, q1, q2, b2_high, b2_low, hidden, side],
        scratch=[wide] + taps_1 + [wide2] + around + [((channels, cells), F32)],
        after=[keep_2],
    )
    keep_1, away_1 = call(
        lambda *refs: products_kernel(scale, cols, 1, *refs),
        [half, half],
        [t_high, t_low, x1_high, x1_low],
    )
    got_1 = core_swap(away_1)
    keep_2, away_2 = call(add_halves, halves_of(each), [keep_2, got_2], flops=LONG)
    got_2 = plane_swap(away_2, True)
    keep_1, away_1 = call(add_halves, halves_of(2 * each), [keep_1, got_1], after=[keep_2])
    got_1 = plane_swap(away_1, False)
    outs = [((rows, cols, channels), F32), ((8, 128), F32)]
    output, token = call(
        output_kernel, outs, [here, x2_high, x2_low, w2_high, w2_low], after=[keep_1]
    )
    direct = lax.axis_size("lon") == 4
    if direct:
        blocks, token = send_blocks(keep_2, got_2, [token], LONG)
    else:
        second_grad = wide_sum(keep_2, got_2)
    keep_1, away_1 = call(add_halves, halves_of(each), [keep_1, got_1], after=[token])
    got_1 = plane_swap(away_1, True)
    input_grad, token = call(
        input_grad_kernel,
        outs,
        [here, grad, x3_high, x3_low, b1_high, b1_low],
        after=[keep_1],
    )
    if direct:
        shape = (blocks[0].shape[1], each)
        (second_grad,) = call(add_blocks, [(shape, F32)], blocks, after=[token], flops=LONG)
        blocks, _ = send_blocks(keep_1, got_1, [second_grad])
        first_grad = sum(blocks[1:], blocks[0]).T
    else:
        first_grad = wide_sum(keep_1, got_1)
    return (output[None], input_grad[None], first_grad, second_grad)


def solution(mesh):
    in_specs = (P("rep", "lat", "lon", None), P("rep", "lat", "lon", None), P(), P())
    out_specs = (
        P("rep", "lat", "lon", None),
        P("rep", "lat", "lon", None),
        P("lon", ("lat", "rep")),
        P("lon", ("lat", "rep")),
    )
    return jax.shard_map(local, mesh=mesh, in_specs=in_specs, out_specs=out_specs, check_vma=False)
```

```python
import math

import jax
import jax.numpy as jnp
from jax import lax
from jax.experimental import pallas as pl
from jax.experimental.pallas import tpu as pltpu
from jax.sharding import PartitionSpec as P

F32 = jnp.float32
BF16 = jnp.bfloat16
VMEM = pl.BlockSpec(memory_space=pltpu.VMEM)
LONG = 10**10
LINE = 24
EDGE = 8


def call(body, outs, ins, scratch=(), limit=16, after=(), flops=0):
    used, skip = len(ins), len(after)

    def kernel(*refs):
        body(*refs[:used], *refs[used + skip :])

    ins = list(ins) + list(after)
    return pl.pallas_call(
        kernel,
        out_shape=[jax.ShapeDtypeStruct(shape, dtype) for shape, dtype in outs],
        in_specs=[VMEM] * used + [pl.BlockSpec(memory_space=pl.ANY)] * skip,
        out_specs=[VMEM] * len(outs),
        scratch_shapes=[pltpu.VMEM(shape, dtype) for shape, dtype in scratch],
        compiler_params=pltpu.CompilerParams(vmem_limit_bytes=limit * 1024 * 1024),
        cost_estimate=pl.CostEstimate(flops=flops, bytes_accessed=0, transcendentals=0),
    )(*ins)


def split(value):
    high = value.astype(BF16)
    return high, (value - high.astype(F32)).astype(BF16)


def dot(a, b):
    return jnp.dot(a, b, preferred_element_type=F32)


def sigmoid(value):
    return 0.5 * jnp.tanh(0.5 * value) + 0.5


def silu(value):
    return value * sigmoid(value)


def slope(value):
    sigma = sigmoid(value)
    return sigma * (1.0 + value * (1.0 - sigma))


def relative_blocks(flip):
    lat, y = lax.axis_index("lat"), lax.axis_index("rep")
    x, core = lat // 2, lat % 2
    order = []
    for r_core in range(2):
        c = core + r_core - 2 * core * r_core
        y_first = c == (1 if flip else 0)
        for r_first in range(2):
            for r_second in range(2):
                move_y = jnp.where(y_first, r_first, r_second)
                move_x = jnp.where(y_first, r_second, r_first)
                there_y = y + move_y - 2 * y * move_y
                there_x = x + move_x - 2 * x * move_x
                order.append(there_x * 4 + c * 2 + there_y)
    return order


def pack_rows(low_here, high_here, low_grad, high_grad, one, two):
    even = lax.axis_index("lat") % 2 == 0
    for f, (low, high) in enumerate(((low_here, high_here), (low_grad, high_grad))):
        one[f] = jnp.where(even, high[...], low[...])
        two[f] = jnp.where(even, low[...], high[...])


def pack_cols(here, grad, one, two, first, second):
    rows, cols = here.shape[:2]
    even_lat = lax.axis_index("lat") % 2 == 0
    even = lax.axis_index("lon") % 2 == 0
    for f, field in enumerate((here, grad)):
        low = jnp.where(even_lat, two[f], one[f])
        high = jnp.where(even_lat, one[f], two[f])
        for c in range(2):
            edges = []
            for col in (c, cols - 2 + c):
                edges.append(
                    jnp.concatenate(
                        [
                            low[:, col],
                            field[:, col],
                            high[:, col],
                            jnp.zeros((LINE - rows - 4, field.shape[2]), F32),
                        ],
                        axis=0,
                    )
                )
            first[f, c] = jnp.where(even, edges[1], edges[0])
            second[f, c] = jnp.where(even, edges[0], edges[1])


def pair_swap(one, two, axis, periodic):
    count = lax.axis_size(axis)
    pairs = [(i, i + 1) for i in range(0, count - 1, 2)]
    mates = [(i, i + 1) for i in range(1, count - 1, 2)]
    if periodic:
        mates.append((count - 1, 0))
    return tuple(
        lax.ppermute(block, axis, who + [(b, a) for a, b in who])
        for block, who in ((one, pairs), (two, mates))
    )


def prepare(weights, high, low):
    high[...], low[...] = split(weights[...])


def prepare_back(weights, high, low):
    size = weights.shape[1]
    for tap in range(9):
        there = 8 - tap
        block = weights[there * size : (there + 1) * size, :].T
        high[tap * size : (tap + 1) * size, :], low[tap * size : (tap + 1) * size, :] = split(block)


def turn(flip, value, high, low, scratch):
    channels = value.shape[1]
    each = channels // 8
    scratch[...] = value.T
    for i, block in enumerate(relative_blocks(flip)):
        part = scratch[pl.ds(pl.multiple_of(block * each, each), each), :]
        high[i * each : (i + 1) * each, :], low[i * each : (i + 1) * each, :] = split(part)


def turn_grad(here, grad, act, high, low, scratch):
    cells = grad.shape[0] * grad.shape[1]
    act[...] = silu(here[...])
    turn(False, grad[...].reshape(cells, grad.shape[2]), high, low, scratch)


def lay_taps(wide, x_high, x_low):
    rows, padded, channels = wide.shape
    cols = padded - 2 * EDGE
    for b in range(3):
        part = wide[:, EDGE - 1 + b : EDGE - 1 + b + cols, :].reshape(rows * cols, channels)
        high, low = split(part)
        x_high[:, b * channels : (b + 1) * channels] = high
        x_low[:, b * channels : (b + 1) * channels] = low


def convolve(x_high, x_low, first_row, rows, cols, w_high, w_low):
    channels = w_high.shape[1]
    total = None
    for a in range(3):
        cells = slice((first_row + a) * cols, (first_row + a + rows) * cols)
        taps = slice(a * 3 * channels, (a + 1) * 3 * channels)
        for x, w in ((x_high, w_high), (x_high, w_low), (x_low, w_high)):
            part = dot(x[cells, :], w[taps, :])
            total = part if total is None else total + part
    return total


def side_columns(mine_one, mine_two, got_one, got_two, f):
    even = lax.axis_index("lon") % 2 == 0

    def either(a, b):
        return jnp.where(even, a, b)

    left = [either(got_two[f, c], got_one[f, c]) for c in range(2)]
    left.append(either(mine_two[f, 0], mine_one[f, 0]))
    right = [either(mine_one[f, 1], mine_two[f, 1])]
    right += [either(got_one[f, c], got_two[f, c]) for c in range(2)]
    return left, right


def ring(left, right, w_high, w_low, r_high, r_low):
    channels = w_high.shape[1]
    for s, columns in enumerate((left, right)):
        for a in range(3):
            for b in range(3):
                high, low = split(columns[b])
                value = columns[b]
                if a:
                    value = jnp.concatenate(
                        [value[a:], jnp.zeros((a, value.shape[1]), F32)], axis=0
                    )
                place = (
                    slice(s * LINE, (s + 1) * LINE),
                    slice((a * 3 + b) * channels, (a * 3 + b + 1) * channels),
                )
                r_high[place], r_low[place] = split(value)
    return (
        dot(r_high[...], w_high[...])
        + dot(r_high[...], w_low[...])
        + dot(r_low[...], w_high[...])
    )


def spread(value, function, got_rows, columns, f, wide):
    rows, cols, channels = value.shape
    even_lat = lax.axis_index("lat") % 2 == 0
    one, two = got_rows
    wide[2 : rows + 2, EDGE : EDGE + cols, :] = value[...]
    wide[0:2, EDGE : EDGE + cols, :] = function(jnp.where(even_lat, two[f], one[f]))
    wide[rows + 2 : rows + 4, EDGE : EDGE + cols, :] = function(
        jnp.where(even_lat, one[f], two[f])
    )
    left, right = columns
    wide[:, EDGE - 1 : EDGE, :] = left[1][: rows + 4].reshape(rows + 4, 1, channels)
    wide[:, EDGE + cols : EDGE + cols + 1, :] = right[1][: rows + 4].reshape(rows + 4, 1, channels)


def inside(rows):
    row = lax.axis_index("lat") * rows - 1 + lax.broadcasted_iota(jnp.int32, (rows + 2, 1, 1), 0)
    return (row >= 0) & (row < rows * lax.axis_size("lat"))


def inside_line(rows):
    row = lax.axis_index("lat") * rows - 1 + lax.broadcasted_iota(jnp.int32, (LINE, 1), 0)
    return (row >= 0) & (row < rows * lax.axis_size("lat"))


def spread_ext(main, side, wide):
    tall, cols, channels = main.shape
    wide[:, EDGE : EDGE + cols, :] = main
    wide[:, EDGE - 1 : EDGE, :] = side[:tall].reshape(tall, 1, channels)
    wide[:, EDGE + cols : EDGE + cols + 1, :] = side[LINE : LINE + tall].reshape(tall, 1, channels)


def products(t_high, t_low, x_high, x_low, first_row, cells, cols, scale, *outs):
    width = x_high.shape[1]
    size = t_high.shape[0] // len(outs)
    for a in range(3):
        rows = slice((first_row + a) * cols, (first_row + a) * cols + cells)
        total = (
            dot(t_high[...], x_high[rows, :])
            + dot(t_high[...], x_low[rows, :])
            + dot(t_low[...], x_high[rows, :])
        ) * scale
        for i, out in enumerate(outs):
            out[:, a * width : (a + 1) * width] = total[i * size : (i + 1) * size]


def hidden_kernel(
    act, r1, r2, m1, m2, q1, q2, w_high, w_low,
    hidden, side, x1_high, x1_low, x2_high, x2_low,
    wide, wide2, r_high, r_low,
):
    rows, cols, channels = act.shape
    left, right = side_columns(m1, m2, q1, q2, 0)
    left, right = [silu(v) for v in left], [silu(v) for v in right]
    spread(act, silu, (r1, r2), (left, right), 0, wide)
    lay_taps(wide, x1_high, x1_low)
    main = convolve(x1_high, x1_low, 0, rows + 2, cols, w_high, w_low)
    around = ring(left, right, w_high, w_low, r_high, r_low)
    hidden[...] = main
    side[...] = around
    after = jnp.where(inside(rows), silu(main).reshape(rows + 2, cols, channels), 0.0)
    line = inside_line(rows)
    around = jnp.where(jnp.concatenate([line, line], axis=0), silu(around), 0.0)
    spread_ext(after, around, wide2)
    lay_taps(wide2, x2_high, x2_low)


def inner_kernel(
    grad, r1, r2, m1, m2, q1, q2, w_high, w_low, hidden, side,
    x3_high, x3_low, t_high, t_low,
    wide, xc_high, xc_low, wide2, r_high, r_low, turned,
):
    rows, cols, channels = grad.shape
    columns = side_columns(m1, m2, q1, q2, 1)
    spread(grad, lambda v: v, (r1, r2), columns, 1, wide)
    lay_taps(wide, xc_high, xc_low)
    main = convolve(xc_high, xc_low, 0, rows + 2, cols, w_high, w_low) * slope(hidden[...])
    around = ring(*columns, w_high, w_low, r_high, r_low) * slope(side[...])
    main = jnp.where(inside(rows), main.reshape(rows + 2, cols, channels), 0.0)
    line = inside_line(rows)
    around = jnp.where(jnp.concatenate([line, line], axis=0), around, 0.0)
    turn(True, main[1 : rows + 1].reshape(rows * cols, channels), t_high, t_low, turned)
    spread_ext(main, around, wide2)
    lay_taps(wide2, x3_high, x3_low)


def products_kernel(scale, cols, first_row, t_high, t_low, x_high, x_low, *outs):
    products(t_high, t_low, x_high, x_low, first_row, t_high.shape[1], cols, scale, *outs)


def output_kernel(here, x_high, x_low, w_high, w_low, out, token):
    token[...] = jnp.zeros(token.shape, F32)
    rows, cols, channels = here.shape
    total = convolve(x_high, x_low, 0, rows, cols, w_high, w_low)
    out[...] = here[...] + total.reshape(rows, cols, channels)


def input_grad_kernel(here, grad, x_high, x_low, w_high, w_low, out, token):
    token[...] = jnp.zeros(token.shape, F32)
    rows, cols, channels = here.shape
    total = convolve(x_high, x_low, 0, rows, cols, w_high, w_low)
    out[...] = grad[...] + total.reshape(rows, cols, channels) * slope(here[...])


def plane_perm(count, even, odd):
    return [(i, i ^ (odd if (i // 2) % 2 else even)) for i in range(count)]


def plane_swap(away, across):
    count = lax.axis_size("lat") * lax.axis_size("rep")
    one, two = (4, 1) if across else (1, 4)
    return lax.ppermute(away, ("lat", "rep"), plane_perm(count, one, two))


def core_swap(away):
    count = lax.axis_size("lat") * lax.axis_size("rep")
    return lax.ppermute(away, ("lat", "rep"), plane_perm(count, 2, 2))


def add_halves(keep, got, next_keep, next_away, *token):
    for ref in token:
        ref[...] = jnp.zeros(ref.shape, F32)
    half = keep.shape[0] // 2
    next_keep[...] = keep[:half] + got[:half]
    next_away[...] = keep[half:] + got[half:]


def cut_blocks(keep, got, *outs):
    blocks = outs[:4]
    for token in outs[4:]:
        token[...] = jnp.zeros(token.shape, F32)
    total = keep[...] + got[...]
    count = len(blocks)
    size = total.shape[1] // count
    parts = [total[:, i * size : (i + 1) * size] for i in range(count)]
    z = lax.axis_index("lon")
    for step, block in enumerate(blocks):
        value = parts[step]
        for place in range(1, count):
            value = jnp.where(z == place, parts[place ^ step], value)
        block[...] = value


def wide_sum(keep, got):
    return lax.psum_scatter(keep + got, "lon", scatter_dimension=1, tiled=True).T


def add_blocks(one, two, three, four, out, token):
    token[...] = jnp.zeros(token.shape, F32)
    out[...] = one[...] + two[...] + three[...] + four[...]


def send_blocks(keep, got, after=(), flops=0, tokens=()):
    each, taps = keep.shape
    lon = lax.axis_size("lon")
    outs = [((each, taps // lon), F32)] * lon + list(tokens)
    blocks = call(cut_blocks, outs, [keep, got], after=after, flops=flops)
    gots = [
        lax.ppermute(blocks[step], "lon", [(i, i ^ step) for i in range(lon)])
        for step in (3, 2, 1)
    ]
    return [blocks[0], *gots], blocks[lon:]


def local(inputs, cotangent, first_weight, second_weight):
    here, grad = inputs[0], cotangent[0]
    rows, cols, channels = here.shape
    cells, tall = rows * cols, rows + 2
    width = 3 * channels
    scale = 1.0 / math.sqrt(
        cells * lax.axis_size("rep") * lax.axis_size("lat") * lax.axis_size("lon")
    )
    edge = ((2, 2, cols, channels), F32)
    edges = [here[:2], here[rows - 2 :], grad[:2], grad[rows - 2 :]]
    one, two = call(pack_rows, [edge] * 2, edges)
    r1, r2 = pair_swap(one, two, "lat", False)
    pair = [((9 * channels, channels), BF16)] * 2
    w1_high, w1_low = call(prepare, pair, [first_weight])
    act, t_high, t_low = call(
        turn_grad,
        [((rows, cols, channels), F32)] + [((channels, cells), BF16)] * 2,
        [here, grad],
        scratch=[((channels, cells), F32)],
    )
    line = ((2, 2, LINE, channels), F32)
    m1, m2 = call(pack_cols, [line] * 2, [here, grad, r1, r2], after=[t_low])
    q1, q2 = pair_swap(m1, m2, "lon", True)
    lines = ((2 * LINE, channels), F32)
    wide = ((rows + 4, cols + 2 * EDGE, channels), F32)
    wide2 = ((tall, cols + 2 * EDGE, channels), F32)
    taps_1 = [(((rows + 4) * cols, width), BF16)] * 2
    taps_2 = [((tall * cols, width), BF16)] * 2
    around = [((2 * LINE, 3 * width), BF16)] * 2
    halves = [((channels // 2, 9 * channels), F32)] * 2
    hidden, side, x1_high, x1_low, x2_high, x2_low = call(
        hidden_kernel,
        [((tall * cols, channels), F32), lines] + taps_1 + taps_2,
        [act, r1, r2, m1, m2, q1, q2, w1_high, w1_low],
        scratch=[wide, wide2] + around,
    )
    half = halves[0]
    each = channels // 8

    def halves_of(count):
        return [((count, 9 * channels), F32)] * 2

    def second_products(name, after):
        part = slice(0, channels // 2) if name == "keep" else slice(channels // 2, channels)
        return call(
            lambda high, low, *refs: products_kernel(
                scale, cols, 0, high.at[part], low.at[part], *refs
            ),
            [half],
            [t_high, t_low, x2_high, x2_low],
            after=after,
        )[0]

    away_2 = second_products("away", [])
    got_2 = core_swap(away_2)
    keep_2 = second_products("keep", [away_2])
    b2_high, b2_low = call(prepare_back, pair, [second_weight], after=[away_2])
    w2_high, w2_low = call(prepare, pair, [second_weight], after=[away_2])
    b1_high, b1_low = call(prepare_back, pair, [first_weight], after=[away_2])
    keep_2, away_2 = call(
        add_halves, halves_of(2 * each), [keep_2, got_2], after=[b2_low]
    )
    got_2 = plane_swap(away_2, False)
    x3_high, x3_low, t_high, t_low = call(
        inner_kernel,
        taps_2 + [((channels, cells), BF16)] * 2,
        [grad, r1, r2, m1, m2, q1, q2, b2_high, b2_low, hidden, side],
        scratch=[wide] + taps_1 + [wide2] + around + [((channels, cells), F32)],
        after=[keep_2],
    )
    keep_1, away_1 = call(
        lambda *refs: products_kernel(scale, cols, 1, *refs),
        [half, half],
        [t_high, t_low, x1_high, x1_low],
    )
    got_1 = core_swap(away_1)
    keep_2, away_2 = call(add_halves, halves_of(each), [keep_2, got_2], flops=LONG)
    got_2 = plane_swap(away_2, True)
    keep_1, away_1 = call(add_halves, halves_of(2 * each), [keep_1, got_1], after=[keep_2])
    got_1 = plane_swap(away_1, True)
    outs = [((rows, cols, channels), F32), ((8, 128), F32)]
    output, token = call(
        output_kernel, outs, [here, x2_high, x2_low, w2_high, w2_low], after=[keep_1]
    )
    direct = lax.axis_size("lon") == 4
    if direct:
        blocks, (token,) = send_blocks(keep_2, got_2, [token], LONG, outs[1:])
    else:
        second_grad = wide_sum(keep_2, got_2)
    keep_1, away_1 = call(add_halves, halves_of(each), [keep_1, got_1], after=[token])
    got_1 = plane_swap(away_1, False)
    input_grad, token = call(
        input_grad_kernel,
        outs,
        [here, grad, x3_high, x3_low, b1_high, b1_low],
        after=[keep_1],
    )
    if direct:
        shape = (each, blocks[0].shape[1])
        summed, token = call(
            add_blocks, [(shape, F32), outs[1]], blocks, after=[token], flops=LONG
        )
        second_grad = summed.T
        blocks, _ = send_blocks(keep_1, got_1, [token])
        first_grad = sum(blocks[1:], blocks[0]).T
    else:
        first_grad = wide_sum(keep_1, got_1)
    return (output[None], input_grad[None], first_grad, second_grad)


def solution(mesh):
    in_specs = (P("rep", "lat", "lon", None), P("rep", "lat", "lon", None), P(), P())
    out_specs = (
        P("rep", "lat", "lon", None),
        P("rep", "lat", "lon", None),
        P("lon", ("lat", "rep")),
        P("lon", ("lat", "rep")),
    )
    return jax.shard_map(local, mesh=mesh, in_specs=in_specs, out_specs=out_specs, check_vma=False)
```

```python
import math

import jax
import jax.numpy as jnp
from jax import lax
from jax.experimental import pallas as pl
from jax.experimental.pallas import tpu as pltpu
from jax.sharding import PartitionSpec as P

F32 = jnp.float32
BF16 = jnp.bfloat16
VMEM = pl.BlockSpec(memory_space=pltpu.VMEM)
LONG = 10**10
LINE = 24
EDGE = 8


def call(body, outs, ins, scratch=(), limit=16, after=(), flops=0):
    used, skip = len(ins), len(after)

    def kernel(*refs):
        body(*refs[:used], *refs[used + skip :])

    ins = list(ins) + list(after)
    return pl.pallas_call(
        kernel,
        out_shape=[jax.ShapeDtypeStruct(shape, dtype) for shape, dtype in outs],
        in_specs=[VMEM] * used + [pl.BlockSpec(memory_space=pl.ANY)] * skip,
        out_specs=[VMEM] * len(outs),
        scratch_shapes=[pltpu.VMEM(shape, dtype) for shape, dtype in scratch],
        compiler_params=pltpu.CompilerParams(vmem_limit_bytes=limit * 1024 * 1024),
        cost_estimate=pl.CostEstimate(flops=flops, bytes_accessed=0, transcendentals=0),
    )(*ins)


def split(value):
    high = value.astype(BF16)
    return high, (value - high.astype(F32)).astype(BF16)


def dot(a, b):
    return jnp.dot(a, b, preferred_element_type=F32)


def sigmoid(value):
    return 0.5 * jnp.tanh(0.5 * value) + 0.5


def silu(value):
    return value * sigmoid(value)


def slope(value):
    sigma = sigmoid(value)
    return sigma * (1.0 + value * (1.0 - sigma))


def relative_blocks(flip):
    lat, y = lax.axis_index("lat"), lax.axis_index("rep")
    x, core = lat // 2, lat % 2
    order = []
    for r_core in range(2):
        c = core + r_core - 2 * core * r_core
        y_first = c == (1 if flip else 0)
        for r_first in range(2):
            for r_second in range(2):
                move_y = jnp.where(y_first, r_first, r_second)
                move_x = jnp.where(y_first, r_second, r_first)
                there_y = y + move_y - 2 * y * move_y
                there_x = x + move_x - 2 * x * move_x
                order.append(there_x * 4 + c * 2 + there_y)
    return order


def pack_rows(low_here, high_here, low_grad, high_grad, one, two):
    even = lax.axis_index("lat") % 2 == 0
    for f, (low, high) in enumerate(((low_here, high_here), (low_grad, high_grad))):
        one[f] = jnp.where(even, high[...], low[...])
        two[f] = jnp.where(even, low[...], high[...])


def pack_cols(here, grad, one, two, first, second):
    rows, cols = here.shape[:2]
    tall = rows + 4
    even_lat = lax.axis_index("lat") % 2 == 0
    even = lax.axis_index("lon") % 2 == 0
    for f, field in enumerate((here, grad)):
        low = jnp.where(even_lat, two[f], one[f])
        high = jnp.where(even_lat, one[f], two[f])
        for c in range(2):
            edges = [
                jnp.concatenate([low[:, col], field[:, col], high[:, col]], axis=0)
                for col in (c, cols - 2 + c)
            ]
            place = slice((2 * f + c) * tall, (2 * f + c + 1) * tall)
            first[place] = jnp.where(even, edges[1], edges[0])
            second[place] = jnp.where(even, edges[0], edges[1])


def pair_swap(one, two, axis, periodic):
    count = lax.axis_size(axis)
    pairs = [(i, i + 1) for i in range(0, count - 1, 2)]
    mates = [(i, i + 1) for i in range(1, count - 1, 2)]
    if periodic:
        mates.append((count - 1, 0))
    return tuple(
        lax.ppermute(block, axis, who + [(b, a) for a, b in who])
        for block, who in ((one, pairs), (two, mates))
    )


def prepare(weights, high, low):
    high[...], low[...] = split(weights[...])


def prepare_back(weights, high, low):
    size = weights.shape[1]
    for tap in range(9):
        there = 8 - tap
        block = weights[there * size : (there + 1) * size, :].T
        high[tap * size : (tap + 1) * size, :], low[tap * size : (tap + 1) * size, :] = split(block)


def turn(flip, value, high, low, scratch):
    channels = value.shape[1]
    each = channels // 8
    scratch[...] = value.T
    for i, block in enumerate(relative_blocks(flip)):
        part = scratch[pl.ds(pl.multiple_of(block * each, each), each), :]
        high[i * each : (i + 1) * each, :], low[i * each : (i + 1) * each, :] = split(part)


def turn_grad(here, grad, act, high, low, scratch):
    cells = grad.shape[0] * grad.shape[1]
    act[...] = silu(here[...])
    turn(False, grad[...].reshape(cells, grad.shape[2]), high, low, scratch)


def lay_taps(wide, x_high, x_low):
    rows, padded, channels = wide.shape
    cols = padded - 2 * EDGE
    for b in range(3):
        part = wide[:, EDGE - 1 + b : EDGE - 1 + b + cols, :].reshape(rows * cols, channels)
        high, low = split(part)
        x_high[:, b * channels : (b + 1) * channels] = high
        x_low[:, b * channels : (b + 1) * channels] = low


def convolve(x_high, x_low, first_row, rows, cols, w_high, w_low):
    channels = w_high.shape[1]
    total = None
    for a in range(3):
        cells = slice((first_row + a) * cols, (first_row + a + rows) * cols)
        taps = slice(a * 3 * channels, (a + 1) * 3 * channels)
        for x, w in ((x_high, w_high), (x_high, w_low), (x_low, w_high)):
            part = dot(x[cells, :], w[taps, :])
            total = part if total is None else total + part
    return total


def side_columns(mine_one, mine_two, got_one, got_two, f):
    even = lax.axis_index("lon") % 2 == 0
    tall = mine_one.shape[0] // 4
    rest = jnp.zeros((LINE - tall, mine_one.shape[1]), F32)

    def either(a, b, c):
        place = slice((2 * f + c) * tall, (2 * f + c + 1) * tall)
        return jnp.concatenate([jnp.where(even, a[place], b[place]), rest], axis=0)

    left = [either(got_two, got_one, c) for c in range(2)] + [either(mine_two, mine_one, 0)]
    right = [either(mine_one, mine_two, 1)] + [either(got_one, got_two, c) for c in range(2)]
    return left, right


def ring(left, right, w_high, w_low, r_high, r_low):
    channels = w_high.shape[1]
    for s, columns in enumerate((left, right)):
        for a in range(3):
            for b in range(3):
                high, low = split(columns[b])
                value = columns[b]
                if a:
                    value = jnp.concatenate(
                        [value[a:], jnp.zeros((a, value.shape[1]), F32)], axis=0
                    )
                place = (
                    slice(s * LINE, (s + 1) * LINE),
                    slice((a * 3 + b) * channels, (a * 3 + b + 1) * channels),
                )
                r_high[place], r_low[place] = split(value)
    return (
        dot(r_high[...], w_high[...])
        + dot(r_high[...], w_low[...])
        + dot(r_low[...], w_high[...])
    )


def spread(value, function, got_rows, columns, f, wide):
    rows, cols, channels = value.shape
    even_lat = lax.axis_index("lat") % 2 == 0
    one, two = got_rows
    wide[2 : rows + 2, EDGE : EDGE + cols, :] = value[...]
    wide[0:2, EDGE : EDGE + cols, :] = function(jnp.where(even_lat, two[f], one[f]))
    wide[rows + 2 : rows + 4, EDGE : EDGE + cols, :] = function(
        jnp.where(even_lat, one[f], two[f])
    )
    left, right = columns
    wide[:, EDGE - 1 : EDGE, :] = left[1][: rows + 4].reshape(rows + 4, 1, channels)
    wide[:, EDGE + cols : EDGE + cols + 1, :] = right[1][: rows + 4].reshape(rows + 4, 1, channels)


def inside(rows):
    row = lax.axis_index("lat") * rows - 1 + lax.broadcasted_iota(jnp.int32, (rows + 2, 1, 1), 0)
    return (row >= 0) & (row < rows * lax.axis_size("lat"))


def inside_line(rows):
    row = lax.axis_index("lat") * rows - 1 + lax.broadcasted_iota(jnp.int32, (LINE, 1), 0)
    return (row >= 0) & (row < rows * lax.axis_size("lat"))


def spread_ext(main, side, wide):
    tall, cols, channels = main.shape
    wide[:, EDGE : EDGE + cols, :] = main
    wide[:, EDGE - 1 : EDGE, :] = side[:tall].reshape(tall, 1, channels)
    wide[:, EDGE + cols : EDGE + cols + 1, :] = side[LINE : LINE + tall].reshape(tall, 1, channels)


def products(t_high, t_low, x_high, x_low, first_row, cells, cols, scale, *outs):
    width = x_high.shape[1]
    size = t_high.shape[0] // len(outs)
    for a in range(3):
        rows = slice((first_row + a) * cols, (first_row + a) * cols + cells)
        total = (
            dot(t_high[...], x_high[rows, :])
            + dot(t_high[...], x_low[rows, :])
            + dot(t_low[...], x_high[rows, :])
        ) * scale
        for i, out in enumerate(outs):
            out[:, a * width : (a + 1) * width] = total[i * size : (i + 1) * size]


def hidden_kernel(
    act, r1, r2, m1, m2, q1, q2, w_high, w_low,
    hidden, side, x1_high, x1_low, x2_high, x2_low,
    wide, wide2, r_high, r_low,
):
    rows, cols, channels = act.shape
    left, right = side_columns(m1, m2, q1, q2, 0)
    left, right = [silu(v) for v in left], [silu(v) for v in right]
    spread(act, silu, (r1, r2), (left, right), 0, wide)
    lay_taps(wide, x1_high, x1_low)
    main = convolve(x1_high, x1_low, 0, rows + 2, cols, w_high, w_low)
    around = ring(left, right, w_high, w_low, r_high, r_low)
    hidden[...] = main
    side[...] = around
    after = jnp.where(inside(rows), silu(main).reshape(rows + 2, cols, channels), 0.0)
    line = inside_line(rows)
    around = jnp.where(jnp.concatenate([line, line], axis=0), silu(around), 0.0)
    spread_ext(after, around, wide2)
    lay_taps(wide2, x2_high, x2_low)


def inner_kernel(
    grad, r1, r2, m1, m2, q1, q2, w_high, w_low, hidden, side,
    x3_high, x3_low, t_high, t_low,
    wide, xc_high, xc_low, wide2, r_high, r_low, turned,
):
    rows, cols, channels = grad.shape
    columns = side_columns(m1, m2, q1, q2, 1)
    spread(grad, lambda v: v, (r1, r2), columns, 1, wide)
    lay_taps(wide, xc_high, xc_low)
    main = convolve(xc_high, xc_low, 0, rows + 2, cols, w_high, w_low) * slope(hidden[...])
    around = ring(*columns, w_high, w_low, r_high, r_low) * slope(side[...])
    main = jnp.where(inside(rows), main.reshape(rows + 2, cols, channels), 0.0)
    line = inside_line(rows)
    around = jnp.where(jnp.concatenate([line, line], axis=0), around, 0.0)
    turn(True, main[1 : rows + 1].reshape(rows * cols, channels), t_high, t_low, turned)
    spread_ext(main, around, wide2)
    lay_taps(wide2, x3_high, x3_low)


def products_kernel(scale, cols, first_row, t_high, t_low, x_high, x_low, *outs):
    products(t_high, t_low, x_high, x_low, first_row, t_high.shape[1], cols, scale, *outs)


def output_kernel(here, x_high, x_low, w_high, w_low, out, token):
    token[...] = jnp.zeros(token.shape, F32)
    rows, cols, channels = here.shape
    total = convolve(x_high, x_low, 0, rows, cols, w_high, w_low)
    out[...] = here[...] + total.reshape(rows, cols, channels)


def input_grad_kernel(here, grad, x_high, x_low, w_high, w_low, out, token):
    token[...] = jnp.zeros(token.shape, F32)
    rows, cols, channels = here.shape
    total = convolve(x_high, x_low, 0, rows, cols, w_high, w_low)
    out[...] = grad[...] + total.reshape(rows, cols, channels) * slope(here[...])


def plane_perm(count, even, odd):
    return [(i, i ^ (odd if (i // 2) % 2 else even)) for i in range(count)]


def plane_swap(away, across):
    count = lax.axis_size("lat") * lax.axis_size("rep")
    one, two = (4, 1) if across else (1, 4)
    return lax.ppermute(away, ("lat", "rep"), plane_perm(count, one, two))


def core_swap(away):
    count = lax.axis_size("lat") * lax.axis_size("rep")
    return lax.ppermute(away, ("lat", "rep"), plane_perm(count, 2, 2))


def add_halves(keep, got, next_keep, next_away, *token):
    for ref in token:
        ref[...] = jnp.zeros(ref.shape, F32)
    half = keep.shape[0] // 2
    next_keep[...] = keep[:half] + got[:half]
    next_away[...] = keep[half:] + got[half:]


def add_up(keep, got, away):
    away[...] = keep[...] + got[...]


def add_three(keep_one, keep_two, core_one, core_two, got, next_keep, next_away):
    half = keep_one.shape[0]
    next_keep[...] = keep_one[...] + core_one[...] + got[:half]
    next_away[...] = keep_two[...] + core_two[...] + got[half:]


def cut_blocks(keep, got, *outs):
    blocks = outs[:4]
    for token in outs[4:]:
        token[...] = jnp.zeros(token.shape, F32)
    total = keep[...] + got[...]
    count = len(blocks)
    size = total.shape[1] // count
    parts = [total[:, i * size : (i + 1) * size] for i in range(count)]
    z = lax.axis_index("lon")
    for step, block in enumerate(blocks):
        value = parts[step]
        for place in range(1, count):
            value = jnp.where(z == place, parts[place ^ step], value)
        block[...] = value


def wide_sum(keep, got):
    return lax.psum_scatter(keep + got, "lon", scatter_dimension=1, tiled=True).T


def add_blocks(one, two, three, four, out, token):
    token[...] = jnp.zeros(token.shape, F32)
    out[...] = one[...] + two[...] + three[...] + four[...]


def send_blocks(keep, got, after=(), flops=0, tokens=()):
    each, taps = keep.shape
    lon = lax.axis_size("lon")
    outs = [((each, taps // lon), F32)] * lon + list(tokens)
    blocks = call(cut_blocks, outs, [keep, got], after=after, flops=flops)
    gots = [
        lax.ppermute(blocks[step], "lon", [(i, i ^ step) for i in range(lon)])
        for step in (3, 2, 1)
    ]
    return [blocks[0], *gots], blocks[lon:]


def local(inputs, cotangent, first_weight, second_weight):
    here, grad = inputs[0], cotangent[0]
    rows, cols, channels = here.shape
    cells, tall = rows * cols, rows + 2
    width = 3 * channels
    scale = 1.0 / math.sqrt(
        cells * lax.axis_size("rep") * lax.axis_size("lat") * lax.axis_size("lon")
    )
    edge = ((2, 2, cols, channels), F32)
    edges = [here[:2], here[rows - 2 :], grad[:2], grad[rows - 2 :]]
    one, two = call(pack_rows, [edge] * 2, edges)
    r1, r2 = pair_swap(one, two, "lat", False)
    pair = [((9 * channels, channels), BF16)] * 2
    w1_high, w1_low = call(prepare, pair, [first_weight])
    act, t_high, t_low = call(
        turn_grad,
        [((rows, cols, channels), F32)] + [((channels, cells), BF16)] * 2,
        [here, grad],
        scratch=[((channels, cells), F32)],
    )
    line = ((4 * (rows + 4), channels), F32)
    m1, m2 = call(pack_cols, [line] * 2, [here, grad, r1, r2], after=[t_low])
    q1, q2 = pair_swap(m1, m2, "lon", True)
    lines = ((2 * LINE, channels), F32)
    wide = ((rows + 4, cols + 2 * EDGE, channels), F32)
    wide2 = ((tall, cols + 2 * EDGE, channels), F32)
    taps_1 = [(((rows + 4) * cols, width), BF16)] * 2
    taps_2 = [((tall * cols, width), BF16)] * 2
    around = [((2 * LINE, 3 * width), BF16)] * 2
    halves = [((channels // 2, 9 * channels), F32)] * 2
    hidden, side, x1_high, x1_low, x2_high, x2_low = call(
        hidden_kernel,
        [((tall * cols, channels), F32), lines] + taps_1 + taps_2,
        [act, r1, r2, m1, m2, q1, q2, w1_high, w1_low],
        scratch=[wide, wide2] + around,
    )
    half = halves[0]
    each = channels // 8

    def halves_of(count):
        return [((count, 9 * channels), F32)] * 2

    quarter = ((2 * each, 9 * channels), F32)
    eighth = ((each, 9 * channels), F32)

    def second_products(first, outs, after):
        def rows_of(ref):
            starts = [first * 2 * each, (first + 2) * 2 * each]
            return jnp.concatenate([ref[i : i + 2 * each] for i in starts], axis=0)

        return call(
            lambda high, low, *refs: products_kernel(
                scale, cols, 0, rows_of(high), rows_of(low), *refs
            ),
            outs,
            [t_high, t_low, x2_high, x2_low],
            after=after,
        )

    keep_2, away_2 = second_products(1, [quarter] * 2, [])
    got_2 = core_swap(away_2)
    b2_high, b2_low = call(prepare_back, pair, [second_weight], after=[away_2])
    w2_high, w2_low = call(prepare, pair, [second_weight], after=[away_2])
    b1_high, b1_low = call(prepare_back, pair, [first_weight], after=[away_2])
    (away_2,) = call(add_up, [quarter], [keep_2, got_2], after=[b2_low])
    got_2 = plane_swap(away_2, False)
    *keeps, away_one, away_two = second_products(0, [eighth] * 4, [away_2])
    cores = [core_swap(away_one), core_swap(away_two)]
    x3_high, x3_low, t_high, t_low = call(
        inner_kernel,
        taps_2 + [((channels, cells), BF16)] * 2,
        [grad, r1, r2, m1, m2, q1, q2, b2_high, b2_low, hidden, side],
        scratch=[wide] + taps_1 + [wide2] + around + [((channels, cells), F32)],
        after=keeps[:1],
    )
    keep_1, away_1 = call(
        lambda *refs: products_kernel(scale, cols, 1, *refs),
        [half, half],
        [t_high, t_low, x1_high, x1_low],
    )
    got_1 = core_swap(away_1)
    keep_2, away_2 = call(
        add_three, halves_of(each), [*keeps, *cores, got_2], flops=LONG
    )
    got_2 = plane_swap(away_2, True)
    keep_1, away_1 = call(add_halves, halves_of(2 * each), [keep_1, got_1], after=[keep_2])
    got_1 = plane_swap(away_1, True)
    outs = [((rows, cols, channels), F32), ((8, 128), F32)]
    output, token = call(
        output_kernel, outs, [here, x2_high, x2_low, w2_high, w2_low], after=[keep_1]
    )
    direct = lax.axis_size("lon") == 4
    if direct:
        blocks, (token,) = send_blocks(keep_2, got_2, [token], LONG, outs[1:])
    else:
        second_grad = wide_sum(keep_2, got_2)
    keep_1, away_1 = call(add_halves, halves_of(each), [keep_1, got_1], after=[token])
    got_1 = plane_swap(away_1, False)
    input_grad, token = call(
        input_grad_kernel,
        outs,
        [here, grad, x3_high, x3_low, b1_high, b1_low],
        after=[keep_1],
    )
    if direct:
        shape = (each, blocks[0].shape[1])
        summed, token = call(
            add_blocks, [(shape, F32), outs[1]], blocks, after=[token], flops=LONG
        )
        second_grad = summed.T
        blocks, _ = send_blocks(keep_1, got_1, [token])
        first_grad = sum(blocks[1:], blocks[0]).T
    else:
        first_grad = wide_sum(keep_1, got_1)
    return (output[None], input_grad[None], first_grad, second_grad)


def solution(mesh):
    in_specs = (P("rep", "lat", "lon", None), P("rep", "lat", "lon", None), P(), P())
    out_specs = (
        P("rep", "lat", "lon", None),
        P("rep", "lat", "lon", None),
        P("lon", ("lat", "rep")),
        P("lon", ("lat", "rep")),
    )
    return jax.shard_map(local, mesh=mesh, in_specs=in_specs, out_specs=out_specs, check_vma=False)
```

```python
import math

import jax
import jax.numpy as jnp
from jax import lax
from jax.experimental import pallas as pl
from jax.experimental.pallas import tpu as pltpu
from jax.sharding import PartitionSpec as P

F32 = jnp.float32
BF16 = jnp.bfloat16
VMEM = pl.BlockSpec(memory_space=pltpu.VMEM)
LONG = 10**10
LANES = 128
LINE = 24
EDGE = 8


def call(body, outs, ins, scratch=(), limit=16, after=(), flops=0):
    used, skip = len(ins), len(after)

    def kernel(*refs):
        body(*refs[:used], *refs[used + skip :])

    ins = list(ins) + list(after)
    return pl.pallas_call(
        kernel,
        out_shape=[jax.ShapeDtypeStruct(shape, dtype) for shape, dtype in outs],
        in_specs=[VMEM] * used + [pl.BlockSpec(memory_space=pl.ANY)] * skip,
        out_specs=[VMEM] * len(outs),
        scratch_shapes=[pltpu.VMEM(shape, dtype) for shape, dtype in scratch],
        compiler_params=pltpu.CompilerParams(vmem_limit_bytes=limit * 1024 * 1024),
        cost_estimate=pl.CostEstimate(flops=flops, bytes_accessed=0, transcendentals=0),
    )(*ins)


def split(value):
    high = value.astype(BF16)
    return high, (value - high.astype(F32)).astype(BF16)


def dot(a, b):
    return jnp.dot(a, b, preferred_element_type=F32)


def sigmoid(value):
    return 0.5 * jnp.tanh(0.5 * value) + 0.5


def silu(value):
    return value * sigmoid(value)


def slope(value):
    sigma = sigmoid(value)
    return sigma * (1.0 + value * (1.0 - sigma))


def relative_blocks(flip):
    lat, y = lax.axis_index("lat"), lax.axis_index("rep")
    x, core = lat // 2, lat % 2
    order = []
    for r_core in range(2):
        c = core + r_core - 2 * core * r_core
        y_first = c == (1 if flip else 0)
        for r_first in range(2):
            for r_second in range(2):
                move_y = jnp.where(y_first, r_first, r_second)
                move_x = jnp.where(y_first, r_second, r_first)
                there_y = y + move_y - 2 * y * move_y
                there_x = x + move_x - 2 * x * move_x
                order.append(there_x * 4 + c * 2 + there_y)
    return order


def pack_rows(low_here, high_here, low_grad, high_grad, one, two):
    even = lax.axis_index("lat") % 2 == 0
    for f, (low, high) in enumerate(((low_here, high_here), (low_grad, high_grad))):
        one[f] = jnp.where(even, high[...], low[...])
        two[f] = jnp.where(even, low[...], high[...])


def pack_cols(here, grad, one, two, first, second):
    rows, cols = here.shape[:2]
    tall = rows + 4
    even_lat = lax.axis_index("lat") % 2 == 0
    even = lax.axis_index("lon") % 2 == 0
    for f, field in enumerate((here, grad)):
        low = jnp.where(even_lat, two[f], one[f])
        high = jnp.where(even_lat, one[f], two[f])
        for c in range(2):
            edges = [
                jnp.concatenate([low[:, col], field[:, col], high[:, col]], axis=0)
                for col in (c, cols - 2 + c)
            ]
            place = slice((2 * f + c) * tall, (2 * f + c + 1) * tall)
            first[place] = jnp.where(even, edges[1], edges[0])
            second[place] = jnp.where(even, edges[0], edges[1])


def pair_swap(one, two, axis, periodic):
    count = lax.axis_size(axis)
    pairs = [(i, i + 1) for i in range(0, count - 1, 2)]
    mates = [(i, i + 1) for i in range(1, count - 1, 2)]
    if periodic:
        mates.append((count - 1, 0))
    return tuple(
        lax.ppermute(block, axis, who + [(b, a) for a, b in who])
        for block, who in ((one, pairs), (two, mates))
    )


def prepare(weights, high, low):
    high[...], low[...] = split(weights[...])


def prepare_back(weights, high, low):
    size = weights.shape[1]
    for tap in range(9):
        there = 8 - tap
        block = weights[there * size : (there + 1) * size, :].T
        high[tap * size : (tap + 1) * size, :], low[tap * size : (tap + 1) * size, :] = split(block)


def turn(flip, value, high, low, scratch):
    channels = value.shape[1]
    each = channels // 8
    scratch[...] = value.T
    for i, block in enumerate(relative_blocks(flip)):
        part = scratch[pl.ds(pl.multiple_of(block * each, each), each), :]
        high[i * each : (i + 1) * each, :], low[i * each : (i + 1) * each, :] = split(part)


def turn_grad(here, grad, act, high, low, scratch):
    cells = grad.shape[0] * grad.shape[1]
    act[...] = silu(here[...])
    turn(False, grad[...].reshape(cells, grad.shape[2]), high, low, scratch)


def lay_taps(wide, x_high, x_low):
    rows, padded, channels = wide.shape
    cols = padded - 2 * EDGE
    for b in range(3):
        part = wide[:, EDGE - 1 + b : EDGE - 1 + b + cols, :].reshape(rows * cols, channels)
        high, low = split(part)
        x_high[:, b * channels : (b + 1) * channels] = high
        x_low[:, b * channels : (b + 1) * channels] = low


def convolve(x_high, x_low, first_row, rows, cols, w_high, w_low):
    channels = w_high.shape[1]
    total = None
    for a in range(3):
        cells = slice((first_row + a) * cols, (first_row + a + rows) * cols)
        taps = slice(a * 3 * channels, (a + 1) * 3 * channels)
        for x, w in ((x_high, w_high), (x_high, w_low), (x_low, w_high)):
            part = dot(x[cells, :], w[taps, :])
            total = part if total is None else total + part
    return total


def side_columns(mine_one, mine_two, got_one, got_two, f):
    even = lax.axis_index("lon") % 2 == 0
    tall = mine_one.shape[0] // 4
    rest = jnp.zeros((LINE - tall, mine_one.shape[1]), F32)

    def either(a, b, c):
        place = slice((2 * f + c) * tall, (2 * f + c + 1) * tall)
        return jnp.concatenate([jnp.where(even, a[place], b[place]), rest], axis=0)

    left = [either(got_two, got_one, c) for c in range(2)] + [either(mine_two, mine_one, 0)]
    right = [either(mine_one, mine_two, 1)] + [either(got_one, got_two, c) for c in range(2)]
    return left, right


def ring(left, right, w_high, w_low, r_high, r_low):
    channels = w_high.shape[1]
    for s, columns in enumerate((left, right)):
        for a in range(3):
            for b in range(3):
                high, low = split(columns[b])
                value = columns[b]
                if a:
                    value = jnp.concatenate(
                        [value[a:], jnp.zeros((a, value.shape[1]), F32)], axis=0
                    )
                place = (
                    slice(s * LINE, (s + 1) * LINE),
                    slice((a * 3 + b) * channels, (a * 3 + b + 1) * channels),
                )
                r_high[place], r_low[place] = split(value)
    return (
        dot(r_high[...], w_high[...])
        + dot(r_high[...], w_low[...])
        + dot(r_low[...], w_high[...])
    )


def spread(value, function, got_rows, columns, f, wide):
    rows, cols, channels = value.shape
    even_lat = lax.axis_index("lat") % 2 == 0
    one, two = got_rows
    wide[2 : rows + 2, EDGE : EDGE + cols, :] = value[...]
    wide[0:2, EDGE : EDGE + cols, :] = function(jnp.where(even_lat, two[f], one[f]))
    wide[rows + 2 : rows + 4, EDGE : EDGE + cols, :] = function(
        jnp.where(even_lat, one[f], two[f])
    )
    left, right = columns
    wide[:, EDGE - 1 : EDGE, :] = left[1][: rows + 4].reshape(rows + 4, 1, channels)
    wide[:, EDGE + cols : EDGE + cols + 1, :] = right[1][: rows + 4].reshape(rows + 4, 1, channels)


def inside(rows):
    row = lax.axis_index("lat") * rows - 1 + lax.broadcasted_iota(jnp.int32, (rows + 2, 1, 1), 0)
    return (row >= 0) & (row < rows * lax.axis_size("lat"))


def inside_line(rows):
    row = lax.axis_index("lat") * rows - 1 + lax.broadcasted_iota(jnp.int32, (LINE, 1), 0)
    return (row >= 0) & (row < rows * lax.axis_size("lat"))


def spread_ext(main, side, wide):
    tall, cols, channels = main.shape
    wide[:, EDGE : EDGE + cols, :] = main
    wide[:, EDGE - 1 : EDGE, :] = side[:tall].reshape(tall, 1, channels)
    wide[:, EDGE + cols : EDGE + cols + 1, :] = side[LINE : LINE + tall].reshape(tall, 1, channels)


def products(t_high, t_low, x_high, x_low, first_row, cells, cols, scale, *outs):
    width = x_high.shape[1]
    size = t_high.shape[0] // len(outs)
    for a in range(3):
        rows = slice((first_row + a) * cols, (first_row + a) * cols + cells)
        total = (
            dot(t_high[...], x_high[rows, :])
            + dot(t_high[...], x_low[rows, :])
            + dot(t_low[...], x_high[rows, :])
        ) * scale
        for i, out in enumerate(outs):
            out[:, a * width : (a + 1) * width] = total[i * size : (i + 1) * size]


def hidden_kernel(
    act, r1, r2, m1, m2, q1, q2, w_high, w_low,
    hidden, side, x1_high, x1_low, x2_high, x2_low,
    wide, wide2, r_high, r_low,
):
    rows, cols, channels = act.shape
    left, right = side_columns(m1, m2, q1, q2, 0)
    left, right = [silu(v) for v in left], [silu(v) for v in right]
    spread(act, silu, (r1, r2), (left, right), 0, wide)
    lay_taps(wide, x1_high, x1_low)
    main = convolve(x1_high, x1_low, 0, rows + 2, cols, w_high, w_low)
    around = ring(left, right, w_high, w_low, r_high, r_low)
    hidden[...] = main
    side[...] = around
    after = jnp.where(inside(rows), silu(main).reshape(rows + 2, cols, channels), 0.0)
    line = inside_line(rows)
    around = jnp.where(jnp.concatenate([line, line], axis=0), silu(around), 0.0)
    spread_ext(after, around, wide2)
    lay_taps(wide2, x2_high, x2_low)


def inner_kernel(
    grad, r1, r2, m1, m2, q1, q2, w_high, w_low, hidden, side,
    x3_high, x3_low, t_high, t_low,
    wide, xc_high, xc_low, wide2, r_high, r_low, turned,
):
    rows, cols, channels = grad.shape
    columns = side_columns(m1, m2, q1, q2, 1)
    spread(grad, lambda v: v, (r1, r2), columns, 1, wide)
    lay_taps(wide, xc_high, xc_low)
    main = convolve(xc_high, xc_low, 0, rows + 2, cols, w_high, w_low) * slope(hidden[...])
    around = ring(*columns, w_high, w_low, r_high, r_low) * slope(side[...])
    main = jnp.where(inside(rows), main.reshape(rows + 2, cols, channels), 0.0)
    line = inside_line(rows)
    around = jnp.where(jnp.concatenate([line, line], axis=0), around, 0.0)
    turn(True, main[1 : rows + 1].reshape(rows * cols, channels), t_high, t_low, turned)
    spread_ext(main, around, wide2)
    lay_taps(wide2, x3_high, x3_low)


def products_kernel(scale, cols, first_row, t_high, t_low, x_high, x_low, *outs):
    products(t_high, t_low, x_high, x_low, first_row, t_high.shape[1], cols, scale, *outs)


def output_kernel(here, x_high, x_low, w_high, w_low, out, token):
    token[...] = jnp.zeros(token.shape, F32)
    rows, cols, channels = here.shape
    total = convolve(x_high, x_low, 0, rows, cols, w_high, w_low)
    out[...] = here[...] + total.reshape(rows, cols, channels)


def input_grad_kernel(here, grad, x_high, x_low, w_high, w_low, out, token):
    token[...] = jnp.zeros(token.shape, F32)
    rows, cols, channels = here.shape
    total = convolve(x_high, x_low, 0, rows, cols, w_high, w_low)
    out[...] = grad[...] + total.reshape(rows, cols, channels) * slope(here[...])


def plane_perm(count, even, odd):
    return [(i, i ^ (odd if (i // 2) % 2 else even)) for i in range(count)]


def plane_swap(away, across):
    count = lax.axis_size("lat") * lax.axis_size("rep")
    one, two = (4, 1) if across else (1, 4)
    return lax.ppermute(away, ("lat", "rep"), plane_perm(count, one, two))


def core_swap(away):
    count = lax.axis_size("lat") * lax.axis_size("rep")
    return lax.ppermute(away, ("lat", "rep"), plane_perm(count, 2, 2))


def add_halves(keep, got, next_keep, next_away, *token):
    for ref in token:
        ref[...] = jnp.zeros(ref.shape, F32)
    half = keep.shape[0] // 2
    next_keep[...] = keep[:half] + got[:half]
    next_away[...] = keep[half:] + got[half:]


def add_up(keep, got, away):
    away[...] = keep[...] + got[...]


def add_three(keep_one, keep_two, core_one, core_two, got, next_keep, next_away):
    half = keep_one.shape[0]
    next_keep[...] = keep_one[...] + core_one[...] + got[:half]
    next_away[...] = keep_two[...] + core_two[...] + got[half:]


def pack(block):
    rows, width = block.shape
    whole = width // LANES
    pieces = [block[:, i * LANES : (i + 1) * LANES] for i in range(whole)]
    rest = block[:, whole * LANES :]
    pieces.append(jnp.concatenate([rest[: rows // 2], rest[rows // 2 :]], axis=1))
    return jnp.concatenate(pieces, axis=0)


def unpack(packed, rows):
    whole = packed.shape[0] // rows
    pieces = [packed[i * rows : (i + 1) * rows] for i in range(whole)]
    rest = packed[whole * rows :]
    half = LANES // 2
    pieces.append(jnp.concatenate([rest[:, :half], rest[:, half:]], axis=0))
    return jnp.concatenate(pieces, axis=1)


def cut_blocks(keep, got, *outs):
    blocks = outs[:4]
    for token in outs[4:]:
        token[...] = jnp.zeros(token.shape, F32)
    total = keep[...] + got[...]
    count = len(blocks)
    size = total.shape[1] // count
    parts = [total[:, i * size : (i + 1) * size] for i in range(count)]
    z = lax.axis_index("lon")
    for step, block in enumerate(blocks):
        value = parts[step]
        for place in range(1, count):
            value = jnp.where(z == place, parts[place ^ step], value)
        block[...] = pack(value)


def wide_sum(keep, got):
    return lax.psum_scatter(keep + got, "lon", scatter_dimension=1, tiled=True).T


def add_blocks(one, two, three, four, out, *tokens):
    for token in tokens:
        token[...] = jnp.zeros(token.shape, F32)
    out[...] = unpack(one[...] + two[...] + three[...] + four[...], out.shape[0])


def send_blocks(keep, got, after=(), flops=0, tokens=()):
    each, taps = keep.shape
    lon = lax.axis_size("lon")
    outs = [((each * taps // lon // LANES, LANES), F32)] * lon + list(tokens)
    blocks = call(cut_blocks, outs, [keep, got], after=after, flops=flops)
    gots = [
        lax.ppermute(blocks[step], "lon", [(i, i ^ step) for i in range(lon)])
        for step in (3, 2, 1)
    ]
    return [blocks[0], *gots], blocks[lon:]


def local(inputs, cotangent, first_weight, second_weight):
    here, grad = inputs[0], cotangent[0]
    rows, cols, channels = here.shape
    cells, tall = rows * cols, rows + 2
    width = 3 * channels
    scale = 1.0 / math.sqrt(
        cells * lax.axis_size("rep") * lax.axis_size("lat") * lax.axis_size("lon")
    )
    edge = ((2, 2, cols, channels), F32)
    edges = [here[:2], here[rows - 2 :], grad[:2], grad[rows - 2 :]]
    one, two = call(pack_rows, [edge] * 2, edges)
    r1, r2 = pair_swap(one, two, "lat", False)
    pair = [((9 * channels, channels), BF16)] * 2
    w1_high, w1_low = call(prepare, pair, [first_weight])
    act, t_high, t_low = call(
        turn_grad,
        [((rows, cols, channels), F32)] + [((channels, cells), BF16)] * 2,
        [here, grad],
        scratch=[((channels, cells), F32)],
    )
    line = ((4 * (rows + 4), channels), F32)
    m1, m2 = call(pack_cols, [line] * 2, [here, grad, r1, r2], after=[t_low])
    q1, q2 = pair_swap(m1, m2, "lon", True)
    lines = ((2 * LINE, channels), F32)
    wide = ((rows + 4, cols + 2 * EDGE, channels), F32)
    wide2 = ((tall, cols + 2 * EDGE, channels), F32)
    taps_1 = [(((rows + 4) * cols, width), BF16)] * 2
    taps_2 = [((tall * cols, width), BF16)] * 2
    around = [((2 * LINE, 3 * width), BF16)] * 2
    halves = [((channels // 2, 9 * channels), F32)] * 2
    hidden, side, x1_high, x1_low, x2_high, x2_low = call(
        hidden_kernel,
        [((tall * cols, channels), F32), lines] + taps_1 + taps_2,
        [act, r1, r2, m1, m2, q1, q2, w1_high, w1_low],
        scratch=[wide, wide2] + around,
    )
    half = halves[0]
    each = channels // 8

    def halves_of(count):
        return [((count, 9 * channels), F32)] * 2

    quarter = ((2 * each, 9 * channels), F32)
    eighth = ((each, 9 * channels), F32)

    def second_products(first, outs, after):
        def rows_of(ref):
            starts = [first * 2 * each, (first + 2) * 2 * each]
            return jnp.concatenate([ref[i : i + 2 * each] for i in starts], axis=0)

        return call(
            lambda high, low, *refs: products_kernel(
                scale, cols, 0, rows_of(high), rows_of(low), *refs
            ),
            outs,
            [t_high, t_low, x2_high, x2_low],
            after=after,
        )

    keep_2, away_2 = second_products(1, [quarter] * 2, [])
    got_2 = core_swap(away_2)
    b2_high, b2_low = call(prepare_back, pair, [second_weight], after=[away_2])
    w2_high, w2_low = call(prepare, pair, [second_weight], after=[away_2])
    b1_high, b1_low = call(prepare_back, pair, [first_weight], after=[away_2])
    (away_2,) = call(add_up, [quarter], [keep_2, got_2], after=[b2_low])
    got_2 = plane_swap(away_2, False)
    *keeps, away_one, away_two = second_products(0, [eighth] * 4, [away_2])
    cores = [core_swap(away_one), core_swap(away_two)]
    x3_high, x3_low, t_high, t_low = call(
        inner_kernel,
        taps_2 + [((channels, cells), BF16)] * 2,
        [grad, r1, r2, m1, m2, q1, q2, b2_high, b2_low, hidden, side],
        scratch=[wide] + taps_1 + [wide2] + around + [((channels, cells), F32)],
        after=keeps[:1],
    )
    keep_1, away_1 = call(
        lambda *refs: products_kernel(scale, cols, 1, *refs),
        [half, half],
        [t_high, t_low, x1_high, x1_low],
    )
    got_1 = core_swap(away_1)
    keep_2, away_2 = call(
        add_three, halves_of(each), [*keeps, *cores, got_2], flops=LONG
    )
    got_2 = plane_swap(away_2, True)
    keep_1, away_1 = call(add_halves, halves_of(2 * each), [keep_1, got_1], after=[keep_2])
    got_1 = plane_swap(away_1, True)
    outs = [((rows, cols, channels), F32), ((8, 128), F32)]
    output, token = call(
        output_kernel, outs, [here, x2_high, x2_low, w2_high, w2_low], after=[keep_1]
    )
    direct = lax.axis_size("lon") == 4
    if direct:
        blocks, (token,) = send_blocks(keep_2, got_2, [token], LONG, outs[1:])
    else:
        second_grad = wide_sum(keep_2, got_2)
    keep_1, away_1 = call(add_halves, halves_of(each), [keep_1, got_1], after=[token])
    got_1 = plane_swap(away_1, False)
    input_grad, token = call(
        input_grad_kernel,
        outs,
        [here, grad, x3_high, x3_low, b1_high, b1_low],
        after=[keep_1],
    )
    if direct:
        shape = (each, 9 * channels // 4)
        summed, token = call(
            add_blocks, [(shape, F32), outs[1]], blocks, after=[token], flops=LONG
        )
        second_grad = summed.T
        blocks, _ = send_blocks(keep_1, got_1, [token])
        first_grad = call(add_blocks, [(shape, F32)], blocks)[0].T
    else:
        first_grad = wide_sum(keep_1, got_1)
    return (output[None], input_grad[None], first_grad, second_grad)


def solution(mesh):
    in_specs = (P("rep", "lat", "lon", None), P("rep", "lat", "lon", None), P(), P())
    out_specs = (
        P("rep", "lat", "lon", None),
        P("rep", "lat", "lon", None),
        P("lon", ("lat", "rep")),
        P("lon", ("lat", "rep")),
    )
    return jax.shard_map(local, mesh=mesh, in_specs=in_specs, out_specs=out_specs, check_vma=False)
```

```python
import math

import jax
import jax.numpy as jnp
from jax import lax
from jax.experimental import pallas as pl
from jax.experimental.pallas import tpu as pltpu
from jax.sharding import PartitionSpec as P

F32 = jnp.float32
BF16 = jnp.bfloat16
VMEM = pl.BlockSpec(memory_space=pltpu.VMEM)
LONG = 10**10
LANES = 128
LINE = 24
EDGE = 8


def call(body, outs, ins, scratch=(), limit=16, after=(), flops=0):
    used, skip = len(ins), len(after)

    def kernel(*refs):
        body(*refs[:used], *refs[used + skip :])

    ins = list(ins) + list(after)
    return pl.pallas_call(
        kernel,
        out_shape=[jax.ShapeDtypeStruct(shape, dtype) for shape, dtype in outs],
        in_specs=[VMEM] * used + [pl.BlockSpec(memory_space=pl.ANY)] * skip,
        out_specs=[VMEM] * len(outs),
        scratch_shapes=[pltpu.VMEM(shape, dtype) for shape, dtype in scratch],
        compiler_params=pltpu.CompilerParams(vmem_limit_bytes=limit * 1024 * 1024),
        cost_estimate=pl.CostEstimate(flops=flops, bytes_accessed=0, transcendentals=0),
    )(*ins)


def split(value):
    high = value.astype(BF16)
    return high, (value - high.astype(F32)).astype(BF16)


def dot(a, b):
    return jnp.dot(a, b, preferred_element_type=F32)


def sigmoid(value):
    return 0.5 * jnp.tanh(0.5 * value) + 0.5


def silu(value):
    return value * sigmoid(value)


def slope(value):
    sigma = sigmoid(value)
    return sigma * (1.0 + value * (1.0 - sigma))


def relative_blocks(flip):
    lat, y = lax.axis_index("lat"), lax.axis_index("rep")
    x, core = lat // 2, lat % 2
    order = []
    for r_core in range(2):
        c = core + r_core - 2 * core * r_core
        y_first = c == (1 if flip else 0)
        for r_first in range(2):
            for r_second in range(2):
                move_y = jnp.where(y_first, r_first, r_second)
                move_x = jnp.where(y_first, r_second, r_first)
                there_y = y + move_y - 2 * y * move_y
                there_x = x + move_x - 2 * x * move_x
                order.append(there_x * 4 + c * 2 + there_y)
    return order


def pack_rows(low_here, high_here, low_grad, high_grad, one, two):
    even = lax.axis_index("lat") % 2 == 0
    for f, (low, high) in enumerate(((low_here, high_here), (low_grad, high_grad))):
        one[f] = jnp.where(even, high[...], low[...])
        two[f] = jnp.where(even, low[...], high[...])


def pack_cols(here, grad, one, two, first, second):
    rows, cols = here.shape[:2]
    tall = rows + 4
    even_lat = lax.axis_index("lat") % 2 == 0
    even = lax.axis_index("lon") % 2 == 0
    for f, field in enumerate((here, grad)):
        low = jnp.where(even_lat, two[f], one[f])
        high = jnp.where(even_lat, one[f], two[f])
        for c in range(2):
            edges = [
                jnp.concatenate([low[:, col], field[:, col], high[:, col]], axis=0)
                for col in (c, cols - 2 + c)
            ]
            place = slice((2 * f + c) * tall, (2 * f + c + 1) * tall)
            first[place] = jnp.where(even, edges[1], edges[0])
            second[place] = jnp.where(even, edges[0], edges[1])


def pair_swap(one, two, axis, periodic):
    count = lax.axis_size(axis)
    pairs = [(i, i + 1) for i in range(0, count - 1, 2)]
    mates = [(i, i + 1) for i in range(1, count - 1, 2)]
    if periodic:
        mates.append((count - 1, 0))
    return tuple(
        lax.ppermute(block, axis, who + [(b, a) for a, b in who])
        for block, who in ((one, pairs), (two, mates))
    )


def prepare(weights, high, low):
    high[...], low[...] = split(weights[...])


def prepare_back(weights, high, low):
    size = weights.shape[1]
    for tap in range(9):
        there = 8 - tap
        block = weights[there * size : (there + 1) * size, :].T
        high[tap * size : (tap + 1) * size, :], low[tap * size : (tap + 1) * size, :] = split(block)


def turn(flip, value, high, low, scratch):
    channels = value.shape[1]
    each = channels // 8
    scratch[...] = value.T
    for i, block in enumerate(relative_blocks(flip)):
        part = scratch[pl.ds(pl.multiple_of(block * each, each), each), :]
        high[i * each : (i + 1) * each, :], low[i * each : (i + 1) * each, :] = split(part)


def turn_grad(here, grad, act, high, low, scratch):
    cells = grad.shape[0] * grad.shape[1]
    act[...] = silu(here[...])
    turn(False, grad[...].reshape(cells, grad.shape[2]), high, low, scratch)


def lay_taps(wide, x_high, x_low):
    rows, padded, channels = wide.shape
    cols = padded - 2 * EDGE
    for b in range(3):
        part = wide[:, EDGE - 1 + b : EDGE - 1 + b + cols, :].reshape(rows * cols, channels)
        high, low = split(part)
        x_high[:, b * channels : (b + 1) * channels] = high
        x_low[:, b * channels : (b + 1) * channels] = low


def convolve(x_high, x_low, first_row, rows, cols, w_high, w_low):
    channels = w_high.shape[1]
    total = None
    for a in range(3):
        cells = slice((first_row + a) * cols, (first_row + a + rows) * cols)
        taps = slice(a * 3 * channels, (a + 1) * 3 * channels)
        for x, w in ((x_high, w_high), (x_high, w_low), (x_low, w_high)):
            part = dot(x[cells, :], w[taps, :])
            total = part if total is None else total + part
    return total


def side_columns(mine_one, mine_two, got_one, got_two, f):
    even = lax.axis_index("lon") % 2 == 0
    tall = mine_one.shape[0] // 4
    rest = jnp.zeros((LINE - tall, mine_one.shape[1]), F32)

    def either(a, b, c):
        place = slice((2 * f + c) * tall, (2 * f + c + 1) * tall)
        return jnp.concatenate([jnp.where(even, a[place], b[place]), rest], axis=0)

    left = [either(got_two, got_one, c) for c in range(2)] + [either(mine_two, mine_one, 0)]
    right = [either(mine_one, mine_two, 1)] + [either(got_one, got_two, c) for c in range(2)]
    return left, right


def ring(left, right, w_high, w_low, r_high, r_low):
    channels = w_high.shape[1]
    for s, columns in enumerate((left, right)):
        for a in range(3):
            for b in range(3):
                high, low = split(columns[b])
                value = columns[b]
                if a:
                    value = jnp.concatenate(
                        [value[a:], jnp.zeros((a, value.shape[1]), F32)], axis=0
                    )
                place = (
                    slice(s * LINE, (s + 1) * LINE),
                    slice((a * 3 + b) * channels, (a * 3 + b + 1) * channels),
                )
                r_high[place], r_low[place] = split(value)
    return (
        dot(r_high[...], w_high[...])
        + dot(r_high[...], w_low[...])
        + dot(r_low[...], w_high[...])
    )


def spread(value, function, got_rows, columns, f, wide):
    rows, cols, channels = value.shape
    even_lat = lax.axis_index("lat") % 2 == 0
    one, two = got_rows
    wide[2 : rows + 2, EDGE : EDGE + cols, :] = value[...]
    wide[0:2, EDGE : EDGE + cols, :] = function(jnp.where(even_lat, two[f], one[f]))
    wide[rows + 2 : rows + 4, EDGE : EDGE + cols, :] = function(
        jnp.where(even_lat, one[f], two[f])
    )
    left, right = columns
    wide[:, EDGE - 1 : EDGE, :] = left[1][: rows + 4].reshape(rows + 4, 1, channels)
    wide[:, EDGE + cols : EDGE + cols + 1, :] = right[1][: rows + 4].reshape(rows + 4, 1, channels)


def inside(rows):
    row = lax.axis_index("lat") * rows - 1 + lax.broadcasted_iota(jnp.int32, (rows + 2, 1, 1), 0)
    return (row >= 0) & (row < rows * lax.axis_size("lat"))


def inside_line(rows):
    row = lax.axis_index("lat") * rows - 1 + lax.broadcasted_iota(jnp.int32, (LINE, 1), 0)
    return (row >= 0) & (row < rows * lax.axis_size("lat"))


def spread_ext(main, side, wide):
    tall, cols, channels = main.shape
    wide[:, EDGE : EDGE + cols, :] = main
    wide[:, EDGE - 1 : EDGE, :] = side[:tall].reshape(tall, 1, channels)
    wide[:, EDGE + cols : EDGE + cols + 1, :] = side[LINE : LINE + tall].reshape(tall, 1, channels)


def products(t_high, t_low, x_high, x_low, first_row, cells, cols, scale, *outs):
    width = x_high.shape[1]
    size = t_high.shape[0] // len(outs)
    for a in range(3):
        rows = slice((first_row + a) * cols, (first_row + a) * cols + cells)
        total = (
            dot(t_high[...], x_high[rows, :])
            + dot(t_high[...], x_low[rows, :])
            + dot(t_low[...], x_high[rows, :])
        ) * scale
        for i, out in enumerate(outs):
            out[:, a * width : (a + 1) * width] = total[i * size : (i + 1) * size]


def hidden_kernel(
    act, r1, r2, m1, m2, q1, q2, w_high, w_low,
    hidden, side, x1_high, x1_low, x2_high, x2_low,
    wide, wide2, r_high, r_low,
):
    rows, cols, channels = act.shape
    left, right = side_columns(m1, m2, q1, q2, 0)
    left, right = [silu(v) for v in left], [silu(v) for v in right]
    spread(act, silu, (r1, r2), (left, right), 0, wide)
    lay_taps(wide, x1_high, x1_low)
    main = convolve(x1_high, x1_low, 0, rows + 2, cols, w_high, w_low)
    around = ring(left, right, w_high, w_low, r_high, r_low)
    hidden[...] = main
    side[...] = around
    after = jnp.where(inside(rows), silu(main).reshape(rows + 2, cols, channels), 0.0)
    line = inside_line(rows)
    around = jnp.where(jnp.concatenate([line, line], axis=0), silu(around), 0.0)
    spread_ext(after, around, wide2)
    lay_taps(wide2, x2_high, x2_low)


def inner_kernel(
    grad, r1, r2, m1, m2, q1, q2, w_high, w_low, hidden, side,
    x3_high, x3_low, t_high, t_low,
    wide, xc_high, xc_low, wide2, r_high, r_low, turned,
):
    rows, cols, channels = grad.shape
    columns = side_columns(m1, m2, q1, q2, 1)
    spread(grad, lambda v: v, (r1, r2), columns, 1, wide)
    lay_taps(wide, xc_high, xc_low)
    main = convolve(xc_high, xc_low, 0, rows + 2, cols, w_high, w_low) * slope(hidden[...])
    around = ring(*columns, w_high, w_low, r_high, r_low) * slope(side[...])
    main = jnp.where(inside(rows), main.reshape(rows + 2, cols, channels), 0.0)
    line = inside_line(rows)
    around = jnp.where(jnp.concatenate([line, line], axis=0), around, 0.0)
    turn(True, main[1 : rows + 1].reshape(rows * cols, channels), t_high, t_low, turned)
    spread_ext(main, around, wide2)
    lay_taps(wide2, x3_high, x3_low)


def products_kernel(scale, cols, first_row, t_high, t_low, x_high, x_low, *outs):
    products(t_high, t_low, x_high, x_low, first_row, t_high.shape[1], cols, scale, *outs)


def output_kernel(here, x_high, x_low, w_high, w_low, out, token):
    token[...] = jnp.zeros(token.shape, F32)
    rows, cols, channels = here.shape
    total = convolve(x_high, x_low, 0, rows, cols, w_high, w_low)
    out[...] = here[...] + total.reshape(rows, cols, channels)


def input_grad_kernel(here, grad, x_high, x_low, w_high, w_low, out, token):
    token[...] = jnp.zeros(token.shape, F32)
    rows, cols, channels = here.shape
    total = convolve(x_high, x_low, 0, rows, cols, w_high, w_low)
    out[...] = grad[...] + total.reshape(rows, cols, channels) * slope(here[...])


def plane_perm(count, even, odd):
    return [(i, i ^ (odd if (i // 2) % 2 else even)) for i in range(count)]


def plane_swap(away, across):
    count = lax.axis_size("lat") * lax.axis_size("rep")
    one, two = (4, 1) if across else (1, 4)
    return lax.ppermute(away, ("lat", "rep"), plane_perm(count, one, two))


def core_swap(away):
    count = lax.axis_size("lat") * lax.axis_size("rep")
    return lax.ppermute(away, ("lat", "rep"), plane_perm(count, 2, 2))


def add_halves(keep, got, next_keep, next_away, *token):
    for ref in token:
        ref[...] = jnp.zeros(ref.shape, F32)
    half = keep.shape[0] // 2
    next_keep[...] = keep[:half] + got[:half]
    next_away[...] = keep[half:] + got[half:]


def add_up(keep, got, away):
    away[...] = keep[...] + got[...]


def add_three(keep_one, keep_two, core_one, core_two, got, next_keep, next_away):
    half = keep_one.shape[0]
    next_keep[...] = keep_one[...] + core_one[...] + got[:half]
    next_away[...] = keep_two[...] + core_two[...] + got[half:]


def pack(total, place):
    rows, width = total.shape
    tiles = width // LANES // 4
    start = (place // 2) * (2 * tiles + 1)
    whole = start + (place % 2) * (tiles + 1)
    pieces = [total[:, i * LANES : (i + 1) * LANES] for i in range(whole, whole + tiles)]
    half = LANES // 2
    left = (start + tiles) * LANES + (place % 2) * half
    rest = total[:, left : left + half]
    pieces.append(jnp.concatenate([rest[: rows // 2], rest[rows // 2 :]], axis=1))
    return jnp.concatenate(pieces, axis=0)


def unpack(packed, rows):
    whole = packed.shape[0] // rows
    pieces = [packed[i * rows : (i + 1) * rows] for i in range(whole)]
    rest = packed[whole * rows :]
    half = LANES // 2
    rest = jnp.concatenate([rest[:, :half], rest[:, half:]], axis=0)
    odd = lax.axis_index("lon") % 2 == 1
    return jnp.where(
        odd,
        jnp.concatenate([rest, *pieces], axis=1),
        jnp.concatenate([*pieces, rest], axis=1),
    )


def cut_blocks(keep, got, *outs):
    blocks = outs[:4]
    for token in outs[4:]:
        token[...] = jnp.zeros(token.shape, F32)
    total = keep[...] + got[...]
    count = len(blocks)
    parts = [pack(total, place) for place in range(count)]
    z = lax.axis_index("lon")
    for step, block in enumerate(blocks):
        value = parts[step]
        for place in range(1, count):
            value = jnp.where(z == place, parts[place ^ step], value)
        block[...] = value


def wide_sum(keep, got):
    return lax.psum_scatter(keep + got, "lon", scatter_dimension=1, tiled=True).T


def add_blocks(one, two, three, four, out, *tokens):
    for token in tokens:
        token[...] = jnp.zeros(token.shape, F32)
    out[...] = unpack(one[...] + two[...] + three[...] + four[...], out.shape[0])


def send_blocks(keep, got, after=(), flops=0, tokens=()):
    each, taps = keep.shape
    lon = lax.axis_size("lon")
    outs = [((each * taps // lon // LANES, LANES), F32)] * lon + list(tokens)
    blocks = call(cut_blocks, outs, [keep, got], after=after, flops=flops)
    gots = [
        lax.ppermute(blocks[step], "lon", [(i, i ^ step) for i in range(lon)])
        for step in (3, 2, 1)
    ]
    return [blocks[0], *gots], blocks[lon:]


def local(inputs, cotangent, first_weight, second_weight):
    here, grad = inputs[0], cotangent[0]
    rows, cols, channels = here.shape
    cells, tall = rows * cols, rows + 2
    width = 3 * channels
    scale = 1.0 / math.sqrt(
        cells * lax.axis_size("rep") * lax.axis_size("lat") * lax.axis_size("lon")
    )
    edge = ((2, 2, cols, channels), F32)
    edges = [here[:2], here[rows - 2 :], grad[:2], grad[rows - 2 :]]
    one, two = call(pack_rows, [edge] * 2, edges)
    r1, r2 = pair_swap(one, two, "lat", False)
    pair = [((9 * channels, channels), BF16)] * 2
    w1_high, w1_low = call(prepare, pair, [first_weight])
    act, t_high, t_low = call(
        turn_grad,
        [((rows, cols, channels), F32)] + [((channels, cells), BF16)] * 2,
        [here, grad],
        scratch=[((channels, cells), F32)],
    )
    line = ((4 * (rows + 4), channels), F32)
    m1, m2 = call(pack_cols, [line] * 2, [here, grad, r1, r2], after=[t_low])
    q1, q2 = pair_swap(m1, m2, "lon", True)
    lines = ((2 * LINE, channels), F32)
    wide = ((rows + 4, cols + 2 * EDGE, channels), F32)
    wide2 = ((tall, cols + 2 * EDGE, channels), F32)
    taps_1 = [(((rows + 4) * cols, width), BF16)] * 2
    taps_2 = [((tall * cols, width), BF16)] * 2
    around = [((2 * LINE, 3 * width), BF16)] * 2
    halves = [((channels // 2, 9 * channels), F32)] * 2
    hidden, side, x1_high, x1_low, x2_high, x2_low = call(
        hidden_kernel,
        [((tall * cols, channels), F32), lines] + taps_1 + taps_2,
        [act, r1, r2, m1, m2, q1, q2, w1_high, w1_low],
        scratch=[wide, wide2] + around,
    )
    half = halves[0]
    each = channels // 8

    def halves_of(count):
        return [((count, 9 * channels), F32)] * 2

    quarter = ((2 * each, 9 * channels), F32)
    eighth = ((each, 9 * channels), F32)

    def second_products(first, outs, after):
        def rows_of(ref):
            starts = [first * 2 * each, (first + 2) * 2 * each]
            return jnp.concatenate([ref[i : i + 2 * each] for i in starts], axis=0)

        return call(
            lambda high, low, *refs: products_kernel(
                scale, cols, 0, rows_of(high), rows_of(low), *refs
            ),
            outs,
            [t_high, t_low, x2_high, x2_low],
            after=after,
        )

    keep_2, away_2 = second_products(1, [quarter] * 2, [])
    got_2 = core_swap(away_2)
    b2_high, b2_low = call(prepare_back, pair, [second_weight], after=[away_2])
    w2_high, w2_low = call(prepare, pair, [second_weight], after=[away_2])
    b1_high, b1_low = call(prepare_back, pair, [first_weight], after=[away_2])
    (away_2,) = call(add_up, [quarter], [keep_2, got_2], after=[b2_low])
    got_2 = plane_swap(away_2, False)
    *keeps, away_one, away_two = second_products(0, [eighth] * 4, [away_2])
    cores = [core_swap(away_one), core_swap(away_two)]
    x3_high, x3_low, t_high, t_low = call(
        inner_kernel,
        taps_2 + [((channels, cells), BF16)] * 2,
        [grad, r1, r2, m1, m2, q1, q2, b2_high, b2_low, hidden, side],
        scratch=[wide] + taps_1 + [wide2] + around + [((channels, cells), F32)],
        after=keeps[:1],
    )
    keep_1, away_1 = call(
        lambda *refs: products_kernel(scale, cols, 1, *refs),
        [half, half],
        [t_high, t_low, x1_high, x1_low],
    )
    got_1 = core_swap(away_1)
    keep_2, away_2 = call(
        add_three, halves_of(each), [*keeps, *cores, got_2], flops=LONG
    )
    got_2 = plane_swap(away_2, True)
    keep_1, away_1 = call(add_halves, halves_of(2 * each), [keep_1, got_1], after=[keep_2])
    got_1 = plane_swap(away_1, True)
    outs = [((rows, cols, channels), F32), ((8, 128), F32)]
    output, token = call(
        output_kernel, outs, [here, x2_high, x2_low, w2_high, w2_low], after=[keep_1]
    )
    direct = lax.axis_size("lon") == 4
    if direct:
        blocks, (token,) = send_blocks(keep_2, got_2, [token], LONG, outs[1:])
    else:
        second_grad = wide_sum(keep_2, got_2)
    keep_1, away_1 = call(add_halves, halves_of(each), [keep_1, got_1], after=[token])
    got_1 = plane_swap(away_1, False)
    input_grad, token = call(
        input_grad_kernel,
        outs,
        [here, grad, x3_high, x3_low, b1_high, b1_low],
        after=[keep_1],
    )
    if direct:
        shape = (each, 9 * channels // 4)
        summed, token = call(
            add_blocks, [(shape, F32), outs[1]], blocks, after=[token], flops=LONG
        )
        second_grad = summed.T
        blocks, _ = send_blocks(keep_1, got_1, [token])
        first_grad = call(add_blocks, [(shape, F32)], blocks)[0].T
    else:
        first_grad = wide_sum(keep_1, got_1)
    return (output[None], input_grad[None], first_grad, second_grad)


def solution(mesh):
    in_specs = (P("rep", "lat", "lon", None), P("rep", "lat", "lon", None), P(), P())
    out_specs = (
        P("rep", "lat", "lon", None),
        P("rep", "lat", "lon", None),
        P("lon", ("lat", "rep")),
        P("lon", ("lat", "rep")),
    )
    return jax.shard_map(local, mesh=mesh, in_specs=in_specs, out_specs=out_specs, check_vma=False)
```

```python
import math

import jax
import jax.numpy as jnp
from jax import lax
from jax.experimental import pallas as pl
from jax.experimental.pallas import tpu as pltpu
from jax.sharding import PartitionSpec as P

F32 = jnp.float32
BF16 = jnp.bfloat16
VMEM = pl.BlockSpec(memory_space=pltpu.VMEM)
LONG = 10**10
LANES = 128
LINE = 24
EDGE = 8


def call(body, outs, ins, scratch=(), limit=16, after=(), flops=0):
    used, skip = len(ins), len(after)

    def kernel(*refs):
        body(*refs[:used], *refs[used + skip :])

    ins = list(ins) + list(after)
    return pl.pallas_call(
        kernel,
        out_shape=[jax.ShapeDtypeStruct(shape, dtype) for shape, dtype in outs],
        in_specs=[VMEM] * used + [pl.BlockSpec(memory_space=pl.ANY)] * skip,
        out_specs=[VMEM] * len(outs),
        scratch_shapes=[pltpu.VMEM(shape, dtype) for shape, dtype in scratch],
        compiler_params=pltpu.CompilerParams(vmem_limit_bytes=limit * 1024 * 1024),
        cost_estimate=pl.CostEstimate(flops=flops, bytes_accessed=0, transcendentals=0),
    )(*ins)


def split(value):
    high = value.astype(BF16)
    return high, (value - high.astype(F32)).astype(BF16)


def dot(a, b):
    return jnp.dot(a, b, preferred_element_type=F32)


def sigmoid(value):
    return 0.5 * jnp.tanh(0.5 * value) + 0.5


def silu(value):
    return value * sigmoid(value)


def slope(value):
    sigma = sigmoid(value)
    return sigma * (1.0 + value * (1.0 - sigma))


def relative_blocks(flip):
    lat, y = lax.axis_index("lat"), lax.axis_index("rep")
    x, core = lat // 2, lat % 2
    order = []
    for r_core in range(2):
        c = core + r_core - 2 * core * r_core
        y_first = c == (1 if flip else 0)
        for r_first in range(2):
            for r_second in range(2):
                move_y = jnp.where(y_first, r_first, r_second)
                move_x = jnp.where(y_first, r_second, r_first)
                there_y = y + move_y - 2 * y * move_y
                there_x = x + move_x - 2 * x * move_x
                order.append(there_x * 4 + c * 2 + there_y)
    return order


def pack_rows(low_here, high_here, low_grad, high_grad, one, two):
    even = lax.axis_index("lat") % 2 == 0
    for f, (low, high) in enumerate(((low_here, high_here), (low_grad, high_grad))):
        one[f] = jnp.where(even, high[...], low[...])
        two[f] = jnp.where(even, low[...], high[...])


def pack_cols(here, grad, one, two, first, second):
    rows, cols = here.shape[:2]
    tall = rows + 4
    even_lat = lax.axis_index("lat") % 2 == 0
    even = lax.axis_index("lon") % 2 == 0
    for f, field in enumerate((here, grad)):
        low = jnp.where(even_lat, two[f], one[f])
        high = jnp.where(even_lat, one[f], two[f])
        for c in range(2):
            edges = [
                jnp.concatenate([low[:, col], field[:, col], high[:, col]], axis=0)
                for col in (c, cols - 2 + c)
            ]
            place = slice((2 * f + c) * tall, (2 * f + c + 1) * tall)
            first[place] = jnp.where(even, edges[1], edges[0])
            second[place] = jnp.where(even, edges[0], edges[1])


def pair_swap(one, two, axis, periodic):
    count = lax.axis_size(axis)
    pairs = [(i, i + 1) for i in range(0, count - 1, 2)]
    mates = [(i, i + 1) for i in range(1, count - 1, 2)]
    if periodic:
        mates.append((count - 1, 0))
    return tuple(
        lax.ppermute(block, axis, who + [(b, a) for a, b in who])
        for block, who in ((one, pairs), (two, mates))
    )


def prepare(weights, high, low):
    high[...], low[...] = split(weights[...])


def prepare_back(weights, high, low):
    size = weights.shape[1]
    for tap in range(9):
        there = 8 - tap
        block = weights[there * size : (there + 1) * size, :].T
        high[tap * size : (tap + 1) * size, :], low[tap * size : (tap + 1) * size, :] = split(block)


def turn(flip, value, high, low, scratch):
    channels = value.shape[1]
    each = channels // 8
    scratch[...] = value.T
    for i, block in enumerate(relative_blocks(flip)):
        part = scratch[pl.ds(pl.multiple_of(block * each, each), each), :]
        high[i * each : (i + 1) * each, :], low[i * each : (i + 1) * each, :] = split(part)


def turn_grad(here, grad, act, high, low, scratch):
    cells = grad.shape[0] * grad.shape[1]
    act[...] = silu(here[...])
    turn(False, grad[...].reshape(cells, grad.shape[2]), high, low, scratch)


def lay_taps(wide, x_high, x_low):
    rows, padded, channels = wide.shape
    cols = padded - 2 * EDGE
    for b in range(3):
        part = wide[:, EDGE - 1 + b : EDGE - 1 + b + cols, :].reshape(rows * cols, channels)
        high, low = split(part)
        x_high[:, b * channels : (b + 1) * channels] = high
        x_low[:, b * channels : (b + 1) * channels] = low


def convolve(x_high, x_low, first_row, rows, cols, w_high, w_low):
    channels = w_high.shape[1]
    total = None
    for a in range(3):
        cells = slice((first_row + a) * cols, (first_row + a + rows) * cols)
        taps = slice(a * 3 * channels, (a + 1) * 3 * channels)
        for x, w in ((x_high, w_high), (x_high, w_low), (x_low, w_high)):
            part = dot(x[cells, :], w[taps, :])
            total = part if total is None else total + part
    return total


def side_columns(mine_one, mine_two, got_one, got_two, f):
    even = lax.axis_index("lon") % 2 == 0
    tall = mine_one.shape[0] // 4
    rest = jnp.zeros((LINE - tall, mine_one.shape[1]), F32)

    def either(a, b, c):
        place = slice((2 * f + c) * tall, (2 * f + c + 1) * tall)
        return jnp.concatenate([jnp.where(even, a[place], b[place]), rest], axis=0)

    left = [either(got_two, got_one, c) for c in range(2)] + [either(mine_two, mine_one, 0)]
    right = [either(mine_one, mine_two, 1)] + [either(got_one, got_two, c) for c in range(2)]
    return left, right


def ring(left, right, w_high, w_low, r_high, r_low):
    channels = w_high.shape[1]
    for s, columns in enumerate((left, right)):
        for a in range(3):
            for b in range(3):
                high, low = split(columns[b])
                value = columns[b]
                if a:
                    value = jnp.concatenate(
                        [value[a:], jnp.zeros((a, value.shape[1]), F32)], axis=0
                    )
                place = (
                    slice(s * LINE, (s + 1) * LINE),
                    slice((a * 3 + b) * channels, (a * 3 + b + 1) * channels),
                )
                r_high[place], r_low[place] = split(value)
    return (
        dot(r_high[...], w_high[...])
        + dot(r_high[...], w_low[...])
        + dot(r_low[...], w_high[...])
    )


def spread(value, function, got_rows, columns, f, wide):
    rows, cols, channels = value.shape
    even_lat = lax.axis_index("lat") % 2 == 0
    one, two = got_rows
    wide[2 : rows + 2, EDGE : EDGE + cols, :] = value[...]
    wide[0:2, EDGE : EDGE + cols, :] = function(jnp.where(even_lat, two[f], one[f]))
    wide[rows + 2 : rows + 4, EDGE : EDGE + cols, :] = function(
        jnp.where(even_lat, one[f], two[f])
    )
    left, right = columns
    wide[:, EDGE - 1 : EDGE, :] = left[1][: rows + 4].reshape(rows + 4, 1, channels)
    wide[:, EDGE + cols : EDGE + cols + 1, :] = right[1][: rows + 4].reshape(rows + 4, 1, channels)


def inside(rows):
    row = lax.axis_index("lat") * rows - 1 + lax.broadcasted_iota(jnp.int32, (rows + 2, 1, 1), 0)
    return (row >= 0) & (row < rows * lax.axis_size("lat"))


def inside_line(rows):
    row = lax.axis_index("lat") * rows - 1 + lax.broadcasted_iota(jnp.int32, (LINE, 1), 0)
    return (row >= 0) & (row < rows * lax.axis_size("lat"))


def spread_ext(main, side, wide):
    tall, cols, channels = main.shape
    wide[:, EDGE : EDGE + cols, :] = main
    wide[:, EDGE - 1 : EDGE, :] = side[:tall].reshape(tall, 1, channels)
    wide[:, EDGE + cols : EDGE + cols + 1, :] = side[LINE : LINE + tall].reshape(tall, 1, channels)


def products(t_high, t_low, x_high, x_low, first_row, cells, cols, scale, *outs):
    width = x_high.shape[1]
    size = t_high.shape[0] // len(outs)
    for a in range(3):
        rows = slice((first_row + a) * cols, (first_row + a) * cols + cells)
        total = (
            dot(t_high[...], x_high[rows, :])
            + dot(t_high[...], x_low[rows, :])
            + dot(t_low[...], x_high[rows, :])
        ) * scale
        for i, out in enumerate(outs):
            out[:, a * width : (a + 1) * width] = total[i * size : (i + 1) * size]


def hidden_kernel(
    act, r1, r2, m1, m2, q1, q2, w_high, w_low,
    hidden, side, x1_high, x1_low, x2_high, x2_low,
    wide, wide2, r_high, r_low,
):
    rows, cols, channels = act.shape
    left, right = side_columns(m1, m2, q1, q2, 0)
    left, right = [silu(v) for v in left], [silu(v) for v in right]
    spread(act, silu, (r1, r2), (left, right), 0, wide)
    lay_taps(wide, x1_high, x1_low)
    main = convolve(x1_high, x1_low, 0, rows + 2, cols, w_high, w_low)
    around = ring(left, right, w_high, w_low, r_high, r_low)
    hidden[...] = main
    side[...] = around
    after = jnp.where(inside(rows), silu(main).reshape(rows + 2, cols, channels), 0.0)
    line = inside_line(rows)
    around = jnp.where(jnp.concatenate([line, line], axis=0), silu(around), 0.0)
    spread_ext(after, around, wide2)
    lay_taps(wide2, x2_high, x2_low)


def inner_kernel(
    grad, r1, r2, m1, m2, q1, q2, w_high, w_low, hidden, side,
    x3_high, x3_low, t_high, t_low,
    wide, xc_high, xc_low, wide2, r_high, r_low, turned,
):
    rows, cols, channels = grad.shape
    columns = side_columns(m1, m2, q1, q2, 1)
    spread(grad, lambda v: v, (r1, r2), columns, 1, wide)
    lay_taps(wide, xc_high, xc_low)
    main = convolve(xc_high, xc_low, 0, rows + 2, cols, w_high, w_low) * slope(hidden[...])
    around = ring(*columns, w_high, w_low, r_high, r_low) * slope(side[...])
    main = jnp.where(inside(rows), main.reshape(rows + 2, cols, channels), 0.0)
    line = inside_line(rows)
    around = jnp.where(jnp.concatenate([line, line], axis=0), around, 0.0)
    turn(True, main[1 : rows + 1].reshape(rows * cols, channels), t_high, t_low, turned)
    spread_ext(main, around, wide2)
    lay_taps(wide2, x3_high, x3_low)


def products_kernel(scale, cols, first_row, t_high, t_low, x_high, x_low, *outs):
    products(t_high, t_low, x_high, x_low, first_row, t_high.shape[1], cols, scale, *outs)


def output_kernel(here, x_high, x_low, w_high, w_low, out, token):
    token[...] = jnp.zeros(token.shape, F32)
    rows, cols, channels = here.shape
    total = convolve(x_high, x_low, 0, rows, cols, w_high, w_low)
    out[...] = here[...] + total.reshape(rows, cols, channels)


def input_grad_kernel(here, grad, x_high, x_low, w_high, w_low, out, token):
    token[...] = jnp.zeros(token.shape, F32)
    rows, cols, channels = here.shape
    total = convolve(x_high, x_low, 0, rows, cols, w_high, w_low)
    out[...] = grad[...] + total.reshape(rows, cols, channels) * slope(here[...])


def plane_perm(count, even, odd):
    return [(i, i ^ (odd if (i // 2) % 2 else even)) for i in range(count)]


def plane_swap(away, across):
    count = lax.axis_size("lat") * lax.axis_size("rep")
    one, two = (4, 1) if across else (1, 4)
    return lax.ppermute(away, ("lat", "rep"), plane_perm(count, one, two))


def core_swap(away):
    count = lax.axis_size("lat") * lax.axis_size("rep")
    return lax.ppermute(away, ("lat", "rep"), plane_perm(count, 2, 2))


def add_halves(keep, got, next_keep, next_away, *token):
    for ref in token:
        ref[...] = jnp.zeros(ref.shape, F32)
    half = keep.shape[0] // 2
    next_keep[...] = keep[:half] + got[:half]
    next_away[...] = keep[half:] + got[half:]


def add_up(keep, got, away):
    away[...] = keep[...] + got[...]


def add_three(keep_one, keep_two, core_one, core_two, got, next_keep, next_away):
    half = keep_one.shape[0]
    next_keep[...] = keep_one[...] + core_one[...] + got[:half]
    next_away[...] = keep_two[...] + core_two[...] + got[half:]


def pack(total, place):
    rows, width = total.shape
    tiles = width // LANES // 4
    start = (place // 2) * (2 * tiles + 1)
    whole = start + (place % 2) * (tiles + 1)
    pieces = [total[:, i * LANES : (i + 1) * LANES] for i in range(whole, whole + tiles)]
    half = LANES // 2
    left = (start + tiles) * LANES + (place % 2) * half
    rest = total[:, left : left + half]
    pieces.append(jnp.concatenate([rest[: rows // 2], rest[rows // 2 :]], axis=1))
    return jnp.concatenate(pieces, axis=0)


def unpack(packed, rows):
    whole = packed.shape[0] // rows
    pieces = [packed[i * rows : (i + 1) * rows] for i in range(whole)]
    rest = packed[whole * rows :]
    half = LANES // 2
    rest = jnp.concatenate([rest[:, :half], rest[:, half:]], axis=0)
    odd = lax.axis_index("lon") % 2 == 1
    return jnp.where(
        odd,
        jnp.concatenate([rest, *pieces], axis=1),
        jnp.concatenate([*pieces, rest], axis=1),
    )


def cut_blocks(keep, got, *outs):
    blocks = outs[:4]
    for token in outs[4:]:
        token[...] = jnp.zeros(token.shape, F32)
    total = keep[...] + got[...]
    count = len(blocks)
    parts = [pack(total, place) for place in range(count)]
    z = lax.axis_index("lon")
    for step, block in enumerate(blocks):
        value = parts[step]
        for place in range(1, count):
            value = jnp.where(z == place, parts[place ^ step], value)
        block[...] = value


def wide_sum(keep, got):
    return lax.psum_scatter(keep + got, "lon", scatter_dimension=1, tiled=True).T


def add_blocks(one, two, three, four, out, *tokens):
    for token in tokens:
        token[...] = jnp.zeros(token.shape, F32)
    out[...] = unpack(one[...] + two[...] + three[...] + four[...], out.shape[0])


def send_blocks(keep, got, after=(), flops=0, tokens=()):
    each, taps = keep.shape
    lon = lax.axis_size("lon")
    outs = [((each * taps // lon // LANES, LANES), F32)] * lon + list(tokens)
    blocks = call(cut_blocks, outs, [keep, got], after=after, flops=flops)
    gots = [
        lax.ppermute(blocks[step], "lon", [(i, i ^ step) for i in range(lon)])
        for step in (3, 2, 1)
    ]
    return [blocks[0], *gots], blocks[lon:]


def local(inputs, cotangent, first_weight, second_weight):
    here, grad = inputs[0], cotangent[0]
    rows, cols, channels = here.shape
    cells, tall = rows * cols, rows + 2
    width = 3 * channels
    scale = 1.0 / math.sqrt(
        cells * lax.axis_size("rep") * lax.axis_size("lat") * lax.axis_size("lon")
    )
    edge = ((2, 2, cols, channels), F32)
    edges = [here[:2], here[rows - 2 :], grad[:2], grad[rows - 2 :]]
    one, two = call(pack_rows, [edge] * 2, edges)
    r1, r2 = pair_swap(one, two, "lat", False)
    pair = [((9 * channels, channels), BF16)] * 2
    w1_high, w1_low = call(prepare, pair, [first_weight])
    act, t_high, t_low = call(
        turn_grad,
        [((rows, cols, channels), F32)] + [((channels, cells), BF16)] * 2,
        [here, grad],
        scratch=[((channels, cells), F32)],
    )
    line = ((4 * (rows + 4), channels), F32)
    m1, m2 = call(pack_cols, [line] * 2, [here, grad, r1, r2], after=[t_low])
    q1, q2 = pair_swap(m1, m2, "lon", True)
    lines = ((2 * LINE, channels), F32)
    wide = ((rows + 4, cols + 2 * EDGE, channels), F32)
    wide2 = ((tall, cols + 2 * EDGE, channels), F32)
    taps_1 = [(((rows + 4) * cols, width), BF16)] * 2
    taps_2 = [((tall * cols, width), BF16)] * 2
    around = [((2 * LINE, 3 * width), BF16)] * 2
    halves = [((channels // 2, 9 * channels), F32)] * 2
    hidden, side, x1_high, x1_low, x2_high, x2_low = call(
        hidden_kernel,
        [((tall * cols, channels), F32), lines] + taps_1 + taps_2,
        [act, r1, r2, m1, m2, q1, q2, w1_high, w1_low],
        scratch=[wide, wide2] + around,
    )
    half = halves[0]
    each = channels // 8

    def halves_of(count):
        return [((count, 9 * channels), F32)] * 2

    quarter = ((2 * each, 9 * channels), F32)
    eighth = ((each, 9 * channels), F32)

    def second_products(first, outs, after):
        def rows_of(ref):
            starts = [first * 2 * each, (first + 2) * 2 * each]
            return jnp.concatenate([ref[i : i + 2 * each] for i in starts], axis=0)

        return call(
            lambda high, low, *refs: products_kernel(
                scale, cols, 0, rows_of(high), rows_of(low), *refs
            ),
            outs,
            [t_high, t_low, x2_high, x2_low],
            after=after,
        )

    keep_2, away_2 = second_products(1, [quarter] * 2, [])
    got_2 = core_swap(away_2)
    b2_high, b2_low = call(prepare_back, pair, [second_weight], after=[away_2])
    (away_2,) = call(add_up, [quarter], [keep_2, got_2], after=[b2_low])
    got_2 = plane_swap(away_2, False)
    *keeps, away_one, away_two = second_products(0, [eighth] * 4, [away_2])
    cores = [core_swap(away_one), core_swap(away_two)]
    x3_high, x3_low, t_high, t_low = call(
        inner_kernel,
        taps_2 + [((channels, cells), BF16)] * 2,
        [grad, r1, r2, m1, m2, q1, q2, b2_high, b2_low, hidden, side],
        scratch=[wide] + taps_1 + [wide2] + around + [((channels, cells), F32)],
        after=keeps[:1],
    )
    keep_1, away_1 = call(
        lambda *refs: products_kernel(scale, cols, 1, *refs),
        [half, half],
        [t_high, t_low, x1_high, x1_low],
    )
    got_1 = core_swap(away_1)
    keep_2, away_2 = call(
        add_three, halves_of(each), [*keeps, *cores, got_2], flops=LONG
    )
    got_2 = plane_swap(away_2, True)
    keep_1, away_1 = call(add_halves, halves_of(2 * each), [keep_1, got_1], after=[keep_2])
    got_1 = plane_swap(away_1, True)
    w2_high, w2_low = call(prepare, pair, [second_weight], after=[keep_1])
    outs = [((rows, cols, channels), F32), ((8, 128), F32)]
    output, token = call(
        output_kernel, outs, [here, x2_high, x2_low, w2_high, w2_low], after=[keep_1]
    )
    direct = lax.axis_size("lon") == 4
    if direct:
        blocks, (token,) = send_blocks(keep_2, got_2, [token], LONG, outs[1:])
    else:
        second_grad = wide_sum(keep_2, got_2)
    keep_1, away_1 = call(add_halves, halves_of(each), [keep_1, got_1], after=[token])
    got_1 = plane_swap(away_1, False)
    b1_high, b1_low = call(prepare_back, pair, [first_weight], after=[keep_1])
    input_grad, token = call(
        input_grad_kernel,
        outs,
        [here, grad, x3_high, x3_low, b1_high, b1_low],
        after=[keep_1],
    )
    if direct:
        shape = (each, 9 * channels // 4)
        summed, token = call(
            add_blocks, [(shape, F32), outs[1]], blocks, after=[token], flops=LONG
        )
        second_grad = summed.T
        blocks, _ = send_blocks(keep_1, got_1, [token])
        first_grad = call(add_blocks, [(shape, F32)], blocks)[0].T
    else:
        first_grad = wide_sum(keep_1, got_1)
    return (output[None], input_grad[None], first_grad, second_grad)


def solution(mesh):
    in_specs = (P("rep", "lat", "lon", None), P("rep", "lat", "lon", None), P(), P())
    out_specs = (
        P("rep", "lat", "lon", None),
        P("rep", "lat", "lon", None),
        P("lon", ("lat", "rep")),
        P("lon", ("lat", "rep")),
    )
    return jax.shard_map(local, mesh=mesh, in_specs=in_specs, out_specs=out_specs, check_vma=False)
```
